128 devices in a mesh: ulysses: 8 (over y_hi, x), blk: 16 (over z, y_lo, core).
Axes of the slice: x: 4, y: 4 (y_hi: 2, y_lo: 2; y = y_hi * 2 + y_lo), z: 4, core: 2. Of those that a mesh axis runs over, the one named last changes fastest.
Arguments:
- tokens: bfloat16 [16384, 2048], P(('ulysses', 'blk')), may hold values from -6 to 6
- cotangent: bfloat16 [16384, 2048], P(('ulysses', 'blk')), may hold values from -6 to 6
- doc_ids: int32 [128], replicated, may hold values from 0 to 20, never falling along the last dimension, each value on 1 to 16 neighbouring positions
- ln1_gain: bfloat16 [2048], P('blk'), may hold values from 0.099609375 to 1.8984375
- ln1_shift: bfloat16 [2048], P('blk'), may hold values from -1.75 to 1.75
- w_qkv: bfloat16 [2048, 3, 2048], P('blk', None, 'ulysses'), may hold values from -0.125 to 0.125
- b_qkv: bfloat16 [3, 2048], P(None, ('ulysses', 'blk')), may hold values from -0.625 to 0.625
- w_out: bfloat16 [2048, 2048], P('ulysses', 'blk'), may hold values from -0.5 to 0.5
- ln2_gain: bfloat16 [2048], P('blk'), may hold values from 0.099609375 to 1.8984375
- ln2_shift: bfloat16 [2048], P('blk'), may hold values from -1.75 to 1.75
- w_gate: bfloat16 [2048, 5632], P('blk', 'ulysses'), may hold values from -0.125 to 0.125
- w_up: bfloat16 [2048, 5632], P('blk', 'ulysses'), may hold values from -0.125 to 0.125
- w_down: bfloat16 [5632, 2048], P('ulysses', 'blk'), may hold values from -0.15625 to 0.15625
Outputs:
- mixed: bfloat16 [16384, 2048], P(('ulysses', 'blk'))
- input_grad: float32 [16384, 2048], P(('ulysses', 'blk'))
- ln1_gain_grad: float32 [2048], P(('ulysses', 'blk'))
- ln1_shift_grad: float32 [2048], P(('ulysses', 'blk'))
- w_qkv_grad: float32 [2048, 3, 2048], P('blk', None, 'ulysses')
- b_qkv_grad: float32 [3, 2048], P(None, ('ulysses', 'blk'))
- w_out_grad: float32 [2048, 2048], P('ulysses', 'blk')
- ln2_gain_grad: float32 [2048], P(('ulysses', 'blk'))
- ln2_shift_grad: float32 [2048], P(('ulysses', 'blk'))
- w_gate_grad: float32 [2048, 5632], P('blk', 'ulysses')
- w_up_grad: float32 [2048, 5632], P('blk', 'ulysses')
- w_down_grad: float32 [5632, 2048], P('ulysses', 'blk')
The draws below stay inside these ranges and needn't reach their ends.
Inputs may be any that keep to these rules, and one draw needn't show every extreme that they name: `doc_ids`: document numbers never fall along the blocks; each of the 21 documents covers 1 to 16 consecutive blocks, one exactly 16.
All inputs are finite; a program needn't handle non-finite values.
Results may differ from the reference program's by a relative error of at most 0.035.
Values may be sent and summed in bfloat16 or wider, within the bound.
No kernel may reach another device: no remote copies, remote signals or barrier semaphores. Data moves between devices by JAX's collectives and lax.ppermute only.
A program may use at most 128 MiB of HBM per device.

```python
import math
import jax
import jax.numpy as jnp
import numpy as np
from jax import lax

D = 2048
HEADS = 32
HEAD_DIM = 64
ROT = 16
FF = 5632
BLK_TOK = 128
Q_BLOCK = 512
TOKENS = 16384
NBLOCKS = 128
DOC_MOST = 16
DOC_COUNT = 21


def levels(stream_key, shape, cuts, least, high):
    def one(position, parts):
        steps = jax.random.uniform(jax.random.fold_in(jax.random.fold_in(stream_key, 6), position), (parts,), jnp.float32, least / len(cuts), high / len(cuts))
        return jnp.repeat(jnp.exp(steps), shape[position] // parts).reshape((-1,) + (1,) * (len(shape) - position - 1))

    loudness = one(*cuts[0])
    for cut in cuts[1:]:
        loudness = loudness * one(*cut)
    return loudness


def split_up(count, total, reach, skew):
    portions = [(1 << 20) // math.isqrt(standing ** skew) + 1 for standing in range(2, count + 1)]
    surplus, holding = total - reach - (count - 1), [1] * (count - 1)
    while surplus > 0:
        free = [i for i in range(count - 1) if holding[i] < reach]
        pool, left = sum([portions[i] for i in free]), surplus
        for i in free:
            extra = min(reach - holding[i], max(1, left * portions[i] // pool), surplus)
            holding[i] = holding[i] + extra
            surplus = surplus - extra
    return np.array([reach] + holding)


def uneven_parts(own_key, number_of, total, bound, slope):
    if number_of == 2:
        one = jax.random.randint(own_key, (), max(1, total - bound), min(bound, total - 1) + 1)
        return jnp.stack([one, total - one])
    sizes = jnp.asarray(split_up(number_of, total, bound, slope), jnp.int32)
    pairs = (number_of - 1) // 2
    giver, receiver = sizes[1:1 + 2 * pairs:2], sizes[2:2 + 2 * pairs:2]
    room = jnp.minimum(giver - 1, bound - receiver)
    passed = jax.random.randint(jax.random.fold_in(own_key, 1), (pairs,), 0, 1 << 20) % (room + 1)
    sizes = sizes.at[1:1 + 2 * pairs:2].set(giver - passed).at[2:2 + 2 * pairs:2].set(receiver + passed)
    return sizes[jax.random.permutation(jax.random.fold_in(own_key, 2), number_of)]


def scatter_about(own_key, dims, deviation, most, shards=(), kind=jnp.bfloat16):
    array = jax.random.normal(own_key, dims, jnp.float32) * deviation
    if len(shards) > 0:
        array = levels(own_key, dims, shards, -0.22, 0.18) * array
    return jnp.clip(array, min=-most, max=most).astype(kind)


def setup_inputs(seed: int = 0) -> dict:
    splits = jax.random.split(jax.random.key(seed), 14)
    return {
        "tokens": scatter_about(splits[0], (TOKENS, D), 1.0, 6.0, ((0, 128),)),
        "cotangent": scatter_about(splits[1], (TOKENS, D), 1.0, 6.0, ((0, 128),)),
        "doc_ids": jnp.searchsorted(jnp.cumsum(uneven_parts(splits[2], DOC_COUNT, NBLOCKS, DOC_MOST, 2)), jnp.arange(NBLOCKS), side="right").astype(jnp.int32),
        "ln1_gain": jnp.clip(1.0 + 0.18 * jax.random.normal(splits[3], (D,), jnp.float32), 0.099609375, 1.8984375).astype(jnp.bfloat16),
        "ln1_shift": scatter_about(splits[4], (D,), 0.3, 1.75, ((0, 16),)),
        "w_qkv": scatter_about(splits[5], (D, 3, D), D ** -0.5, 0.125, ((0, 16), (2, 8))),
        "b_qkv": scatter_about(splits[6], (3, D), 0.1, 0.625, ((1, 128),)),
        "w_out": scatter_about(splits[7], (D, D), (D // 16) ** -0.5, 0.5, ((0, 8), (1, 16))),
        "ln2_gain": jnp.clip(1.0 + 0.18 * jax.random.normal(splits[8], (D,), jnp.float32), 0.099609375, 1.8984375).astype(jnp.bfloat16),
        "ln2_shift": scatter_about(splits[9], (D,), 0.3, 1.75, ((0, 16),)),
        "w_gate": scatter_about(splits[10], (D, FF), D ** -0.5, 0.125, ((0, 16), (1, 8))),
        "w_up": scatter_about(splits[11], (D, FF), D ** -0.5, 0.125, ((0, 16), (1, 8))),
        "w_down": scatter_about(splits[12], (FF, D), (FF // 4) ** -0.5, 0.15625, ((0, 8), (1, 16))),
    }


@jax.custom_vjp
def low(v):
    return lax.optimization_barrier(v.astype(jnp.bfloat16)).astype(jnp.float32)

@jax.custom_vjp
def low_back(v):
    return v

def low_keep(v):
    return (low(v), None)

def low_pass(kept, grad):
    return (grad,)

def back_keep(v):
    return (v, None)

def back_low(kept, grad):
    return (low(grad),)
low.defvjp(low_keep, low_pass)
low_back.defvjp(back_keep, back_low)
highest = lax.Precision.HIGHEST
eps = 1e-05
rope_base = 10000.0
masked_score = -1e+30

def matmul(former, latter):
    return jnp.dot(former, latter, precision=highest, preferred_element_type=jnp.float32)

def layer_norm(values, gain, shift):
    centred = values - lax.optimization_barrier(jnp.mean(values, -1, keepdims=True))
    inverse = lax.rsqrt(lax.optimization_barrier(jnp.mean(centred * centred, -1, keepdims=True)) + eps)
    return centred * inverse * gain + shift

def rotary_tables(positions):
    halfway = ROT // 2
    counter = jnp.arange(halfway, dtype=jnp.float32)
    frequency = rope_base ** (-2.0 * counter / ROT)
    angles = positions.astype(jnp.float32)[:, None] * frequency[None, :]
    return (jnp.concatenate([jnp.cos(angles)] * 2, -1), jnp.concatenate([jnp.sin(angles)] * 2, -1))

def rotate(values, cosine, sine):
    halfway = ROT // 2
    turning = values[..., :ROT]
    turned = jnp.concatenate([-turning[..., halfway:], turning[..., :halfway]], -1)
    rotated = turning * cosine[:, None, :] + turned * sine[:, None, :]
    return jnp.concatenate([rotated, values[..., ROT:]], -1)

def stream_tables(doc_ids):
    first_block = lax.optimization_barrier(jnp.sum((doc_ids[None, :] < doc_ids[:, None]).astype(jnp.int32), axis=1))
    token_doc = jnp.repeat(doc_ids, BLK_TOK)
    token_index = jnp.arange(TOKENS, dtype=jnp.int32)
    positions = token_index - jnp.repeat(first_block, BLK_TOK) * BLK_TOK
    return (token_doc, token_index, positions)

def attend(query_all, key_all, value_all, token_doc, token_index):
    window = min(TOKENS, DOC_MOST * BLK_TOK + Q_BLOCK)
    score_scale = HEAD_DIM ** (-0.5)

    def one_block(row_start):
        begin = jnp.maximum(row_start + Q_BLOCK - window, 0)
        query_rows = lax.dynamic_slice_in_dim(query_all, row_start, Q_BLOCK, 0)
        key_rows = lax.dynamic_slice_in_dim(key_all, begin, window, 0)
        value_rows = lax.dynamic_slice_in_dim(value_all, begin, window, 0)
        query_doc = lax.dynamic_slice_in_dim(token_doc, row_start, Q_BLOCK, 0)
        key_doc = lax.dynamic_slice_in_dim(token_doc, begin, window, 0)
        query_index = lax.dynamic_slice_in_dim(token_index, row_start, Q_BLOCK, 0)
        key_index = lax.dynamic_slice_in_dim(token_index, begin, window, 0)
        allowed = (query_doc[:, None] == key_doc[None, :]) & (key_index[None, :] <= query_index[:, None])
        scores = jnp.einsum('qhd,khd->hqk', query_rows, key_rows, precision=highest) * score_scale
        scores = low_back(jnp.where(allowed[None], scores, masked_score))
        top_score = lax.optimization_barrier(jnp.max(scores, -1, keepdims=True))
        expo = jnp.exp(scores - top_score)
        softmax_w = low(expo / lax.optimization_barrier(jnp.sum(expo, -1, keepdims=True)))
        return jnp.einsum('hqk,khd->qhd', softmax_w, value_rows, precision=highest)
    starts = jnp.arange(TOKENS // Q_BLOCK, dtype=jnp.int32) * Q_BLOCK
    return lax.map(jax.checkpoint(one_block), starts).reshape(TOKENS, HEADS, HEAD_DIM)

def reference(tokens, cotangent, doc_ids, ln1_gain, ln1_shift, w_qkv, b_qkv, w_out, ln2_gain, ln2_shift, w_gate, w_up, w_down):
    token_doc, token_index, positions = stream_tables(doc_ids)
    cosine, sine = rotary_tables(positions)

    def forward(inputs, gain_one, shift_one, qkv_weight, qkv_bias, out_weight, gain_two, shift_two, gate_weight, up_weight, down_weight):
        normed_one = low(layer_norm(inputs, gain_one, shift_one))
        joint = low_back(matmul(normed_one, qkv_weight.reshape(D, 3 * D)) + qkv_bias.reshape(3 * D))
        joint = joint.reshape(TOKENS, 3, HEADS, HEAD_DIM)
        query_all = low(rotate(joint[:, 0], cosine, sine))
        key_all = low(rotate(joint[:, 1], cosine, sine))
        value_all = low(joint[:, 2])
        attended = low_back(low(attend(query_all, key_all, value_all, token_doc, token_index)))
        mixer_out = low_back(matmul(attended.reshape(TOKENS, D), out_weight))
        middle = inputs + mixer_out
        normed_two = low(layer_norm(middle, gain_two, shift_two))
        gate_pre = low_back(matmul(normed_two, gate_weight))
        up_pre = low_back(matmul(normed_two, up_weight))
        active = low(gate_pre * jax.nn.sigmoid(gate_pre) * up_pre)
        return middle + low_back(matmul(active, down_weight))
    mixed, pullback = jax.vjp(forward, tokens.astype(jnp.float32), ln1_gain.astype(jnp.float32), ln1_shift.astype(jnp.float32), w_qkv.astype(jnp.float32), b_qkv.astype(jnp.float32), w_out.astype(jnp.float32), ln2_gain.astype(jnp.float32), ln2_shift.astype(jnp.float32), w_gate.astype(jnp.float32), w_up.astype(jnp.float32), w_down.astype(jnp.float32))
    grads = pullback(cotangent.astype(jnp.float32))
    return (mixed.astype(jnp.bfloat16), grads[0], grads[1], grads[2], grads[3], grads[4], grads[5], grads[6], grads[7], grads[8], grads[9], grads[10])
```

```python
import functools

import jax
import jax.numpy as jnp
from jax import lax
from jax.experimental import pallas as pl
from jax.experimental.pallas import tpu as pltpu
from jax.sharding import Mesh
from jax.sharding import PartitionSpec as P

D = 2048
HEADS = 32
HEAD_DIM = 64
ROT = 16
BLK_TOK = 128
HID = 704
HID_PAD = 768
SHARED = 3 * HID_PAD + 256

eps = 1e-05
rope_base = 10000.0
masked_score = -1e30
score_scale = HEAD_DIM ** (-0.5)

AXES = ("yh", "x", "z", "yl", "k")
PLANE = ("yh", "z", "yl", "k")
BLK = ("z", "yl", "k")
Y = ("yh", "yl")

VMEM_LIMIT = 60 * 1024 * 1024
TINY = pl.CostEstimate(flops=1, bytes_accessed=1, transcendentals=0)


def mm(a, b, ca=1, cb=0):
    return lax.dot_general(a, b, (((ca,), (cb,)), ((), ())), preferred_element_type=jnp.float32)


def swap_core(value):
    return lax.ppermute(value, ("k",), [(0, 1), (1, 0)])


def exchange(parts, axes):
    return lax.all_to_all(parts, axes, 0, 0, tiled=True)


def send(value, axes, step):
    return lax.ppermute(value, axes, [(i, (i + step) % 4) for i in range(4)])


def gather(value, axes, *others):
    me = lax.axis_index(axes)
    pieces = [send(value, axes, step) for step in (1, 3, 2)]
    if others:
        pieces = after(pieces, *others)
    buffer = jnp.zeros((4,) + value.shape, value.dtype)
    for step, piece in zip((0, 1, 3, 2), [value] + pieces):
        buffer = lax.dynamic_update_index_in_dim(buffer, piece, (me - step) % 4, 0)
    return buffer


def ring_gather(value):
    return exchange(jnp.broadcast_to(value, (4,) + value.shape), ("x",))


def send(value, axes, step):
    return lax.ppermute(value, axes, [(i, (i + step) % 4) for i in range(4)])


def gather(value, axes, *others):
    me = lax.axis_index(axes)
    pieces = [send(value, axes, step) for step in (1, 3, 2)]
    if others:
        pieces = after(pieces, *others)
    buffer = jnp.zeros((4,) + value.shape, value.dtype)
    for step, piece in zip((0, 1, 3, 2), [value] + pieces):
        buffer = lax.dynamic_update_index_in_dim(buffer, piece, (me - step) % 4, 0)
    return buffer


def ring_gather(value):
    return exchange(jnp.broadcast_to(value, (4,) + value.shape), ("x",))


def after(value, *others):
    return lax.optimization_barrier((value,) + others)[0]


def rotary_tables(positions):
    halfway = ROT // 2
    counter = jnp.arange(halfway, dtype=jnp.float32)
    frequency = rope_base ** (-2.0 * counter / ROT)
    lane = jnp.arange(128) % HEAD_DIM
    frequency = jnp.where(lane < ROT, jnp.tile(frequency, 16), 0.0)
    angles = positions.astype(jnp.float32)[:, None] * frequency[None, :]
    sine = jnp.sin(angles)
    return (
        jnp.cos(angles),
        jnp.where(lane < halfway, -sine, 0.0),
        jnp.where((lane >= halfway) & (lane < ROT), sine, 0.0),
    )


def pack_joint_kernel(qkv_ref, out_ref, vectors_ref, bias_ref, h0_ref, h1_ref, small_ref):
    out_t = jnp.transpose(out_ref[...])
    for j, h_ref in enumerate((h0_ref, h1_ref)):
        for part in range(3):
            column = part * 256 + j * 128
            h_ref[:128, part * 128 : (part + 1) * 128] = qkv_ref[:, column : column + 128]
        h_ref[:128, 384:] = out_t[:, j * 128 : (j + 1) * 128]
    small_ref[...] = jnp.zeros_like(small_ref)
    small_ref[0:4, :128] = vectors_ref[...].astype(jnp.float32)
    small_ref[8:11, :16] = bias_ref[...].astype(jnp.float32)
    h0_ref[128:, :] = small_ref[...].astype(jnp.bfloat16)


def pack_joint_call(qkv, out, vectors, bias):
    vmem = pl.BlockSpec(memory_space=pltpu.VMEM)
    return pl.pallas_call(
        pack_joint_kernel,
        in_specs=[vmem] * 4,
        out_specs=[vmem] * 2,
        out_shape=[
            jax.ShapeDtypeStruct((144, 512), jnp.bfloat16),
            jax.ShapeDtypeStruct((128, 512), jnp.bfloat16),
        ],
        scratch_shapes=[pltpu.VMEM((16, 512), jnp.float32)],
    )(qkv, out, vectors, bias)


def pack_hidden_kernel(gate_ref, up_ref, down_ref, rest_ref):
    down = jnp.transpose(down_ref[...])
    for i, weights in enumerate((gate_ref[...], up_ref[...], down)):
        first = i * HID_PAD
        rest_ref[:, first + HID_PAD - 128 : first + HID_PAD] = jnp.zeros((128, 128), jnp.bfloat16)
        rest_ref[:, first : first + HID] = weights


def pack_hidden_call(gate, up, down):
    return whole_call(
        pack_hidden_kernel, jax.ShapeDtypeStruct((128, 3 * HID_PAD), jnp.bfloat16), gate, up, down
    )


def core_columns(ref, core, blocks):
    columns = [ref[:blocks, :, pl.ds(pl.multiple_of((2 * i + core) * 128, 128), 128)] for i in range(8)]
    return jnp.concatenate(columns, 2).reshape(blocks * 128, 1024)


def core_rows(w0_ref, w1_ref):
    w0 = jnp.concatenate([w0_ref[z, 0, yl, :128] for z in range(4) for yl in range(2)], 0)
    w1 = jnp.concatenate([w1_ref[0, yl, z] for z in range(4) for yl in range(2)], 0)
    return jnp.concatenate([w0, w1], 1)


def normalise(values):
    centred = values - jnp.mean(values, -1, keepdims=True)
    inverse = lax.rsqrt(jnp.mean(centred * centred, -1, keepdims=True) + eps)
    return centred * inverse, inverse


def qkv_kernel(
    core_ref,
    x_ref,
    before_ref,
    gain_ref,
    shift_ref,
    own0_ref,
    own1_ref,
    oth0_ref,
    oth1_ref,
    bias_ref,
    cos_ref,
    up_ref,
    down_ref,
    out_ref,
    normed_ref,
    x_cores,
):
    part = pl.program_id(1)
    core = core_ref[0]

    @pl.when((pl.program_id(0) == 0) & (part == 0))
    def _():
        for b in range(5):
            block = x_ref[b] if b < 4 else before_ref[...]
            unit, _ = normalise(block.astype(jnp.float32))
            normed = (unit * gain_ref[...] + shift_ref[...]).astype(jnp.bfloat16)
            if b < 4:
                normed_ref[b] = normed
            for c in range(16):
                column = pl.multiple_of((c // 2 + 8 * ((c + core) % 2)) * 128, 128)
                x_cores[b * 128 : (b + 1) * 128, pl.ds(column, 128)] = normed[:, c * 128 : (c + 1) * 128]

    def joint(rows):
        weights = jnp.concatenate([core_rows(own0_ref, own1_ref), core_rows(oth0_ref, oth1_ref)], 0)
        return mm(x_cores[:rows], weights) + bias_ref[0, 0]

    def turned(value):
        rows = value.shape[0]
        return (
            value * cos_ref[:rows]
            + pltpu.roll(value, 120, 1) * up_ref[:rows]
            + pltpu.roll(value, 8, 1) * down_ref[:rows]
        )

    @pl.when(part == 0)
    def _():
        value = joint(512)
        for j in range(2):
            query = turned(value[:, j * 128 : (j + 1) * 128]) * score_scale
            out_ref[j, 0, :, 4] = query.astype(jnp.bfloat16).reshape(4, 128, 128)

    @pl.when(part > 0)
    def _():
        value = joint(640)
        for j in range(2):
            block = value[:, j * 128 : (j + 1) * 128]
            block = jnp.where(part == 1, turned(block), block)
            block = block.astype(jnp.bfloat16).reshape(5, 128, 128)

            @pl.when(part == 1)
            def _():
                out_ref[j, 0, :, 2] = block[:4]
                out_ref[j, 0, 1:, 0] = block[:3]
                out_ref[j, 0, 0, 0] = block[4]

            @pl.when(part == 2)
            def _():
                out_ref[j, 0, :, 3] = block[:4]
                out_ref[j, 0, 1:, 1] = block[:3]
                out_ref[j, 0, 0, 1] = block[4]


def qkv_call(core, tokens, before, gain, shift, weights, bias, tables):
    table = pl.BlockSpec((640, 128), lambda h, p: (0, 0))
    vector = pl.BlockSpec((1, D), lambda h, p: (0, 0))
    first = pl.BlockSpec((4, 1, 2, 144, 128), lambda h, p: (0, h, 0, 0, p))
    second = pl.BlockSpec((1, 2, 4, 128, 128), lambda h, p: (h, 0, 0, 0, p))
    return pl.pallas_call(
        qkv_kernel,
        grid=(2, 3),
        in_specs=[
            pl.BlockSpec(memory_space=pltpu.SMEM),
            pl.BlockSpec((4, 128, D), lambda h, p: (0, 0, 0)),
            pl.BlockSpec((128, D), lambda h, p: (0, 0)),
            vector,
            vector,
            first,
            second,
            first,
            second,
            pl.BlockSpec((1, 1, 1, 256), lambda h, p: (h, p, 0, 0)),
            table,
            table,
            table,
        ],
        out_specs=[
            pl.BlockSpec((2, 1, 4, 5, 128, 128), lambda h, p: (0, h, 0, 0, 0, 0)),
            pl.BlockSpec((4, 128, D), lambda h, p: (0, 0, 0)),
        ],
        out_shape=[
            jax.ShapeDtypeStruct((2, 2, 4, 5, 128, 128), jnp.bfloat16),
            jax.ShapeDtypeStruct((4, 128, D), jnp.bfloat16),
        ],
        scratch_shapes=[pltpu.VMEM((640, D), jnp.bfloat16)],
        compiler_params=pltpu.CompilerParams(vmem_limit_bytes=VMEM_LIMIT),
        cost_estimate=TINY,
    )(core, tokens, before, gain, shift, *weights, bias, *tables)


def whole_call(kernel, out_shape, *operands, scratch=()):
    vmem = pl.BlockSpec(memory_space=pltpu.VMEM)
    return pl.pallas_call(
        kernel,
        in_specs=[vmem] * len(operands),
        out_specs=jax.tree.map(lambda _: vmem, out_shape),
        out_shape=out_shape,
        scratch_shapes=list(scratch),
        compiler_params=pltpu.CompilerParams(vmem_limit_bytes=VMEM_LIMIT),
        cost_estimate=TINY,
    )(*operands)


def middle_kernel(came_ref, tokens_ref, gain_ref, shift_ref, middle_ref, normed_ref):
    middle = tokens_ref[...].astype(jnp.float32)
    for i in range(4):
        middle = middle + came_ref[i].astype(jnp.float32)
    middle_ref[...] = middle
    normed = (normalise(middle)[0] * gain_ref[...] + shift_ref[...]).astype(jnp.bfloat16)
    for i in range(4):
        normed_ref[i] = normed


def back_through(came_ref, values, gain):
    grad = came_ref[0].astype(jnp.float32)
    for i in range(1, 4):
        grad = grad + came_ref[i].astype(jnp.float32)
    unit, inverse = normalise(values)
    grad_unit = grad * gain
    centred_grad = (
        grad_unit
        - jnp.mean(grad_unit, -1, keepdims=True)
        - unit * jnp.mean(grad_unit * unit, -1, keepdims=True)
    )
    gain_grad = jnp.sum(grad * unit, 0, keepdims=True)
    return inverse * centred_grad, gain_grad, jnp.sum(grad, 0, keepdims=True)


def middle_back_kernel(came_ref, middle_ref, cot_ref, gain_ref, grad_ref, ring_ref, gain_grad_ref, shift_grad_ref):
    grad, gain_grad_ref[...], shift_grad_ref[...] = back_through(came_ref, middle_ref[...], gain_ref[...])
    grad = grad + cot_ref[...].astype(jnp.float32)
    grad_ref[...] = grad
    for i in range(4):
        ring_ref[i] = grad.astype(jnp.bfloat16)


def input_back_kernel(came_ref, tokens_ref, grad_ref, gain_ref, out_ref, gain_grad_ref, shift_grad_ref):
    values = tokens_ref[...].astype(jnp.float32)
    grad, gain_grad_ref[...], shift_grad_ref[...] = back_through(came_ref, values, gain_ref[...])
    out_ref[...] = grad_ref[...] + grad


def mixed_kernel(came_ref, middle_ref, out_ref):
    total = middle_ref[...]
    for i in range(4):
        total = total + came_ref[i].astype(jnp.float32)
    out_ref[...] = total.astype(jnp.bfloat16)


def shared_end_kernel(total_ref, gate_ref, up_ref, down_ref, out_ref):
    total = total_ref[...].astype(jnp.float32)
    for c in range(3):
        width = min(HID, c * 256 + 256) - c * 256
        gate_ref[:, c * 256 : c * 256 + width] = total[:, c * 512 : c * 512 + width]
        up_ref[:, c * 256 : c * 256 + width] = total[:, c * 512 + 256 : c * 512 + 256 + width]
    down_ref[...] = jnp.transpose(total[:, 2 * HID_PAD : 3 * HID_PAD])[:HID]
    out_ref[...] = jnp.transpose(total[:, 3 * HID_PAD :])


def joint_end_kernel(*refs):
    for j in range(2):
        total = sum(ref[...].astype(jnp.float32) for ref in refs[4 * j : 4 * j + 4])
        for part in range(3):
            refs[8][:, part * 256 + j * 128 : part * 256 + j * 128 + 128] = total[:, part * 128 : part * 128 + 128]


def ordered(core_ref, own, other):
    first = core_ref[0] == 0
    return jnp.concatenate([jnp.where(first, own, other), jnp.where(first, other, own)], 0)


def project_kernel(core_ref, att_ref, own0_ref, own1_ref, oth0_ref, oth1_ref, out_ref):
    att = jnp.concatenate([att_ref[j, h].reshape(512, 128) for h in range(2) for j in range(2)], 1)

    def rows(w0_ref, w1_ref):
        return jnp.concatenate(
            [w for h in range(2) for w in (w0_ref[0, h, 0, :128], w1_ref[h, 0, 0])], 1
        )

    weights = ordered(core_ref, rows(own0_ref, own1_ref), rows(oth0_ref, oth1_ref))
    out_ref[...] = mm(att, weights, 1, 1).astype(jnp.bfloat16).reshape(4, 128, 256)


def project_call(core, att, weights):
    first = pl.BlockSpec((1, 2, 1, 144, 128), lambda n: (n // 2, 0, n % 2, 0, 3))
    second = pl.BlockSpec((2, 1, 1, 128, 128), lambda n: (0, n % 2, n // 2, 0, 3))
    return pl.pallas_call(
        project_kernel,
        grid=(8,),
        in_specs=[
            pl.BlockSpec(memory_space=pltpu.SMEM),
            pl.BlockSpec((2, 2, 4, 128, 128), lambda n: (0, 0, 0, 0, 0)),
            first,
            second,
            first,
            second,
        ],
        out_specs=pl.BlockSpec((4, 128, 256), lambda n: (0, 0, n)),
        out_shape=jax.ShapeDtypeStruct((4, 128, D), jnp.bfloat16),
        compiler_params=pltpu.CompilerParams(vmem_limit_bytes=VMEM_LIMIT),
        cost_estimate=TINY,
    )(core, att, *weights)


def project_back_kernel(core_ref, grad_ref, own0_ref, own1_ref, oth0_ref, oth1_ref, out_ref):
    core = core_ref[0]
    grad = mm(core_columns(grad_ref, core, 4), core_rows(own0_ref, own1_ref))
    grad = grad + mm(core_columns(grad_ref, 1 - core, 4), core_rows(oth0_ref, oth1_ref))
    grad = grad.astype(jnp.bfloat16)
    for j in range(2):
        out_ref[j, 0] = grad[:, j * 128 : (j + 1) * 128].reshape(4, 128, 128)


def project_back_call(core, grad, weights):
    first = pl.BlockSpec((4, 1, 2, 144, 128), lambda h: (0, h, 0, 0, 3))
    second = pl.BlockSpec((1, 2, 4, 128, 128), lambda h: (h, 0, 0, 0, 3))
    return pl.pallas_call(
        project_back_kernel,
        grid=(2,),
        in_specs=[
            pl.BlockSpec(memory_space=pltpu.SMEM),
            pl.BlockSpec((4, 128, D), lambda h: (0, 0, 0)),
            first,
            second,
            first,
            second,
        ],
        out_specs=pl.BlockSpec((2, 1, 4, 128, 128), lambda h: (0, h, 0, 0, 0)),
        out_shape=jax.ShapeDtypeStruct((2, 2, 4, 128, 128), jnp.bfloat16),
        compiler_params=pltpu.CompilerParams(vmem_limit_bytes=VMEM_LIMIT),
        cost_estimate=TINY,
    )(core, grad, *weights)


def feed_forward_kernel(
    x_ref, cot_ref, gate_ref, up_ref, down_ref, active_ref, grads_ref, back_ref, out_ref, back_sum, out_sum
):
    step = pl.program_id(0) * 3 + pl.program_id(1)
    x = x_ref[...].reshape(512, D)
    gate = mm(x, gate_ref[0])
    up = mm(x, up_ref[0])
    grad_active = mm(cot_ref[...].reshape(512, D), down_ref[0])
    sigmoid = jax.nn.sigmoid(gate)
    silu = gate * sigmoid
    active = (silu * up).astype(jnp.bfloat16)
    grad_gate = (grad_active * up * (sigmoid + silu * (1.0 - sigmoid))).astype(jnp.bfloat16)
    grad_up = (grad_active * silu).astype(jnp.bfloat16)
    grads = jnp.concatenate([grad_gate, grad_up], 1)
    active_ref[0] = active
    grads_ref[0] = grads
    back = mm(grads, jnp.concatenate([gate_ref[0], up_ref[0]], 1), 1, 1)
    out = mm(active, down_ref[0], 1, 1)

    @pl.when(step == 0)
    def _():
        back_sum[...] = back
        out_sum[...] = out

    @pl.when((step > 0) & (step < 5))
    def _():
        back_sum[...] += back
        out_sum[...] += out

    @pl.when(step == 5)
    def _():
        back_ref[...] = (back_sum[...] + back).astype(jnp.bfloat16).reshape(4, 128, D)
        out_ref[...] = (out_sum[...] + out).astype(jnp.bfloat16).reshape(4, 128, D)


def feed_forward_call(x, ring, rest):
    tokens = pl.BlockSpec((4, 128, D), lambda h, c: (0, 0, 0))
    weight = [pl.BlockSpec((1, D, 256), lambda h, c, first=first: (h, 0, first + c)) for first in (0, 3, 6)]
    ring_shape = jax.ShapeDtypeStruct((4, 128, D), jnp.bfloat16)
    return pl.pallas_call(
        feed_forward_kernel,
        grid=(2, 3),
        in_specs=[tokens, pl.BlockSpec((4, 128, D), lambda h, c: (0, 1, 0))] + weight,
        out_specs=[
            pl.BlockSpec((1, 512, 256), lambda h, c: (h, 0, c)),
            pl.BlockSpec((1, 512, 512), lambda h, c: (h, 0, c)),
            tokens,
            tokens,
        ],
        out_shape=[
            jax.ShapeDtypeStruct((2, 512, HID_PAD), jnp.bfloat16),
            jax.ShapeDtypeStruct((2, 512, 2 * HID_PAD), jnp.bfloat16),
            ring_shape,
            ring_shape,
        ],
        scratch_shapes=[pltpu.VMEM((512, D), jnp.float32), pltpu.VMEM((512, D), jnp.float32)],
        compiler_params=pltpu.CompilerParams(vmem_limit_bytes=VMEM_LIMIT),
        cost_estimate=TINY,
    )(x, ring, rest, rest, rest)


def plane_grad_kernel(core_ref, left_ref, left_other_ref, right_ref, right_other_ref, *refs):
    out_ref, left_t = refs[-2:]

    @pl.when((pl.program_id(0) == 0) & (pl.program_id(1) == 0))
    def _():
        left_t[:, :512] = jnp.transpose(core_columns(left_ref, core_ref[0], 4))
        left_t[:, 512:] = jnp.transpose(core_columns(left_other_ref, core_ref[0], 4))

    total = mm(left_t[...], jnp.concatenate([right_ref[0], right_other_ref[0]], 0)).astype(jnp.bfloat16)
    for z in range(4):
        for yl in range(2):
            row = (z * 2 + yl) * 128
            out_ref[0, yl, z] = total[row : row + 128]


def plane_grad_call(core, left, right, columns, before, first, shared=None):
    left_block = pl.BlockSpec((4, 128, D), lambda n, h: (0, before, 0))
    right_block = pl.BlockSpec((1, 512, 256), lambda n, h: (h, 0, n))
    extra = [] if shared is None else [shared]
    return pl.pallas_call(
        plane_grad_kernel,
        grid=(columns // 256, 2),
        in_specs=[
            pl.BlockSpec(memory_space=pltpu.SMEM),
            left_block,
            left_block,
            right_block,
            right_block,
        ]
        + [pl.BlockSpec(memory_space=pl.ANY)] * len(extra),
        out_specs=pl.BlockSpec((1, 2, 4, 128, 256), lambda n, h: (h, 0, 0, 0, first // 256 + n)),
        out_shape=jax.ShapeDtypeStruct((2, 2, 4, 128, SHARED), jnp.bfloat16),
        input_output_aliases={5: 0} if extra else {},
        scratch_shapes=[pltpu.VMEM((1024, 1024), jnp.bfloat16)],
        compiler_params=pltpu.CompilerParams(vmem_limit_bytes=VMEM_LIMIT),
        cost_estimate=TINY,
    )(core, *left, *right, *extra)


def weight_grad_kernel(core_ref, place_ref, left_ref, left_other_ref, right_ref, right_other_ref, *refs):
    outs, left_t = refs[:4], refs[4]
    h = pl.program_id(1)

    @pl.when((h == 0) & (pl.program_id(0) == 0))
    def _():
        left_t[:, :512] = jnp.transpose(core_columns(left_ref, core_ref[0], 4))
        left_t[:, 512:] = jnp.transpose(core_columns(left_other_ref, core_ref[0], 4))

    total = mm(left_t[...], jnp.concatenate([right_ref[0], right_other_ref[0]], 0)).astype(jnp.bfloat16)
    for z in range(4):
        for yl in range(2):
            row = (z * 2 + yl) * 128
            chip = (h * 2 + yl) * 4 + z
            step, slot = place_ref[0, chip], place_ref[1, chip]
            for t in range(4):

                @pl.when(step == t)
                def _():
                    outs[t][slot] = total[row : row + 128]


def weight_grad_call(core, place, left, right, first, columns):
    width = 256 if columns % 256 == 0 else 384
    smem = pl.BlockSpec(memory_space=pltpu.SMEM)
    left_block = pl.BlockSpec((4, 128, D), lambda n, h: (0, 0, 0))
    right_block = pl.BlockSpec((1, 512, width), lambda n, h: (h, 0, first // width + n))
    return pl.pallas_call(
        weight_grad_kernel,
        grid=(columns // width, 2),
        in_specs=[smem, smem, left_block, left_block, right_block, right_block],
        out_specs=[pl.BlockSpec((4, 128, width), lambda n, h: (0, 0, n))] * 4,
        out_shape=[jax.ShapeDtypeStruct((4, 128, columns), jnp.bfloat16)] * 4,
        scratch_shapes=[pltpu.VMEM((1024, 1024), jnp.bfloat16)],
        compiler_params=pltpu.CompilerParams(vmem_limit_bytes=VMEM_LIMIT),
        cost_estimate=TINY,
    )(core, place, *left, *right)


def split_sum_kernel(place_ref, a_ref, b_ref, c_ref, d_ref, *out_refs):
    for t in range(4):
        i = (place_ref[0] + t) % 4
        total = sum(ref[i].astype(jnp.float32) for ref in (a_ref, b_ref, c_ref, d_ref))
        out_refs[t][...] = total.astype(jnp.bfloat16)


def split_sum_call(place, parts):
    columns = parts[0].shape[2]
    width = 256 if columns % 256 == 0 else 384
    return pl.pallas_call(
        split_sum_kernel,
        grid=(columns // width,),
        in_specs=[pl.BlockSpec(memory_space=pltpu.SMEM)]
        + [pl.BlockSpec((4, 128, width), lambda n: (0, 0, n))] * 4,
        out_specs=[pl.BlockSpec((128, width), lambda n: (0, n))] * 4,
        out_shape=[jax.ShapeDtypeStruct((128, columns), jnp.bfloat16)] * 4,
        compiler_params=pltpu.CompilerParams(vmem_limit_bytes=VMEM_LIMIT),
        cost_estimate=TINY,
    )(place, *parts)


def chip_places(y_first):
    y, z = jnp.arange(16, dtype=jnp.int32) // 4, jnp.arange(16, dtype=jnp.int32) % 4
    if y_first:
        return jnp.stack([(y - lax.axis_index(Y)) % 4, z])
    return jnp.stack([(z - lax.axis_index("z")) % 4, y])


def with_other(value):
    return value, swap_core(value)


def first_send(parts, y_first):
    axes = Y if y_first else ("z",)
    return [parts[0]] + [send(parts[t], axes, t) for t in (1, 3, 2)]


def first_sum(parts, y_first):
    return split_sum_call(lax.axis_index(("z",) if y_first else Y).reshape(1), parts)


def second_send(parts, y_first):
    axes = ("z",) if y_first else Y
    return [parts[0]] + [send(parts[t], axes, t) for t in (1, 3, 2)]


def head_masks():
    lane = lax.broadcasted_iota(jnp.int32, (128, 128), 1)
    low = lane < HEAD_DIM
    return low, low.astype(jnp.float32).astype(jnp.bfloat16), (~low).astype(jnp.float32).astype(jnp.bfloat16)


def attend_kernel(lo_ref, r_ref, o32_ref, o16_ref, lse_ref, s_ref):
    low, first_head, second_head = head_masks()
    row = lax.broadcasted_iota(jnp.int32, (256, 128), 0) % 128
    causal = row >= lax.broadcasted_iota(jnp.int32, (256, 128), 1)

    def one_query(q, _):
        query = r_ref[q, 4]
        stacked = jnp.concatenate([query * first_head, query * second_head], 0)
        lo = lo_ref[q]
        chunks = (q + 18 - lo) // 2

        def scores(kb):
            return mm(stacked, r_ref[kb & 15, (kb >> 4) * 2], 1, 1)

        def values(kb):
            return r_ref[kb & 15, (kb >> 4) * 2 + 1]

        s1 = jnp.where(causal, scores(q + 16), masked_score)
        s0 = jnp.where(q + 15 >= lo, scores(q + 15), masked_score)
        s_ref[0, :, :128] = s0
        s_ref[0, :, 128:] = s1

        def first(i, top):
            kb = q + 15 - 2 * i
            s1 = scores(kb + 1)
            s0 = jnp.where(kb >= lo, scores(kb), masked_score)
            s_ref[i, :, :128] = s0
            s_ref[i, :, 128:] = s1
            return jnp.maximum(top, jnp.maximum(s0, s1))

        top = lax.fori_loop(1, chunks, first, jnp.maximum(s0, s1))
        top = jnp.max(top, -1, keepdims=True)

        def second(i, carry):
            total, sums = carry
            kb = q + 15 - 2 * i
            p0 = jnp.exp(s_ref[i, :, :128] - top)
            p1 = jnp.exp(s_ref[i, :, 128:] - top)
            weights = jnp.concatenate([p0, p1], 1).astype(jnp.bfloat16)
            value = jnp.concatenate([values(kb), values(kb + 1)], 0)
            return total + p0 + p1, sums + mm(weights, value)

        empty = jnp.zeros((256, 128), jnp.float32)
        total, sums = lax.fori_loop(0, chunks, second, (empty, empty))
        total = jnp.sum(total, -1, keepdims=True)
        out = sums / total
        out = jnp.where(low, out[:128], out[128:])
        o32_ref[q] = out
        o16_ref[q] = out.astype(jnp.bfloat16)
        lse = jnp.broadcast_to(top + jnp.log(total), (256, 128))
        lse_ref[q] = jnp.transpose(lse)[:1]
        return 0

    lax.fori_loop(0, 16, one_query, 0)


def attend_call(lo, blocks):
    vmem = pl.BlockSpec(memory_space=pltpu.VMEM)
    return pl.pallas_call(
        attend_kernel,
        in_specs=[pl.BlockSpec(memory_space=pltpu.SMEM), vmem],
        out_specs=[vmem, vmem, vmem],
        out_shape=[
            jax.ShapeDtypeStruct((16, 128, 128), jnp.float32),
            jax.ShapeDtypeStruct((16, 128, 128), jnp.bfloat16),
            jax.ShapeDtypeStruct((16, 1, 256), jnp.float32),
        ],
        scratch_shapes=[pltpu.VMEM((8, 256, 256), jnp.float32)],
        compiler_params=pltpu.CompilerParams(vmem_limit_bytes=VMEM_LIMIT),
        cost_estimate=TINY,
    )(lo, blocks)


def attend_back_kernel(lo_ref, r_ref, do_ref, o32_ref, lse_ref, out_ref, dk_ref, dv_ref):
    low, first_head, second_head = head_masks()
    key_row = lax.broadcasted_iota(jnp.int32, (128, 256), 0)
    causal = key_row <= lax.broadcasted_iota(jnp.int32, (128, 256), 1) % 128
    dk_ref[...] = jnp.zeros_like(dk_ref)
    dv_ref[...] = jnp.zeros_like(dv_ref)

    def one_query(q, _):
        def stack(block):
            return jnp.concatenate([block * first_head, block * second_head], 0)

        queries = stack(r_ref[q, 4])
        grads = stack(do_ref[q])
        out = o32_ref[q]
        delta = grads.astype(jnp.float32) * jnp.concatenate([out, out], 0)
        delta = jnp.sum(jnp.transpose(delta), 0, keepdims=True)
        lse = lse_ref[q]
        lo = lo_ref[q]
        chunks = (q + 18 - lo) // 2

        def chunk(i, grad_query, mask1):
            kb = q + 15 - 2 * i

            def half(kb, mask):
                key = r_ref[kb & 15, (kb >> 4) * 2]
                value = r_ref[kb & 15, (kb >> 4) * 2 + 1]
                weights = jnp.exp(mm(key, queries, 1, 1) - lse)
                if mask is not None:
                    weights = jnp.where(mask, weights, 0.0)
                grad_scores = weights * (mm(value, grads, 1, 1) - delta)
                grad_scores = grad_scores.astype(jnp.bfloat16)
                dv_ref[kb] += mm(weights.astype(jnp.bfloat16), grads)
                dk_ref[kb] += mm(grad_scores, queries)
                return key, grad_scores

            key1, grad1 = half(kb + 1, mask1)
            key0, grad0 = half(kb, kb >= lo)
            keys = jnp.concatenate([key0, key1], 0)
            grad_scores = jnp.concatenate([grad0, grad1], 0)
            return grad_query + mm(grad_scores, keys, 0, 0)

        grad_query = chunk(0, jnp.zeros((256, 128), jnp.float32), causal)
        grad_query = lax.fori_loop(1, chunks, lambda i, g: chunk(i, g, None), grad_query)
        grad_query = jnp.where(low, grad_query[:128], grad_query[128:]) * score_scale
        out_ref[q, 4] = grad_query.astype(jnp.bfloat16)
        return 0

    lax.fori_loop(0, 16, one_query, 0)

    def finish(c, _):
        out_ref[c, 0] = dk_ref[c].astype(jnp.bfloat16)
        out_ref[c, 1] = dv_ref[c].astype(jnp.bfloat16)
        out_ref[c, 2] = dk_ref[c + 16].astype(jnp.bfloat16)
        out_ref[c, 3] = dv_ref[c + 16].astype(jnp.bfloat16)
        return 0

    lax.fori_loop(0, 16, finish, 0)


def attend_back_call(lo, blocks, grads, out, lse):
    vmem = pl.BlockSpec(memory_space=pltpu.VMEM)
    return pl.pallas_call(
        attend_back_kernel,
        in_specs=[pl.BlockSpec(memory_space=pltpu.SMEM), vmem, vmem, vmem, vmem],
        out_specs=vmem,
        out_shape=jax.ShapeDtypeStruct((16, 5, 128, 128), jnp.bfloat16),
        scratch_shapes=[
            pltpu.VMEM((32, 128, 128), jnp.float32),
            pltpu.VMEM((32, 128, 128), jnp.float32),
        ],
        compiler_params=pltpu.CompilerParams(vmem_limit_bytes=VMEM_LIMIT),
        cost_estimate=TINY,
    )(lo, blocks, grads, out, lse)


def turn_back_kernel(r_ref, halo_ref, cos_ref, up_ref, down_ref, out_ref, bias_ref):
    for j in range(2):
        sums = [jnp.zeros((1, 128), jnp.float32) for _ in range(3)]
        for x in range(4):
            rows = slice(x * 128, (x + 1) * 128)

            def turned(grad):
                return (
                    grad * cos_ref[rows]
                    - pltpu.roll(grad, 120, 1) * up_ref[rows]
                    - pltpu.roll(grad, 8, 1) * down_ref[rows]
                )

            def read(slot):
                later = r_ref[j, 0, x + 1, slot] if x < 3 else halo_ref[j, 0, slot]
                return r_ref[j, 0, x, slot + 2].astype(jnp.float32) + later.astype(jnp.float32)

            parts = (
                turned(r_ref[j, 0, x, 4].astype(jnp.float32)),
                turned(read(0)),
                read(1),
            )
            for part in range(3):
                grad = parts[part].astype(jnp.bfloat16)
                column = (j * 3 + part) * 128
                out_ref[0, rows, column : column + 128] = grad
                sums[part] = sums[part] + jnp.sum(grad.astype(jnp.float32), 0, keepdims=True)
        for part in range(3):
            column = (j * 3 + part) * 128
            bias_ref[0, :, column : column + 128] = sums[part]


def turn_back_call(blocks, halo, tables):
    table = pl.BlockSpec((512, 128), lambda h: (0, 0))
    return pl.pallas_call(
        turn_back_kernel,
        grid=(2,),
        in_specs=[
            pl.BlockSpec((2, 1, 4, 5, 128, 128), lambda h: (0, h, 0, 0, 0, 0)),
            pl.BlockSpec((2, 1, 2, 128, 128), lambda h: (0, h, 0, 0, 0)),
            table,
            table,
            table,
        ],
        out_specs=[
            pl.BlockSpec((1, 512, 768), lambda h: (h, 0, 0)),
            pl.BlockSpec((1, 1, 768), lambda h: (h, 0, 0)),
        ],
        out_shape=[
            jax.ShapeDtypeStruct((2, 512, 768), jnp.bfloat16),
            jax.ShapeDtypeStruct((2, 1, 768), jnp.float32),
        ],
        compiler_params=pltpu.CompilerParams(vmem_limit_bytes=VMEM_LIMIT),
        cost_estimate=TINY,
    )(blocks, halo, *tables)


def normed_back_kernel(core_ref, g_ref, own0_ref, own1_ref, oth0_ref, oth1_ref, out_ref):
    grads = jnp.concatenate([g_ref[0], g_ref[1]], 1)

    def rows(w0_ref, w1_ref):
        return jnp.concatenate(
            [w[:, :384] for h in range(2) for w in (w0_ref[0, h, 0, :128], w1_ref[h, 0, 0])], 1
        )

    weights = ordered(core_ref, rows(own0_ref, own1_ref), rows(oth0_ref, oth1_ref))
    out_ref[...] = mm(grads, weights, 1, 1).astype(jnp.bfloat16).reshape(4, 128, 256)


def normed_back_call(core, grad_joint, weights):
    first = pl.BlockSpec((1, 2, 1, 144, 512), lambda n: (n // 2, 0, n % 2, 0, 0))
    second = pl.BlockSpec((2, 1, 1, 128, 512), lambda n: (0, n % 2, n // 2, 0, 0))
    return pl.pallas_call(
        normed_back_kernel,
        grid=(8,),
        in_specs=[
            pl.BlockSpec(memory_space=pltpu.SMEM),
            pl.BlockSpec((2, 512, 768), lambda n: (0, 0, 0)),
            first,
            second,
            first,
            second,
        ],
        out_specs=pl.BlockSpec((4, 128, 256), lambda n: (0, 0, n)),
        out_shape=jax.ShapeDtypeStruct((4, 128, D), jnp.bfloat16),
        compiler_params=pltpu.CompilerParams(vmem_limit_bytes=VMEM_LIMIT),
        cost_estimate=TINY,
    )(core, grad_joint, *weights)


def local(
    tokens,
    cotangent,
    doc_ids,
    ln1_gain,
    ln1_shift,
    w_qkv,
    b_qkv,
    w_out,
    ln2_gain,
    ln2_shift,
    w_gate,
    w_up,
    w_down,
):
    half = lax.axis_index("yh")
    blk = lax.axis_index(BLK)

    core = lax.axis_index("k").reshape(1)
    vectors = jnp.stack([ln1_gain, ln1_shift, ln2_gain, ln2_shift])
    first_pair, second_pair = pack_joint_call(w_qkv.reshape(128, 768), w_out, vectors, b_qkv)
    ring = ring_gather(jnp.concatenate([tokens, cotangent], 0))
    own0 = gather(gather(first_pair, Y), ("z",)).reshape(4, 2, 2, 144, 512)
    own1 = gather(gather(second_pair, ("z",)), Y).reshape(2, 2, 4, 128, 512)
    own0 = after(own0, ring)
    weights = (own0, own1, swap_core(own0), swap_core(own1))
    rest = pack_hidden_call(w_gate, w_up, w_down)
    rest = after(rest, own0, own1)
    rest = lax.all_gather(rest, PLANE, axis=0, tiled=True).reshape(2, D, 3 * HID_PAD)

    small = jnp.stack([own0[:, :, :, 128:, :128], weights[2][:, :, :, 128:, :128]])
    small = jnp.where(core[0] == 0, small, small[::-1]).astype(jnp.float32)
    bias = small[..., 8:11, :16].transpose(2, 4, 1, 3, 0, 5).reshape(2, 3, 2, 128).reshape(2, 3, 1, 256)
    vectors = small[:, :, 0, :, :4].transpose(3, 1, 2, 0, 4).reshape(4, D)
    gain_one, shift_one, gain_two, shift_two = [vectors[i : i + 1] for i in range(4)]

    first_block = jnp.sum((doc_ids[None, :] < doc_ids[:, None]).astype(jnp.int32), axis=1)
    cycles = jnp.arange(4, dtype=jnp.int32) * 16 + half * 64 + blk
    cycles = jnp.concatenate([cycles, 48 + blk.reshape(1)])
    block_position = (cycles - first_block[cycles]) * BLK_TOK
    positions = (block_position[:, None] + jnp.arange(BLK_TOK, dtype=jnp.int32)).reshape(640)
    tables = rotary_tables(positions)
    first_query = half * 64 + (blk % 4) * 16
    lo = lax.dynamic_slice(first_block, (first_query,), (16,)) - (first_query - 16)

    before = lax.ppermute(ring[3, :128], ("yh",), [(0, 1)])
    payload, normed_one = qkv_call(core, ring, before, gain_one, shift_one, weights, bias, tables)
    blocks = exchange(payload.reshape(16, 5, 128, 128), BLK)
    att32, att16, lse = attend_call(lo, blocks)
    attended = exchange(att16, BLK).reshape(2, 2, 4, 128, 128)
    came = exchange(project_call(core, attended, weights), ("x",))
    token_shape = jax.ShapeDtypeStruct((128, D), jnp.float32)
    ring_shape = jax.ShapeDtypeStruct((4, 128, D), jnp.bfloat16)
    vector_shape = jax.ShapeDtypeStruct((1, D), jnp.float32)
    middle, normed_two = whole_call(
        middle_kernel, [token_shape, ring_shape], came, tokens, gain_two, shift_two
    )

    ring_two = exchange(normed_two, ("x",))
    active, grad_gu, ring_grad, ring_out = feed_forward_call(ring_two, ring, rest)
    shared = plane_grad_call(core, with_other(ring), with_other(active), HID_PAD, 1, 2 * HID_PAD)
    came = after(exchange(ring_grad, ("x",)), shared)
    grad_middle, ring_branch, grad_gain_two, grad_shift_two = whole_call(
        middle_back_kernel,
        [token_shape, ring_shape, vector_shape, vector_shape],
        came,
        middle,
        cotangent,
        gain_two,
    )
    shared = plane_grad_call(
        core, with_other(ring_two), with_other(grad_gu), 2 * HID_PAD, 0, 0, shared
    )
    ring_branch = after(exchange(ring_branch, ("x",)), shared)
    grad_att = project_back_call(core, ring_branch, weights).reshape(16, 128, 128)
    attended = attended.transpose(1, 2, 3, 0, 4).reshape(2, 512, 256)
    shared = plane_grad_call(
        core, with_other(ring_branch), with_other(attended), 256, 0, 3 * HID_PAD, shared
    )
    shared = lax.psum_scatter(
        shared.reshape(2048, SHARED), ("yh", "yl", "z"), scatter_dimension=0, tiled=True
    )
    grad_att = exchange(grad_att, BLK)

    out_came = exchange(after(ring_out, grad_att), ("x",))
    back = attend_back_call(lo, blocks, grad_att, att32, lse)
    mixed = whole_call(
        mixed_kernel, jax.ShapeDtypeStruct((128, D), jnp.bfloat16), after(out_came, back), middle
    )
    back = exchange(back, BLK).reshape(2, 2, 4, 5, 128, 128)
    back = after(back, mixed)
    halo_back = lax.ppermute(back[:, :, 0, :2], ("yh",), [(1, 0)])
    grad_joint, grad_bias = turn_back_call(back, halo_back, tables)
    ring_one = normed_back_call(core, grad_joint, weights)
    places = (chip_places(True), chip_places(False))
    joint_left, joint_right = with_other(normed_one), with_other(grad_joint)
    pair_parts = [
        weight_grad_call(core, places[j], joint_left, joint_right, j * 384, 384) for j in range(2)
    ]
    pair_came = [first_send(part, j == 0) for j, part in enumerate(pair_parts)]
    came = after(exchange(ring_one, ("x",)), pair_parts[0][0], pair_parts[1][0])
    input_grad, grad_gain_one, grad_shift_one = whole_call(
        input_back_kernel,
        [token_shape, vector_shape, vector_shape],
        came,
        tokens,
        grad_middle,
        gain_one,
    )
    pair_came = [second_send(first_sum(part, j == 0), j == 0) for j, part in enumerate(pair_came)]

    def shape(*dims):
        return jax.ShapeDtypeStruct(dims, jnp.float32)

    grad_gate, grad_up, grad_down, grad_out = whole_call(
        shared_end_kernel,
        [shape(128, HID), shape(128, HID), shape(HID, 128), shape(256, 128)],
        after(shared, input_grad),
    )
    grad_qkv = whole_call(joint_end_kernel, shape(128, 768), *pair_came[0], *pair_came[1])

    norms = jnp.concatenate([grad_gain_one, grad_shift_one, grad_gain_two, grad_shift_two], 0)
    norms = norms.reshape(4, 2, 4, 16, 16).transpose(1, 2, 3, 0, 4).reshape(2, 4, 16, 64)
    biases = grad_bias.reshape(2, 2, 3, 8, 16).transpose(0, 1, 3, 2, 4).reshape(2, 1, 16, 48)
    plane = jnp.arange(4).reshape(1, 4, 1, 1) == lax.axis_index("x")
    biases = jnp.where(plane, biases, 0.0)
    sums = jnp.concatenate([norms, biases, jnp.zeros((2, 4, 16, 16), jnp.float32)], 3)
    sums = jnp.sum(exchange(sums.reshape(128, 128), AXES), 0)
    norms = sums[:64].reshape(4, 16)

    return (
        mixed,
        input_grad,
        norms[0],
        norms[1],
        grad_qkv.reshape(128, 3, 256),
        sums[64:112].reshape(3, 16),
        grad_out,
        norms[2],
        norms[3],
        grad_gate,
        grad_up,
        grad_down,
    )


def solution(mesh):
    whole = Mesh(mesh.devices.reshape(2, 4, 4, 2, 2), AXES)
    ulysses, blk = ("yh", "x"), BLK
    both = ulysses + blk
    placed = (
        P(both, None),
        P(both, None),
        P(),
        P(blk),
        P(blk),
        P(blk, None, ulysses),
        P(None, both),
        P(ulysses, blk),
        P(blk),
        P(blk),
        P(blk, ulysses),
        P(blk, ulysses),
        P(ulysses, blk),
    )
    return jax.shard_map(
        local,
        mesh=whole,
        in_specs=placed,
        out_specs=(
            P(both, None),
            P(both, None),
            P(both),
            P(both),
            P(blk, None, ulysses),
            P(None, both),
            P(ulysses, blk),
            P(both),
            P(both),
            P(blk, ulysses),
            P(blk, ulysses),
            P(ulysses, blk),
        ),
        check_vma=False,
    )
```

```python
import functools

import jax
import jax.numpy as jnp
from jax import lax
from jax.experimental import pallas as pl
from jax.experimental.pallas import tpu as pltpu
from jax.sharding import Mesh
from jax.sharding import PartitionSpec as P

D = 2048
HEADS = 32
HEAD_DIM = 64
ROT = 16
BLK_TOK = 128
HID = 704
HID_PAD = 768
SHARED = 3 * HID_PAD

eps = 1e-05
rope_base = 10000.0
masked_score = -1e30
score_scale = HEAD_DIM ** (-0.5)

AXES = ("yh", "x", "z", "yl", "k")
PLANE = ("yh", "z", "yl", "k")
BLK = ("z", "yl", "k")
Y = ("yh", "yl")

VMEM_LIMIT = 60 * 1024 * 1024
TINY = pl.CostEstimate(flops=1, bytes_accessed=1, transcendentals=0)


def mm(a, b, ca=1, cb=0):
    return lax.dot_general(a, b, (((ca,), (cb,)), ((), ())), preferred_element_type=jnp.float32)


def swap_core(value):
    return lax.ppermute(value, ("k",), [(0, 1), (1, 0)])


def exchange(parts, axes):
    return lax.all_to_all(parts, axes, 0, 0, tiled=True)


def send(value, axes, step):
    return lax.ppermute(value, axes, [(i, (i + step) % 4) for i in range(4)])


def gather(value, axes, *others):
    me = lax.axis_index(axes)
    pieces = [send(value, axes, step) for step in (1, 3, 2)]
    if others:
        pieces = after(pieces, *others)
    buffer = jnp.zeros((4,) + value.shape, value.dtype)
    for step, piece in zip((0, 1, 3, 2), [value] + pieces):
        buffer = lax.dynamic_update_index_in_dim(buffer, piece, (me - step) % 4, 0)
    return buffer


def ring_gather(value):
    return exchange(jnp.broadcast_to(value, (4,) + value.shape), ("x",))


def send(value, axes, step):
    return lax.ppermute(value, axes, [(i, (i + step) % 4) for i in range(4)])


def gather(value, axes, *others):
    me = lax.axis_index(axes)
    pieces = [send(value, axes, step) for step in (1, 3, 2)]
    if others:
        pieces = after(pieces, *others)
    buffer = jnp.zeros((4,) + value.shape, value.dtype)
    for step, piece in zip((0, 1, 3, 2), [value] + pieces):
        buffer = lax.dynamic_update_index_in_dim(buffer, piece, (me - step) % 4, 0)
    return buffer


def ring_gather(value):
    return exchange(jnp.broadcast_to(value, (4,) + value.shape), ("x",))


def after(value, *others):
    return lax.optimization_barrier((value,) + others)[0]


def rotary_tables(positions):
    halfway = ROT // 2
    counter = jnp.arange(halfway, dtype=jnp.float32)
    frequency = rope_base ** (-2.0 * counter / ROT)
    lane = jnp.arange(128) % HEAD_DIM
    frequency = jnp.where(lane < ROT, jnp.tile(frequency, 16), 0.0)
    angles = positions.astype(jnp.float32)[:, None] * frequency[None, :]
    sine = jnp.sin(angles)
    return (
        jnp.cos(angles),
        jnp.where(lane < halfway, -sine, 0.0),
        jnp.where((lane >= halfway) & (lane < ROT), sine, 0.0),
    )


def pack_joint_kernel(qkv_ref, out_ref, vectors_ref, bias_ref, h0_ref, h1_ref, small_ref):
    out_t = jnp.transpose(out_ref[...])
    for j, h_ref in enumerate((h0_ref, h1_ref)):
        for part in range(3):
            h_ref[:128, part * 128 : (part + 1) * 128] = qkv_ref[part, :, j * 128 : (j + 1) * 128]
        h_ref[:128, 384:] = out_t[:, j * 128 : (j + 1) * 128]
    small_ref[...] = jnp.zeros_like(small_ref)
    small_ref[0:4, :128] = vectors_ref[...].astype(jnp.float32)
    small_ref[8:11, :16] = bias_ref[...].astype(jnp.float32)
    h0_ref[128:, :] = small_ref[...].astype(jnp.bfloat16)


def pack_joint_call(qkv, out, vectors, bias):
    vmem = pl.BlockSpec(memory_space=pltpu.VMEM)
    return pl.pallas_call(
        pack_joint_kernel,
        in_specs=[vmem] * 4,
        out_specs=[vmem] * 2,
        out_shape=[
            jax.ShapeDtypeStruct((144, 512), jnp.bfloat16),
            jax.ShapeDtypeStruct((128, 512), jnp.bfloat16),
        ],
        scratch_shapes=[pltpu.VMEM((16, 512), jnp.float32)],
    )(qkv, out, vectors, bias)


def pack_hidden_kernel(gate_ref, up_ref, down_ref, rest_ref):
    for i, ref in enumerate((gate_ref, up_ref, down_ref)):
        first = i * HID_PAD
        rest_ref[:, first + HID_PAD - 128 : first + HID_PAD] = jnp.zeros((128, 128), jnp.bfloat16)
        rest_ref[:, first : first + HID] = jnp.transpose(ref[...])


def pack_hidden_call(gate, up, down):
    return whole_call(
        pack_hidden_kernel, jax.ShapeDtypeStruct((128, 3 * HID_PAD), jnp.bfloat16), gate, up, down
    )


def core_columns(ref, core, blocks):
    columns = [ref[:blocks, :, pl.ds(pl.multiple_of((2 * i + core) * 128, 128), 128)] for i in range(8)]
    return jnp.concatenate(columns, 2).reshape(blocks * 128, 1024)


def core_rows(w0_ref, w1_ref):
    w0 = jnp.concatenate([w0_ref[z, 0, yl, :128] for z in range(4) for yl in range(2)], 0)
    w1 = jnp.concatenate([w1_ref[0, yl, z] for z in range(4) for yl in range(2)], 0)
    return jnp.concatenate([w0, w1], 1)


def normalise(values):
    centred = values - jnp.mean(values, -1, keepdims=True)
    inverse = lax.rsqrt(jnp.mean(centred * centred, -1, keepdims=True) + eps)
    return centred * inverse, inverse


def qkv_kernel(
    core_ref,
    x_ref,
    before_ref,
    gain_ref,
    shift_ref,
    own0_ref,
    own1_ref,
    oth0_ref,
    oth1_ref,
    bias_ref,
    cos_ref,
    up_ref,
    down_ref,
    out_ref,
    normed_ref,
    unit_ref,
    x_cores,
):
    part = pl.program_id(1)
    core = core_ref[0]

    @pl.when((pl.program_id(0) == 0) & (part == 0))
    def _():
        for b in range(5):
            block = x_ref[b] if b < 4 else before_ref[...]
            unit, _ = normalise(block.astype(jnp.float32))
            normed = (unit * gain_ref[...] + shift_ref[...]).astype(jnp.bfloat16)
            if b < 4:
                normed_ref[b] = normed
                unit_ref[b] = unit.astype(jnp.bfloat16)
            for c in range(16):
                column = pl.multiple_of((c // 2 + 8 * ((c + core) % 2)) * 128, 128)
                x_cores[b * 128 : (b + 1) * 128, pl.ds(column, 128)] = normed[:, c * 128 : (c + 1) * 128]

    def joint(rows):
        weights = jnp.concatenate([core_rows(own0_ref, own1_ref), core_rows(oth0_ref, oth1_ref)], 0)
        return mm(x_cores[:rows], weights) + bias_ref[0, 0]

    def turned(value):
        rows = value.shape[0]
        return (
            value * cos_ref[:rows]
            + pltpu.roll(value, 120, 1) * up_ref[:rows]
            + pltpu.roll(value, 8, 1) * down_ref[:rows]
        )

    @pl.when(part == 0)
    def _():
        value = joint(512)
        for j in range(2):
            query = turned(value[:, j * 128 : (j + 1) * 128]) * score_scale
            out_ref[j, 0, :, 4] = query.astype(jnp.bfloat16).reshape(4, 128, 128)

    @pl.when(part > 0)
    def _():
        value = joint(640)
        for j in range(2):
            block = value[:, j * 128 : (j + 1) * 128]
            block = jnp.where(part == 1, turned(block), block)
            block = block.astype(jnp.bfloat16).reshape(5, 128, 128)

            @pl.when(part == 1)
            def _():
                out_ref[j, 0, :, 2] = block[:4]
                out_ref[j, 0, 1:, 0] = block[:3]
                out_ref[j, 0, 0, 0] = block[4]

            @pl.when(part == 2)
            def _():
                out_ref[j, 0, :, 3] = block[:4]
                out_ref[j, 0, 1:, 1] = block[:3]
                out_ref[j, 0, 0, 1] = block[4]


def qkv_call(core, tokens, before, gain, shift, weights, bias, tables):
    table = pl.BlockSpec((640, 128), lambda h, p: (0, 0))
    vector = pl.BlockSpec((1, D), lambda h, p: (0, 0))
    first = pl.BlockSpec((4, 1, 2, 144, 128), lambda h, p: (0, h, 0, 0, p))
    second = pl.BlockSpec((1, 2, 4, 128, 128), lambda h, p: (h, 0, 0, 0, p))
    return pl.pallas_call(
        qkv_kernel,
        grid=(2, 3),
        in_specs=[
            pl.BlockSpec(memory_space=pltpu.SMEM),
            pl.BlockSpec((4, 128, D), lambda h, p: (0, 0, 0)),
            pl.BlockSpec((128, D), lambda h, p: (0, 0)),
            vector,
            vector,
            first,
            second,
            first,
            second,
            pl.BlockSpec((1, 1, 1, 256), lambda h, p: (h, p, 0, 0)),
            table,
            table,
            table,
        ],
        out_specs=[
            pl.BlockSpec((2, 1, 4, 5, 128, 128), lambda h, p: (0, h, 0, 0, 0, 0)),
            pl.BlockSpec((4, 128, D), lambda h, p: (0, 0, 0)),
            pl.BlockSpec((4, 128, D), lambda h, p: (0, 0, 0)),
        ],
        out_shape=[
            jax.ShapeDtypeStruct((2, 2, 4, 5, 128, 128), jnp.bfloat16),
            jax.ShapeDtypeStruct((4, 128, D), jnp.bfloat16),
            jax.ShapeDtypeStruct((4, 128, D), jnp.bfloat16),
        ],
        scratch_shapes=[pltpu.VMEM((640, D), jnp.bfloat16)],
        compiler_params=pltpu.CompilerParams(vmem_limit_bytes=VMEM_LIMIT),
        cost_estimate=TINY,
    )(core, tokens, before, gain, shift, *weights, bias, *tables)


def whole_call(kernel, out_shape, *operands, scratch=()):
    vmem = pl.BlockSpec(memory_space=pltpu.VMEM)
    return pl.pallas_call(
        kernel,
        in_specs=[vmem] * len(operands),
        out_specs=jax.tree.map(lambda _: vmem, out_shape),
        out_shape=out_shape,
        scratch_shapes=list(scratch),
        compiler_params=pltpu.CompilerParams(vmem_limit_bytes=VMEM_LIMIT),
        cost_estimate=TINY,
    )(*operands)


def middle_kernel(came_ref, tokens_ref, gain_ref, shift_ref, middle_ref, normed_ref):
    middle = tokens_ref[...].astype(jnp.float32)
    for i in range(4):
        middle = middle + came_ref[i].astype(jnp.float32)
    middle_ref[...] = middle
    normed = (normalise(middle)[0] * gain_ref[...] + shift_ref[...]).astype(jnp.bfloat16)
    for i in range(4):
        normed_ref[i] = normed


def back_through(came_ref, values, gain):
    grad = came_ref[0].astype(jnp.float32)
    for i in range(1, 4):
        grad = grad + came_ref[i].astype(jnp.float32)
    unit, inverse = normalise(values)
    grad_unit = grad * gain
    centred_grad = (
        grad_unit
        - jnp.mean(grad_unit, -1, keepdims=True)
        - unit * jnp.mean(grad_unit * unit, -1, keepdims=True)
    )
    gain_grad = jnp.sum(grad * unit, 0, keepdims=True)
    return inverse * centred_grad, gain_grad, jnp.sum(grad, 0, keepdims=True)


def middle_back_kernel(came_ref, middle_ref, cot_ref, gain_ref, grad_ref, ring_ref, gain_grad_ref, shift_grad_ref):
    grad, gain_grad_ref[...], shift_grad_ref[...] = back_through(came_ref, middle_ref[...], gain_ref[...])
    grad = grad + cot_ref[...].astype(jnp.float32)
    grad_ref[...] = grad
    for i in range(4):
        ring_ref[i] = grad.astype(jnp.bfloat16)


def input_back_kernel(came_ref, tokens_ref, grad_ref, gain_ref, out_ref):
    values = tokens_ref[...].astype(jnp.float32)
    out_ref[...] = grad_ref[...] + back_through(came_ref, values, gain_ref[...])[0]


def mixed_kernel(came_ref, middle_ref, out_ref):
    total = middle_ref[...]
    for i in range(4):
        total = total + came_ref[i].astype(jnp.float32)
    out_ref[...] = total.astype(jnp.bfloat16)


def shared_end_kernel(total_ref, gate_ref, up_ref, down_ref):
    total = jnp.transpose(total_ref[...].astype(jnp.float32))
    for c in range(3):
        width = min(HID, c * 256 + 256) - c * 256
        gate_ref[c * 256 : c * 256 + width] = total[c * 512 : c * 512 + width]
        up_ref[c * 256 : c * 256 + width] = total[c * 512 + 256 : c * 512 + 256 + width]
    down_ref[...] = total[2 * HID_PAD : 2 * HID_PAD + HID]


def out_end_kernel(*refs):
    refs[4][...] = jnp.transpose(sum(ref[...].astype(jnp.float32) for ref in refs[:4]))


def joint_end_kernel(*refs):
    for j in range(2):
        total = sum(ref[...].astype(jnp.float32) for ref in refs[4 * j : 4 * j + 4])
        for part in range(3):
            refs[8][part, :, j * 128 : (j + 1) * 128] = total[:, part * 128 : part * 128 + 128]


def ordered(core_ref, own, other):
    first = core_ref[0] == 0
    return jnp.concatenate([jnp.where(first, own, other), jnp.where(first, other, own)], 0)


def project_kernel(core_ref, att_ref, own0_ref, own1_ref, oth0_ref, oth1_ref, out_ref):
    att = jnp.concatenate([att_ref[j, h].reshape(512, 128) for h in range(2) for j in range(2)], 1)

    def rows(w0_ref, w1_ref, yl):
        return jnp.concatenate(
            [w for h in range(2) for w in (w0_ref[0, h, yl, :128], w1_ref[h, yl, 0])], 1
        )

    weights = jnp.concatenate(
        [ordered(core_ref, rows(own0_ref, own1_ref, yl), rows(oth0_ref, oth1_ref, yl)) for yl in range(2)], 0
    )
    out_ref[...] = mm(att, weights, 1, 1).astype(jnp.bfloat16).reshape(4, 128, 512)


def project_call(core, att, weights):
    first = pl.BlockSpec((1, 2, 2, 144, 128), lambda n: (n, 0, 0, 0, 3))
    second = pl.BlockSpec((2, 2, 1, 128, 128), lambda n: (0, 0, n, 0, 3))
    return pl.pallas_call(
        project_kernel,
        grid=(4,),
        in_specs=[
            pl.BlockSpec(memory_space=pltpu.SMEM),
            pl.BlockSpec((2, 2, 4, 128, 128), lambda n: (0, 0, 0, 0, 0)),
            first,
            second,
            first,
            second,
        ],
        out_specs=pl.BlockSpec((4, 128, 512), lambda n: (0, 0, n)),
        out_shape=jax.ShapeDtypeStruct((4, 128, D), jnp.bfloat16),
        compiler_params=pltpu.CompilerParams(vmem_limit_bytes=VMEM_LIMIT),
        cost_estimate=TINY,
    )(core, att, *weights)


def project_back_kernel(core_ref, grad_ref, own0_ref, own1_ref, oth0_ref, oth1_ref, out_ref):
    core = core_ref[0]
    grad = mm(core_columns(grad_ref, core, 4), core_rows(own0_ref, own1_ref))
    grad = grad + mm(core_columns(grad_ref, 1 - core, 4), core_rows(oth0_ref, oth1_ref))
    grad = grad.astype(jnp.bfloat16)
    for j in range(2):
        out_ref[j, 0] = grad[:, j * 128 : (j + 1) * 128].reshape(4, 128, 128)


def project_back_call(core, grad, weights):
    first = pl.BlockSpec((4, 1, 2, 144, 128), lambda h: (0, h, 0, 0, 3))
    second = pl.BlockSpec((1, 2, 4, 128, 128), lambda h: (h, 0, 0, 0, 3))
    return pl.pallas_call(
        project_back_kernel,
        grid=(2,),
        in_specs=[
            pl.BlockSpec(memory_space=pltpu.SMEM),
            pl.BlockSpec((4, 128, D), lambda h: (0, 0, 0)),
            first,
            second,
            first,
            second,
        ],
        out_specs=pl.BlockSpec((2, 1, 4, 128, 128), lambda h: (0, h, 0, 0, 0)),
        out_shape=jax.ShapeDtypeStruct((2, 2, 4, 128, 128), jnp.bfloat16),
        compiler_params=pltpu.CompilerParams(vmem_limit_bytes=VMEM_LIMIT),
        cost_estimate=TINY,
    )(core, grad, *weights)


def feed_forward_kernel(
    x_ref, cot_ref, gate_ref, up_ref, down_ref, active_ref, grads_ref, back_ref, out_ref, back_sum, out_sum
):
    step = pl.program_id(0) * 3 + pl.program_id(1)
    x = x_ref[...].reshape(512, D)
    gate = mm(x, gate_ref[0])
    up = mm(x, up_ref[0])
    grad_active = mm(cot_ref[...].reshape(512, D), down_ref[0])
    sigmoid = jax.nn.sigmoid(gate)
    silu = gate * sigmoid
    active = (silu * up).astype(jnp.bfloat16)
    grad_gate = (grad_active * up * (sigmoid + silu * (1.0 - sigmoid))).astype(jnp.bfloat16)
    grad_up = (grad_active * silu).astype(jnp.bfloat16)
    grads = jnp.concatenate([grad_gate, grad_up], 1)
    active_ref[0] = active
    grads_ref[0] = grads
    back = mm(grads, jnp.concatenate([gate_ref[0], up_ref[0]], 1), 1, 1)
    out = mm(active, down_ref[0], 1, 1)

    @pl.when(step == 0)
    def _():
        back_sum[...] = back
        out_sum[...] = out

    @pl.when((step > 0) & (step < 5))
    def _():
        back_sum[...] += back
        out_sum[...] += out

    @pl.when(step == 5)
    def _():
        back_ref[...] = (back_sum[...] + back).astype(jnp.bfloat16).reshape(4, 128, D)
        out_ref[...] = (out_sum[...] + out).astype(jnp.bfloat16).reshape(4, 128, D)


def feed_forward_call(x, ring, rest):
    tokens = pl.BlockSpec((4, 128, D), lambda h, c: (0, 0, 0))
    weight = [pl.BlockSpec((1, D, 256), lambda h, c, first=first: (h, 0, first + c)) for first in (0, 3, 6)]
    ring_shape = jax.ShapeDtypeStruct((4, 128, D), jnp.bfloat16)
    return pl.pallas_call(
        feed_forward_kernel,
        grid=(2, 3),
        in_specs=[tokens, tokens] + weight,
        out_specs=[
            pl.BlockSpec((1, 512, 256), lambda h, c: (h, 0, c)),
            pl.BlockSpec((1, 512, 512), lambda h, c: (h, 0, c)),
            tokens,
            tokens,
        ],
        out_shape=[
            jax.ShapeDtypeStruct((2, 512, HID_PAD), jnp.bfloat16),
            jax.ShapeDtypeStruct((2, 512, 2 * HID_PAD), jnp.bfloat16),
            ring_shape,
            ring_shape,
        ],
        scratch_shapes=[pltpu.VMEM((512, D), jnp.float32), pltpu.VMEM((512, D), jnp.float32)],
        compiler_params=pltpu.CompilerParams(vmem_limit_bytes=VMEM_LIMIT),
        cost_estimate=TINY,
    )(x, ring, rest, rest, rest)


def plane_grad_kernel(core_ref, left_ref, left_other_ref, right_ref, right_other_ref, *refs):
    out_ref, left_t = refs[-2:]

    @pl.when((pl.program_id(0) == 0) & (pl.program_id(1) == 0))
    def _():
        left_t[:, :512] = jnp.transpose(core_columns(left_ref, core_ref[0], 4))
        left_t[:, 512:] = jnp.transpose(core_columns(left_other_ref, core_ref[0], 4))

    total = mm(left_t[...], jnp.concatenate([right_ref[0], right_other_ref[0]], 0)).astype(jnp.bfloat16)
    for z in range(4):
        for yl in range(2):
            row = (z * 2 + yl) * 128
            out_ref[0, yl, z] = total[row : row + 128]


def plane_grad_call(core, left, right, columns, first, shared=None):
    left_block = pl.BlockSpec((4, 128, D), lambda n, h: (0, 0, 0))
    right_block = pl.BlockSpec((1, 512, 256), lambda n, h: (h, 0, n))
    extra = [] if shared is None else [shared]
    return pl.pallas_call(
        plane_grad_kernel,
        grid=(columns // 256, 2),
        in_specs=[
            pl.BlockSpec(memory_space=pltpu.SMEM),
            left_block,
            left_block,
            right_block,
            right_block,
        ]
        + [pl.BlockSpec(memory_space=pl.ANY)] * len(extra),
        out_specs=pl.BlockSpec((1, 2, 4, 128, 256), lambda n, h: (h, 0, 0, 0, first // 256 + n)),
        out_shape=jax.ShapeDtypeStruct((2, 2, 4, 128, SHARED), jnp.bfloat16),
        input_output_aliases={5: 0} if extra else {},
        scratch_shapes=[pltpu.VMEM((1024, 1024), jnp.bfloat16)],
        compiler_params=pltpu.CompilerParams(vmem_limit_bytes=VMEM_LIMIT),
        cost_estimate=TINY,
    )(core, *left, *right, *extra)


def weight_grad_kernel(core_ref, place_ref, left_ref, left_other_ref, right_ref, right_other_ref, *refs):
    outs, left_t = refs[:4], refs[4]
    h = pl.program_id(1)

    @pl.when((h == 0) & (pl.program_id(0) == 0))
    def _():
        left_t[:, :512] = jnp.transpose(core_columns(left_ref, core_ref[0], 4))
        left_t[:, 512:] = jnp.transpose(core_columns(left_other_ref, core_ref[0], 4))

    total = mm(left_t[...], jnp.concatenate([right_ref[0], right_other_ref[0]], 0)).astype(jnp.bfloat16)
    for z in range(4):
        for yl in range(2):
            row = (z * 2 + yl) * 128
            chip = (h * 2 + yl) * 4 + z
            step, slot = place_ref[0, chip], place_ref[1, chip]
            for t in range(4):

                @pl.when(step == t)
                def _():
                    outs[t][slot] = total[row : row + 128]


def weight_grad_call(core, place, left, right, columns):
    smem = pl.BlockSpec(memory_space=pltpu.SMEM)
    left_block = pl.BlockSpec((4, 128, D), lambda n, h: (0, 0, 0))
    right_block = pl.BlockSpec((1, 512, 256), lambda n, h: (h, 0, n))
    return pl.pallas_call(
        weight_grad_kernel,
        grid=(columns // 256, 2),
        in_specs=[smem, smem, left_block, left_block, right_block, right_block],
        out_specs=[pl.BlockSpec((4, 128, 256), lambda n, h: (0, 0, n))] * 4,
        out_shape=[jax.ShapeDtypeStruct((4, 128, columns), jnp.bfloat16)] * 4,
        scratch_shapes=[pltpu.VMEM((1024, 1024), jnp.bfloat16)],
        compiler_params=pltpu.CompilerParams(vmem_limit_bytes=VMEM_LIMIT),
        cost_estimate=TINY,
    )(core, place, *left, *right)


def joint_grad_kernel(core_ref, place_ref, left_ref, left_other_ref, right_ref, right_other_ref, *refs):
    outs, left_t = refs[:8], refs[8]
    h = pl.program_id(0)

    @pl.when(h == 0)
    def _():
        left_t[:, :512] = jnp.transpose(core_columns(left_ref, core_ref[0], 4))
        left_t[:, 512:] = jnp.transpose(core_columns(left_other_ref, core_ref[0], 4))

    right = jnp.concatenate([right_ref[0], right_other_ref[0]], 0)
    total = mm(left_t[...], right).astype(jnp.bfloat16)
    for z in range(4):
        for yl in range(2):
            row = (z * 2 + yl) * 128
            chip = (h * 2 + yl) * 4 + z
            for j in range(2):
                step, slot = place_ref[2 * j, chip], place_ref[2 * j + 1, chip]
                for t in range(4):

                    @pl.when(step == t)
                    def _():
                        outs[4 * j + t][slot] = total[row : row + 128, j * 384 : j * 384 + 384]


def joint_grad_call(core, places, left, right):
    smem = pl.BlockSpec(memory_space=pltpu.SMEM)
    left_block = pl.BlockSpec((4, 128, D), lambda h: (0, 0, 0))
    right_block = pl.BlockSpec((1, 512, 768), lambda h: (h, 0, 0))
    return pl.pallas_call(
        joint_grad_kernel,
        grid=(2,),
        in_specs=[smem, smem, left_block, left_block, right_block, right_block],
        out_specs=[pl.BlockSpec((4, 128, 384), lambda h: (0, 0, 0))] * 8,
        out_shape=[jax.ShapeDtypeStruct((4, 128, 384), jnp.bfloat16)] * 8,
        scratch_shapes=[pltpu.VMEM((1024, 1024), jnp.bfloat16)],
        compiler_params=pltpu.CompilerParams(vmem_limit_bytes=VMEM_LIMIT),
        cost_estimate=TINY,
    )(core, jnp.concatenate(places, 0), *left, *right)


def split_sum_kernel(place_ref, a_ref, b_ref, c_ref, d_ref, *out_refs):
    for t in range(4):
        i = (place_ref[0] + t) % 4
        total = sum(ref[i].astype(jnp.float32) for ref in (a_ref, b_ref, c_ref, d_ref))
        out_refs[t][...] = total.astype(jnp.bfloat16)


def split_sum_call(place, parts):
    columns = parts[0].shape[2]
    width = 256 if columns % 256 == 0 else 384
    return pl.pallas_call(
        split_sum_kernel,
        grid=(columns // width,),
        in_specs=[pl.BlockSpec(memory_space=pltpu.SMEM)]
        + [pl.BlockSpec((4, 128, width), lambda n: (0, 0, n))] * 4,
        out_specs=[pl.BlockSpec((128, width), lambda n: (0, n))] * 4,
        out_shape=[jax.ShapeDtypeStruct((128, columns), jnp.bfloat16)] * 4,
        compiler_params=pltpu.CompilerParams(vmem_limit_bytes=VMEM_LIMIT),
        cost_estimate=TINY,
    )(place, *parts)


def chip_places(y_first):
    y, z = jnp.arange(16, dtype=jnp.int32) // 4, jnp.arange(16, dtype=jnp.int32) % 4
    if y_first:
        return jnp.stack([(y - lax.axis_index(Y)) % 4, z])
    return jnp.stack([(z - lax.axis_index("z")) % 4, y])


def plane_sum(parts):
    parts = parts.reshape(2048, parts.shape[-1])
    return lax.psum_scatter(parts, ("yh", "yl", "z"), scatter_dimension=0, tiled=True)


def with_other(value):
    return value, swap_core(value)


def first_send(parts, y_first):
    axes = Y if y_first else ("z",)
    return [parts[0]] + [send(parts[t], axes, t) for t in (1, 3, 2)]


def first_sum(parts, y_first):
    return split_sum_call(lax.axis_index(("z",) if y_first else Y).reshape(1), parts)


def second_send(parts, y_first):
    axes = ("z",) if y_first else Y
    return [parts[0]] + [send(parts[t], axes, t) for t in (1, 3, 2)]


def stack_heads(ref, *index):
    first = (lax.broadcasted_iota(jnp.int32, (128, 128), 1) < HEAD_DIM).astype(jnp.float32).astype(jnp.bfloat16)
    masks = (first, 1 - first)
    return jnp.concatenate([ref[i] * mask for i in index for mask in masks], 0)


def unstack_heads(values, block):
    low = lax.broadcasted_iota(jnp.int32, (128, 128), 1) < HEAD_DIM
    rows = values[block * 256 : block * 256 + 256]
    return jnp.where(low, rows[:128], rows[128:])


def key_blocks(r_ref, block, slot):
    rows = []
    for i in range(4):
        index = jnp.maximum(block + i, 0)
        rows.append(r_ref[index & 15, (index >> 4) * 2 + slot])
    return jnp.concatenate(rows, 0)


def masked(values, a, block, lo_a, lo_b, diagonal, fill):
    key_row = lax.broadcasted_iota(jnp.int32, (128, 256), 0)
    causal = key_row <= lax.broadcasted_iota(jnp.int32, (128, 256), 1) % 128
    rows = []
    for k in range(4):
        parts = []
        for i, lo in enumerate((lo_a, lo_b)):
            mask = block + k >= lo
            if diagonal and k == 2 + i:
                mask = causal
            part = values[k * 128 : k * 128 + 128, i * 256 : i * 256 + 256]
            if diagonal and k == 3 and i == 0:
                parts.append(jnp.full((128, 256), fill, jnp.float32))
            else:
                parts.append(jnp.where(mask, part, fill))
        rows.append(jnp.concatenate(parts, 1))
    return jnp.concatenate(rows, 0)


def attend_kernel(lo_ref, r_ref, o32_ref, o16_ref, lse_ref):
    def one_pair(a, _):
        lo_a, lo_b = lo_ref[2 * a], lo_ref[2 * a + 1]
        queries = stack_heads(r_ref, (2 * a, 4), (2 * a + 1, 4))

        def scores(block, diagonal):
            values = mm(key_blocks(r_ref, block, 0), queries, 1, 1)
            return masked(values, a, block, lo_a, lo_b, diagonal, masked_score)

        def add(scores, block, top):
            weights = jnp.exp(scores - top)
            sums = mm(key_blocks(r_ref, block, 1), weights.astype(jnp.bfloat16), 0, 0)
            return jnp.sum(weights, 0, keepdims=True), sums

        diagonal = scores(2 * a + 14, True)
        top = jnp.max(diagonal, 0, keepdims=True)
        total, sums = add(diagonal, 2 * a + 14, top)

        def earlier(i, carry):
            top, total, sums = carry
            block = 2 * a + 14 - 4 * i
            values = scores(block, False)
            new = jnp.maximum(top, jnp.max(values, 0, keepdims=True))
            scale = jnp.exp(top - new)
            more, more_sums = add(values, block, new)
            return new, total * scale + more, sums * scale + more_sums

        steps = (2 * a + 21 - lo_a) // 4
        top, total, sums = lax.fori_loop(1, steps, earlier, (top, total, sums))
        out = jnp.transpose(sums / total)
        for block in range(2):
            rows = unstack_heads(out, block)
            o32_ref[2 * a + block] = rows
            o16_ref[2 * a + block] = rows.astype(jnp.bfloat16)
        lse_ref[a] = top + jnp.log(total)
        return 0

    lax.fori_loop(0, 8, one_pair, 0)


def attend_call(lo, blocks):
    vmem = pl.BlockSpec(memory_space=pltpu.VMEM)
    return pl.pallas_call(
        attend_kernel,
        in_specs=[pl.BlockSpec(memory_space=pltpu.SMEM), vmem],
        out_specs=[vmem, vmem, vmem],
        out_shape=[
            jax.ShapeDtypeStruct((16, 128, 128), jnp.float32),
            jax.ShapeDtypeStruct((16, 128, 128), jnp.bfloat16),
            jax.ShapeDtypeStruct((8, 1, 512), jnp.float32),
        ],
        compiler_params=pltpu.CompilerParams(vmem_limit_bytes=VMEM_LIMIT),
        cost_estimate=TINY,
    )(lo, blocks)


def attend_back_kernel(lo_ref, r_ref, do_ref, o32_ref, lse_ref, out_ref, dk_ref, dv_ref):
    dk_ref[...] = jnp.zeros_like(dk_ref)
    dv_ref[...] = jnp.zeros_like(dv_ref)

    def one_pair(a, _):
        lo_a, lo_b = lo_ref[2 * a], lo_ref[2 * a + 1]
        queries = stack_heads(r_ref, (2 * a, 4), (2 * a + 1, 4))
        grads = stack_heads(do_ref, 2 * a, 2 * a + 1)
        out = jnp.concatenate([o32_ref[2 * a]] * 2 + [o32_ref[2 * a + 1]] * 2, 0)
        delta = jnp.sum(jnp.transpose(grads.astype(jnp.float32) * out), 0, keepdims=True)
        lse = lse_ref[a]

        def blocks_back(block, diagonal):
            keys, values = key_blocks(r_ref, block, 0), key_blocks(r_ref, block, 1)
            weights = jnp.exp(mm(keys, queries, 1, 1) - lse)
            weights = masked(weights, a, block, lo_a, lo_b, diagonal, 0.0)
            grad_scores = (weights * (mm(values, grads, 1, 1) - delta)).astype(jnp.bfloat16)
            grad_values = mm(weights.astype(jnp.bfloat16), grads)
            grad_keys = mm(grad_scores, queries)
            for k in range(4):
                index, rows = jnp.maximum(block + k, 0), slice(k * 128, k * 128 + 128)
                dv_ref[index] += grad_values[rows]
                dk_ref[index] += grad_keys[rows]
            return mm(grad_scores, keys, 0, 0)

        def earlier(i, grad_query):
            return grad_query + blocks_back(2 * a + 14 - 4 * i, False)

        steps = (2 * a + 21 - lo_a) // 4
        grad_query = blocks_back(2 * a + 14, True)
        grad_query = lax.fori_loop(1, steps, earlier, grad_query)
        for block in range(2):
            rows = unstack_heads(grad_query, block) * score_scale
            out_ref[2 * a + block, 4] = rows.astype(jnp.bfloat16)
        return 0

    lax.fori_loop(0, 8, one_pair, 0)

    def finish(c, _):
        out_ref[c, 0] = dk_ref[c].astype(jnp.bfloat16)
        out_ref[c, 1] = dv_ref[c].astype(jnp.bfloat16)
        out_ref[c, 2] = dk_ref[c + 16].astype(jnp.bfloat16)
        out_ref[c, 3] = dv_ref[c + 16].astype(jnp.bfloat16)
        return 0

    lax.fori_loop(0, 16, finish, 0)


def attend_back_call(lo, blocks, grads, out, lse):
    vmem = pl.BlockSpec(memory_space=pltpu.VMEM)
    return pl.pallas_call(
        attend_back_kernel,
        in_specs=[pl.BlockSpec(memory_space=pltpu.SMEM), vmem, vmem, vmem, vmem],
        out_specs=vmem,
        out_shape=jax.ShapeDtypeStruct((16, 5, 128, 128), jnp.bfloat16),
        scratch_shapes=[
            pltpu.VMEM((32, 128, 128), jnp.float32),
            pltpu.VMEM((32, 128, 128), jnp.float32),
        ],
        compiler_params=pltpu.CompilerParams(vmem_limit_bytes=VMEM_LIMIT),
        cost_estimate=TINY,
    )(lo, blocks, grads, out, lse)


def turn_back_kernel(r_ref, halo_ref, cos_ref, up_ref, down_ref, out_ref, bias_ref):
    for j in range(2):
        sums = [jnp.zeros((1, 128), jnp.float32) for _ in range(3)]
        for x in range(4):
            rows = slice(x * 128, (x + 1) * 128)

            def turned(grad):
                return (
                    grad * cos_ref[rows]
                    - pltpu.roll(grad, 120, 1) * up_ref[rows]
                    - pltpu.roll(grad, 8, 1) * down_ref[rows]
                )

            def read(slot):
                later = r_ref[j, 0, x + 1, slot] if x < 3 else halo_ref[j, 0, slot]
                return r_ref[j, 0, x, slot + 2].astype(jnp.float32) + later.astype(jnp.float32)

            parts = (
                turned(r_ref[j, 0, x, 4].astype(jnp.float32)),
                turned(read(0)),
                read(1),
            )
            for part in range(3):
                grad = parts[part].astype(jnp.bfloat16)
                column = (j * 3 + part) * 128
                out_ref[0, rows, column : column + 128] = grad
                sums[part] = sums[part] + jnp.sum(grad.astype(jnp.float32), 0, keepdims=True)
        for part in range(3):
            column = (j * 3 + part) * 128
            bias_ref[0, :, column : column + 128] = sums[part]


def turn_back_call(blocks, halo, tables):
    table = pl.BlockSpec((512, 128), lambda h: (0, 0))
    return pl.pallas_call(
        turn_back_kernel,
        grid=(2,),
        in_specs=[
            pl.BlockSpec((2, 1, 4, 5, 128, 128), lambda h: (0, h, 0, 0, 0, 0)),
            pl.BlockSpec((2, 1, 2, 128, 128), lambda h: (0, h, 0, 0, 0)),
            table,
            table,
            table,
        ],
        out_specs=[
            pl.BlockSpec((1, 512, 768), lambda h: (h, 0, 0)),
            pl.BlockSpec((1, 1, 768), lambda h: (h, 0, 0)),
        ],
        out_shape=[
            jax.ShapeDtypeStruct((2, 512, 768), jnp.bfloat16),
            jax.ShapeDtypeStruct((2, 1, 768), jnp.float32),
        ],
        compiler_params=pltpu.CompilerParams(vmem_limit_bytes=VMEM_LIMIT),
        cost_estimate=TINY,
    )(blocks, halo, *tables)


def normed_back_kernel(
    core_ref, g_ref, unit_ref, own0_ref, own1_ref, oth0_ref, oth1_ref, out_ref, gain_grad_ref, shift_grad_ref
):
    grads = jnp.concatenate([g_ref[0], g_ref[1]], 1)

    def rows(w0_ref, w1_ref, yl):
        return jnp.concatenate(
            [w[:, :384] for h in range(2) for w in (w0_ref[0, h, yl, :128], w1_ref[h, yl, 0])], 1
        )

    weights = jnp.concatenate(
        [ordered(core_ref, rows(own0_ref, own1_ref, yl), rows(oth0_ref, oth1_ref, yl)) for yl in range(2)], 0
    )
    total = mm(grads, weights, 1, 1)
    out_ref[...] = total.astype(jnp.bfloat16).reshape(4, 128, 512)
    unit = unit_ref[...].reshape(512, 512).astype(jnp.float32)
    gain_grad_ref[...] = jnp.sum(total * unit, 0, keepdims=True)
    shift_grad_ref[...] = jnp.sum(total, 0, keepdims=True)


def normed_back_call(core, grad_joint, unit, weights):
    first = pl.BlockSpec((1, 2, 2, 144, 512), lambda n: (n, 0, 0, 0, 0))
    second = pl.BlockSpec((2, 2, 1, 128, 512), lambda n: (0, 0, n, 0, 0))
    ring = pl.BlockSpec((4, 128, 512), lambda n: (0, 0, n))
    vector = pl.BlockSpec((1, 512), lambda n: (0, n))
    return pl.pallas_call(
        normed_back_kernel,
        grid=(4,),
        in_specs=[
            pl.BlockSpec(memory_space=pltpu.SMEM),
            pl.BlockSpec((2, 512, 768), lambda n: (0, 0, 0)),
            ring,
            first,
            second,
            first,
            second,
        ],
        out_specs=[ring, vector, vector],
        out_shape=[
            jax.ShapeDtypeStruct((4, 128, D), jnp.bfloat16),
            jax.ShapeDtypeStruct((1, D), jnp.float32),
            jax.ShapeDtypeStruct((1, D), jnp.float32),
        ],
        compiler_params=pltpu.CompilerParams(vmem_limit_bytes=VMEM_LIMIT),
        cost_estimate=TINY,
    )(core, grad_joint, unit, *weights)


def local(
    tokens,
    cotangent,
    doc_ids,
    ln1_gain,
    ln1_shift,
    w_qkv,
    b_qkv,
    w_out,
    ln2_gain,
    ln2_shift,
    w_gate,
    w_up,
    w_down,
):
    half = lax.axis_index("yh")
    blk = lax.axis_index(BLK)

    core = lax.axis_index("k").reshape(1)
    vectors = jnp.stack([ln1_gain, ln1_shift, ln2_gain, ln2_shift])
    first_pair, second_pair = pack_joint_call(w_qkv.transpose(1, 0, 2), w_out, vectors, b_qkv)
    ring = ring_gather(tokens)
    own0 = gather(gather(first_pair, Y), ("z",)).reshape(4, 2, 2, 144, 512)
    own1 = gather(gather(second_pair, ("z",)), Y).reshape(2, 2, 4, 128, 512)
    own0 = after(own0, ring)
    weights = (own0, own1, swap_core(own0), swap_core(own1))
    before = lax.ppermute(ring[3], ("yh",), [(0, 1)])
    rest = pack_hidden_call(w_gate.T, w_up.T, w_down)
    rest = after(rest, own0, own1, before)
    rest = lax.all_gather(rest, PLANE, axis=0, tiled=True).reshape(2, D, 3 * HID_PAD)

    small = jnp.stack([own0[:, :, :, 128:, :128], weights[2][:, :, :, 128:, :128]])
    small = jnp.where(core[0] == 0, small, small[::-1]).astype(jnp.float32)
    bias = small[..., 8:11, :16].transpose(2, 4, 1, 3, 0, 5).reshape(2, 3, 2, 128).reshape(2, 3, 1, 256)
    vectors = small[:, :, 0, :, :4].transpose(3, 1, 2, 0, 4).reshape(4, D)
    gain_one, shift_one, gain_two, shift_two = [vectors[i : i + 1] for i in range(4)]

    first_block = jnp.sum((doc_ids[None, :] < doc_ids[:, None]).astype(jnp.int32), axis=1)
    cycles = jnp.arange(4, dtype=jnp.int32) * 16 + half * 64 + blk
    cycles = jnp.concatenate([cycles, 48 + blk.reshape(1)])
    block_position = (cycles - first_block[cycles]) * BLK_TOK
    positions = (block_position[:, None] + jnp.arange(BLK_TOK, dtype=jnp.int32)).reshape(640)
    tables = rotary_tables(positions)
    first_query = half * 64 + (blk % 4) * 16
    lo = lax.dynamic_slice(first_block, (first_query,), (16,)) - (first_query - 16)

    payload, normed_one, unit_one = qkv_call(
        core, ring, before, gain_one, shift_one, weights, bias, tables
    )
    cot, payload = lax.optimization_barrier((cotangent, payload))
    ring_cot = gather(cot, ("x",))
    blocks = after(exchange(payload.reshape(16, 5, 128, 128), BLK), ring_cot)
    att32, att16, lse = attend_call(lo, blocks)
    attended = exchange(att16, BLK).reshape(2, 2, 4, 128, 128)
    came = exchange(project_call(core, attended, weights), ("x",))
    token_shape = jax.ShapeDtypeStruct((128, D), jnp.float32)
    ring_shape = jax.ShapeDtypeStruct((4, 128, D), jnp.bfloat16)
    vector_shape = jax.ShapeDtypeStruct((1, D), jnp.float32)
    middle, normed_two = whole_call(
        middle_kernel, [token_shape, ring_shape], came, tokens, gain_two, shift_two
    )

    ring_two = exchange(normed_two, ("x",))
    active, grad_gu, ring_grad, ring_out = feed_forward_call(ring_two, ring_cot, rest)
    shared = plane_grad_call(core, with_other(ring_cot), with_other(active), HID_PAD, 2 * HID_PAD)
    came = after(exchange(ring_grad, ("x",)), shared)
    grad_middle, ring_branch, grad_gain_two, grad_shift_two = whole_call(
        middle_back_kernel,
        [token_shape, ring_shape, vector_shape, vector_shape],
        came,
        middle,
        cotangent,
        gain_two,
    )
    shared = plane_grad_call(core, with_other(ring_two), with_other(grad_gu), 2 * HID_PAD, 0, shared)
    ring_branch = after(exchange(ring_branch, ("x",)), shared)
    grad_att = project_back_call(core, ring_branch, weights).reshape(16, 128, 128)
    attended_pair = with_other(attended.transpose(1, 2, 3, 0, 4).reshape(2, 512, 256))
    shared = plane_sum(after(shared, ring_branch))
    branch_pair = with_other(after(ring_branch, grad_att))
    grad_att = exchange(grad_att, BLK)

    mixed_came = exchange(after(ring_out, grad_att), ("x",))
    back = attend_back_call(lo, blocks, grad_att, att32, lse)
    mixed = whole_call(
        mixed_kernel, jax.ShapeDtypeStruct((128, D), jnp.bfloat16), after(mixed_came, back), middle
    )
    places = (chip_places(True), chip_places(False))
    out_parts = weight_grad_call(core, places[1], after(branch_pair, back), attended_pair, 256)
    out_came = first_send(out_parts, False)
    back = exchange(back, BLK).reshape(2, 2, 4, 5, 128, 128)
    back = after(back, mixed)
    out_came = second_send(first_sum(after(out_came, back), False), False)
    halo_back = lax.ppermute(back[:, :, 0, :2], ("yh",), [(1, 0)])
    grad_joint, grad_bias = turn_back_call(back, halo_back, tables)
    ring_one, grad_gain_one, grad_shift_one = normed_back_call(core, grad_joint, unit_one, weights)
    joint_left, joint_right = after((with_other(normed_one), with_other(grad_joint)), out_came[0])
    parts = joint_grad_call(core, places, joint_left, joint_right)
    pair_came = [first_send(parts[4 * j : 4 * j + 4], j == 0) for j in range(2)]
    pair_came = [second_send(first_sum(part, j == 0), j == 0) for j, part in enumerate(pair_came)]
    came = after(exchange(ring_one, ("x",)), pair_came[0][0], pair_came[1][0])
    input_grad = whole_call(input_back_kernel, token_shape, came, tokens, grad_middle, gain_one)

    def shape(*dims):
        return jax.ShapeDtypeStruct(dims, jnp.float32)

    grad_gate, grad_up, grad_down = whole_call(
        shared_end_kernel, [shape(HID, 128)] * 3, after(shared, input_grad)
    )
    grad_out = whole_call(out_end_kernel, shape(256, 128), *after(out_came, input_grad))
    grad_qkv = whole_call(joint_end_kernel, shape(3, 128, 256), *pair_came[0], *pair_came[1])

    norms = jnp.concatenate([grad_gain_one, grad_shift_one, grad_gain_two, grad_shift_two], 0)
    norms = norms.reshape(4, 2, 4, 16, 16).transpose(1, 2, 3, 0, 4).reshape(2, 4, 16, 64)
    biases = grad_bias.reshape(2, 2, 3, 8, 16).transpose(0, 1, 3, 2, 4).reshape(2, 1, 16, 48)
    plane = jnp.arange(4).reshape(1, 4, 1, 1) == lax.axis_index("x")
    biases = jnp.where(plane, biases, 0.0)
    sums = jnp.concatenate([norms, biases, jnp.zeros((2, 4, 16, 16), jnp.float32)], 3)
    sums = jnp.sum(exchange(after(sums.reshape(128, 128), came), AXES), 0)
    norms = sums[:64].reshape(4, 16)

    return (
        mixed,
        input_grad,
        norms[0],
        norms[1],
        grad_qkv.transpose(1, 0, 2),
        sums[64:112].reshape(3, 16),
        grad_out,
        norms[2],
        norms[3],
        grad_gate.T,
        grad_up.T,
        grad_down,
    )


def solution(mesh):
    whole = Mesh(mesh.devices.reshape(2, 4, 4, 2, 2), AXES)
    ulysses, blk = ("yh", "x"), BLK
    both = ulysses + blk
    placed = (
        P(both, None),
        P(both, None),
        P(),
        P(blk),
        P(blk),
        P(blk, None, ulysses),
        P(None, both),
        P(ulysses, blk),
        P(blk),
        P(blk),
        P(blk, ulysses),
        P(blk, ulysses),
        P(ulysses, blk),
    )
    return jax.shard_map(
        local,
        mesh=whole,
        in_specs=placed,
        out_specs=(
            P(both, None),
            P(both, None),
            P(both),
            P(both),
            P(blk, None, ulysses),
            P(None, both),
            P(ulysses, blk),
            P(both),
            P(both),
            P(blk, ulysses),
            P(blk, ulysses),
            P(ulysses, blk),
        ),
        check_vma=False,
    )
```

```python
import functools

import jax
import jax.numpy as jnp
from jax import lax
from jax.experimental import pallas as pl
from jax.experimental.pallas import tpu as pltpu
from jax.sharding import Mesh
from jax.sharding import PartitionSpec as P

D = 2048
HEADS = 32
HEAD_DIM = 64
ROT = 16
BLK_TOK = 128
HID = 704
HID_PAD = 768
SHARED = 3 * HID_PAD + 256

eps = 1e-05
rope_base = 10000.0
masked_score = -1e30
score_scale = HEAD_DIM ** (-0.5)

AXES = ("yh", "x", "z", "yl", "k")
PLANE = ("yh", "z", "yl", "k")
BLK = ("z", "yl", "k")
Y = ("yh", "yl")

VMEM_LIMIT = 60 * 1024 * 1024
TINY = pl.CostEstimate(flops=1, bytes_accessed=1, transcendentals=0)


def mm(a, b, ca=1, cb=0):
    return lax.dot_general(a, b, (((ca,), (cb,)), ((), ())), preferred_element_type=jnp.float32)


def swap_core(value):
    return lax.ppermute(value, ("k",), [(0, 1), (1, 0)])


def exchange(parts, axes):
    return lax.all_to_all(parts, axes, 0, 0, tiled=True)


def send(value, axes, step):
    return lax.ppermute(value, axes, [(i, (i + step) % 4) for i in range(4)])


def gather(value, axes, *others):
    me = lax.axis_index(axes)
    pieces = [send(value, axes, step) for step in (1, 3, 2)]
    if others:
        pieces = after(pieces, *others)
    buffer = jnp.zeros((4,) + value.shape, value.dtype)
    for step, piece in zip((0, 1, 3, 2), [value] + pieces):
        buffer = lax.dynamic_update_index_in_dim(buffer, piece, (me - step) % 4, 0)
    return buffer


def ring_gather(value):
    return exchange(jnp.broadcast_to(value, (4,) + value.shape), ("x",))


def send(value, axes, step):
    return lax.ppermute(value, axes, [(i, (i + step) % 4) for i in range(4)])


def gather(value, axes, *others):
    me = lax.axis_index(axes)
    pieces = [send(value, axes, step) for step in (1, 3, 2)]
    if others:
        pieces = after(pieces, *others)
    buffer = jnp.zeros((4,) + value.shape, value.dtype)
    for step, piece in zip((0, 1, 3, 2), [value] + pieces):
        buffer = lax.dynamic_update_index_in_dim(buffer, piece, (me - step) % 4, 0)
    return buffer


def ring_gather(value):
    return exchange(jnp.broadcast_to(value, (4,) + value.shape), ("x",))


def after(value, *others):
    return lax.optimization_barrier((value,) + others)[0]


def rotary_tables(positions):
    halfway = ROT // 2
    counter = jnp.arange(halfway, dtype=jnp.float32)
    frequency = rope_base ** (-2.0 * counter / ROT)
    lane = jnp.arange(128) % HEAD_DIM
    frequency = jnp.where(lane < ROT, jnp.tile(frequency, 16), 0.0)
    angles = positions.astype(jnp.float32)[:, None] * frequency[None, :]
    sine = jnp.sin(angles)
    return (
        jnp.cos(angles),
        jnp.where(lane < halfway, -sine, 0.0),
        jnp.where((lane >= halfway) & (lane < ROT), sine, 0.0),
    )


def pack_joint_kernel(qkv_ref, out_ref, vectors_ref, bias_ref, h0_ref, h1_ref, small_ref):
    out_t = jnp.transpose(out_ref[...])
    for j, h_ref in enumerate((h0_ref, h1_ref)):
        for part in range(3):
            h_ref[:128, part * 128 : (part + 1) * 128] = qkv_ref[part, :, j * 128 : (j + 1) * 128]
        h_ref[:128, 384:] = out_t[:, j * 128 : (j + 1) * 128]
    small_ref[...] = jnp.zeros_like(small_ref)
    small_ref[0:4, :128] = vectors_ref[...].astype(jnp.float32)
    small_ref[8:11, :16] = bias_ref[...].astype(jnp.float32)
    h0_ref[128:, :] = small_ref[...].astype(jnp.bfloat16)


def pack_joint_call(qkv, out, vectors, bias):
    vmem = pl.BlockSpec(memory_space=pltpu.VMEM)
    return pl.pallas_call(
        pack_joint_kernel,
        in_specs=[vmem] * 4,
        out_specs=[vmem] * 2,
        out_shape=[
            jax.ShapeDtypeStruct((144, 512), jnp.bfloat16),
            jax.ShapeDtypeStruct((128, 512), jnp.bfloat16),
        ],
        scratch_shapes=[pltpu.VMEM((16, 512), jnp.float32)],
    )(qkv, out, vectors, bias)


def pack_hidden_kernel(gate_ref, up_ref, down_ref, rest_ref):
    for i, ref in enumerate((gate_ref, up_ref, down_ref)):
        first = i * HID_PAD
        rest_ref[:, first + HID_PAD - 128 : first + HID_PAD] = jnp.zeros((128, 128), jnp.bfloat16)
        rest_ref[:, first : first + HID] = jnp.transpose(ref[...])


def pack_hidden_call(gate, up, down):
    return whole_call(
        pack_hidden_kernel, jax.ShapeDtypeStruct((128, 3 * HID_PAD), jnp.bfloat16), gate, up, down
    )


def core_columns(ref, core, blocks):
    columns = [ref[:blocks, :, pl.ds(pl.multiple_of((2 * i + core) * 128, 128), 128)] for i in range(8)]
    return jnp.concatenate(columns, 2).reshape(blocks * 128, 1024)


def core_rows(w0_ref, w1_ref):
    w0 = jnp.concatenate([w0_ref[z, 0, yl, :128] for z in range(4) for yl in range(2)], 0)
    w1 = jnp.concatenate([w1_ref[0, yl, z] for z in range(4) for yl in range(2)], 0)
    return jnp.concatenate([w0, w1], 1)


def normalise(values):
    centred = values - jnp.mean(values, -1, keepdims=True)
    inverse = lax.rsqrt(jnp.mean(centred * centred, -1, keepdims=True) + eps)
    return centred * inverse, inverse


def qkv_kernel(
    core_ref,
    x_ref,
    before_ref,
    gain_ref,
    shift_ref,
    own0_ref,
    own1_ref,
    oth0_ref,
    oth1_ref,
    bias_ref,
    cos_ref,
    up_ref,
    down_ref,
    out_ref,
    normed_ref,
    unit_ref,
    x_cores,
):
    part = pl.program_id(1)
    core = core_ref[0]

    @pl.when((pl.program_id(0) == 0) & (part == 0))
    def _():
        for b in range(5):
            block = x_ref[b] if b < 4 else before_ref[...]
            unit, _ = normalise(block.astype(jnp.float32))
            normed = (unit * gain_ref[...] + shift_ref[...]).astype(jnp.bfloat16)
            if b < 4:
                normed_ref[b] = normed
                unit_ref[b] = unit.astype(jnp.bfloat16)
            for c in range(16):
                column = pl.multiple_of((c // 2 + 8 * ((c + core) % 2)) * 128, 128)
                x_cores[b * 128 : (b + 1) * 128, pl.ds(column, 128)] = normed[:, c * 128 : (c + 1) * 128]

    def joint(rows):
        weights = jnp.concatenate([core_rows(own0_ref, own1_ref), core_rows(oth0_ref, oth1_ref)], 0)
        return mm(x_cores[:rows], weights) + bias_ref[0, 0]

    def turned(value):
        rows = value.shape[0]
        return (
            value * cos_ref[:rows]
            + pltpu.roll(value, 120, 1) * up_ref[:rows]
            + pltpu.roll(value, 8, 1) * down_ref[:rows]
        )

    @pl.when(part == 0)
    def _():
        value = joint(512)
        for j in range(2):
            query = turned(value[:, j * 128 : (j + 1) * 128]) * score_scale
            out_ref[:, j, 0, 4] = query.astype(jnp.bfloat16).reshape(4, 128, 128)

    @pl.when(part > 0)
    def _():
        value = joint(640)
        for j in range(2):
            block = value[:, j * 128 : (j + 1) * 128]
            block = jnp.where(part == 1, turned(block), block)
            block = block.astype(jnp.bfloat16).reshape(5, 128, 128)

            @pl.when(part == 1)
            def _():
                out_ref[:, j, 0, 2] = block[:4]
                out_ref[1:, j, 0, 0] = block[:3]
                out_ref[0, j, 0, 0] = block[4]

            @pl.when(part == 2)
            def _():
                out_ref[:, j, 0, 3] = block[:4]
                out_ref[1:, j, 0, 1] = block[:3]
                out_ref[0, j, 0, 1] = block[4]


def qkv_call(core, tokens, before, gain, shift, weights, bias, tables):
    table = pl.BlockSpec((640, 128), lambda h, p: (0, 0))
    vector = pl.BlockSpec((1, D), lambda h, p: (0, 0))
    first = pl.BlockSpec((4, 1, 2, 144, 128), lambda h, p: (0, h, 0, 0, p))
    second = pl.BlockSpec((1, 2, 4, 128, 128), lambda h, p: (h, 0, 0, 0, p))
    return pl.pallas_call(
        qkv_kernel,
        grid=(2, 3),
        in_specs=[
            pl.BlockSpec(memory_space=pltpu.SMEM),
            pl.BlockSpec((4, 128, D), lambda h, p: (0, 0, 0)),
            pl.BlockSpec((128, D), lambda h, p: (0, 0)),
            vector,
            vector,
            first,
            second,
            first,
            second,
            pl.BlockSpec((1, 1, 1, 256), lambda h, p: (h, p, 0, 0)),
            table,
            table,
            table,
        ],
        out_specs=[
            pl.BlockSpec((4, 2, 1, 5, 128, 128), lambda h, p: (0, 0, h, 0, 0, 0)),
            pl.BlockSpec((4, 128, D), lambda h, p: (0, 0, 0)),
            pl.BlockSpec((4, 128, D), lambda h, p: (0, 0, 0)),
        ],
        out_shape=[
            jax.ShapeDtypeStruct((4, 2, 2, 5, 128, 128), jnp.bfloat16),
            jax.ShapeDtypeStruct((4, 128, D), jnp.bfloat16),
            jax.ShapeDtypeStruct((4, 128, D), jnp.bfloat16),
        ],
        scratch_shapes=[pltpu.VMEM((640, D), jnp.bfloat16)],
        compiler_params=pltpu.CompilerParams(vmem_limit_bytes=VMEM_LIMIT),
        cost_estimate=TINY,
    )(core, tokens, before, gain, shift, *weights, bias, *tables)


def whole_call(kernel, out_shape, *operands, scratch=()):
    vmem = pl.BlockSpec(memory_space=pltpu.VMEM)
    return pl.pallas_call(
        kernel,
        in_specs=[vmem] * len(operands),
        out_specs=jax.tree.map(lambda _: vmem, out_shape),
        out_shape=out_shape,
        scratch_shapes=list(scratch),
        compiler_params=pltpu.CompilerParams(vmem_limit_bytes=VMEM_LIMIT),
        cost_estimate=TINY,
    )(*operands)


def back_through(came_ref, values, gain):
    grad = came_ref[0].astype(jnp.float32)
    for i in range(1, 4):
        grad = grad + came_ref[i].astype(jnp.float32)
    unit, inverse = normalise(values)
    grad_unit = grad * gain
    centred_grad = (
        grad_unit
        - jnp.mean(grad_unit, -1, keepdims=True)
        - unit * jnp.mean(grad_unit * unit, -1, keepdims=True)
    )
    gain_grad = jnp.sum(grad * unit, 0, keepdims=True)
    return inverse * centred_grad, gain_grad, jnp.sum(grad, 0, keepdims=True)


def input_back_kernel(came_ref, tokens_ref, grad_ref, gain_ref, out_ref):
    values = tokens_ref[...].astype(jnp.float32)
    out_ref[...] = grad_ref[...] + back_through(came_ref, values, gain_ref[...])[0]


def shared_end_kernel(total_ref, gate_ref, up_ref, down_ref, out_ref):
    total = jnp.transpose(total_ref[...].astype(jnp.float32))
    for c in range(3):
        width = min(HID, c * 256 + 256) - c * 256
        gate_ref[c * 256 : c * 256 + width] = total[c * 512 : c * 512 + width]
        up_ref[c * 256 : c * 256 + width] = total[c * 512 + 256 : c * 512 + 256 + width]
    down_ref[...] = total[2 * HID_PAD : 2 * HID_PAD + HID]
    out_ref[...] = total[3 * HID_PAD :]


def joint_end_kernel(*refs):
    for j in range(2):
        total = sum(ref[...].astype(jnp.float32) for ref in refs[4 * j : 4 * j + 4])
        for part in range(3):
            refs[8][part, :, j * 128 : (j + 1) * 128] = total[:, part * 128 : part * 128 + 128]


def ordered(core_ref, own, other):
    first = core_ref[0] == 0
    return jnp.concatenate([jnp.where(first, own, other), jnp.where(first, other, own)], 0)


def out_rows_kernel(own0_ref, own1_ref, out_ref):
    for yl in range(2):
        for h in range(2):
            out_ref[yl, :, h * 256 : h * 256 + 128] = own0_ref[0, h, yl, :128]
            out_ref[yl, :, h * 256 + 128 : h * 256 + 256] = own1_ref[h, yl, 0]


def out_rows_call(own0, own1):
    return pl.pallas_call(
        out_rows_kernel,
        grid=(4,),
        in_specs=[
            pl.BlockSpec((1, 2, 2, 144, 128), lambda n: (n, 0, 0, 0, 3)),
            pl.BlockSpec((2, 2, 1, 128, 128), lambda n: (0, 0, n, 0, 3)),
        ],
        out_specs=pl.BlockSpec((2, 128, 512), lambda n: (n, 0, 0)),
        out_shape=jax.ShapeDtypeStruct((8, 128, 512), jnp.bfloat16),
        compiler_params=pltpu.CompilerParams(vmem_limit_bytes=VMEM_LIMIT),
        cost_estimate=TINY,
    )(own0, own1)


def planes_columns(refs, yl):
    return jnp.concatenate([ref[yl] for ref in refs], 1)


def project_kernel(place_ref, att_ref, tokens_ref, gain_ref, shift_ref, *refs):
    own_refs, other_refs, (middle_ref, normed_ref, att_cols, total) = refs[:4], refs[4:8], refs[8:]
    n, me, core = pl.program_id(0), place_ref[0], place_ref[1]

    @pl.when(n == 0)
    def _():
        for t in range(4):
            x = (me + 4 - t) % 4
            for h in range(2):
                for j in range(2):
                    column = t * 512 + h * 256 + j * 128
                    att_cols[:, column : column + 128] = att_ref[x, j, h]

    weights = jnp.concatenate(
        [planes_columns(refs, yl) for refs in (own_refs, other_refs) for yl in range(2)], 0
    )
    values = mm(att_cols[...], weights, 1, 1)
    for i in range(4):
        holder = core if i < 2 else 1 - core
        column = pl.multiple_of((n * 4 + i % 2 * 2 + holder) * 128, 128)
        total[:, pl.ds(column, 128)] = values[:, i * 128 : i * 128 + 128]

    @pl.when(n == 3)
    def _():
        middle = tokens_ref[...].astype(jnp.float32) + total[...]
        middle_ref[...] = middle
        normed = (normalise(middle)[0] * gain_ref[...] + shift_ref[...]).astype(jnp.bfloat16)
        for i in range(4):
            normed_ref[i] = normed


def project_call(place, att, tokens, gain, shift, own, other):
    def whole(*dims):
        return pl.BlockSpec(dims, lambda n: (0,) * len(dims))

    rows = pl.BlockSpec((2, 128, 512), lambda n: (n, 0, 0))
    return pl.pallas_call(
        project_kernel,
        grid=(4,),
        in_specs=[
            pl.BlockSpec(memory_space=pltpu.SMEM),
            whole(4, 2, 2, 128, 128),
            whole(128, D),
            whole(1, D),
            whole(1, D),
        ]
        + [rows] * 8,
        out_specs=[whole(128, D), whole(4, 128, D)],
        out_shape=[
            jax.ShapeDtypeStruct((128, D), jnp.float32),
            jax.ShapeDtypeStruct((4, 128, D), jnp.bfloat16),
        ],
        scratch_shapes=[pltpu.VMEM((128, D), jnp.bfloat16), pltpu.VMEM((128, D), jnp.float32)],
        compiler_params=pltpu.CompilerParams(vmem_limit_bytes=VMEM_LIMIT),
        cost_estimate=TINY,
    )(place, att, tokens, gain, shift, *own, *other)


def project_back_kernel(place_ref, came_ref, middle_ref, cot_ref, gain_ref, *refs):
    own_refs, other_refs = refs[:4], refs[4:8]
    grad_ref, low_ref, gain_grad_ref, shift_grad_ref, out_ref, low, total = refs[8:]
    n, me, core = pl.program_id(0), place_ref[0], place_ref[1]

    @pl.when(n == 0)
    def _():
        grad, gain_grad_ref[...], shift_grad_ref[...] = back_through(came_ref, middle_ref[...], gain_ref[...])
        grad = grad + cot_ref[...].astype(jnp.float32)
        grad_ref[...] = grad
        low[...] = grad.astype(jnp.bfloat16)
        low_ref[...] = low[...]
        total[...] = jnp.zeros_like(total)

    columns = []
    for i in range(4):
        holder = core if i < 2 else 1 - core
        column = pl.multiple_of((n * 4 + i % 2 * 2 + holder) * 128, 128)
        columns.append(low[:, pl.ds(column, 128)])
    weights = jnp.concatenate(
        [planes_columns(refs, yl) for refs in (own_refs, other_refs) for yl in range(2)], 0
    )
    total[...] += mm(jnp.concatenate(columns, 1), weights)

    @pl.when(n == 3)
    def _():
        for t in range(4):
            x = (me + 4 - t) % 4
            for h in range(2):
                for j in range(2):
                    column = t * 512 + h * 256 + j * 128
                    out_ref[x, j, h] = total[:, column : column + 128].astype(jnp.bfloat16)


def project_back_call(place, came, middle, cot, gain, own, other):
    def whole(*dims):
        return pl.BlockSpec(dims, lambda n: (0,) * len(dims))

    rows = pl.BlockSpec((2, 128, 512), lambda n: (n, 0, 0))
    return pl.pallas_call(
        project_back_kernel,
        grid=(4,),
        in_specs=[
            pl.BlockSpec(memory_space=pltpu.SMEM),
            whole(4, 128, D),
            whole(128, D),
            whole(128, D),
            whole(1, D),
        ]
        + [rows] * 8,
        out_specs=[whole(128, D), whole(128, D), whole(1, D), whole(1, D), whole(4, 2, 2, 128, 128)],
        out_shape=[
            jax.ShapeDtypeStruct((128, D), jnp.float32),
            jax.ShapeDtypeStruct((128, D), jnp.bfloat16),
            jax.ShapeDtypeStruct((1, D), jnp.float32),
            jax.ShapeDtypeStruct((1, D), jnp.float32),
            jax.ShapeDtypeStruct((4, 2, 2, 128, 128), jnp.bfloat16),
        ],
        scratch_shapes=[pltpu.VMEM((128, D), jnp.bfloat16), pltpu.VMEM((128, D), jnp.float32)],
        compiler_params=pltpu.CompilerParams(vmem_limit_bytes=VMEM_LIMIT),
        cost_estimate=TINY,
    )(place, came, middle, cot, gain, *own, *other)


def feed_forward_kernel(
    x_ref, cot_ref, gate_ref, up_ref, down_ref, active_ref, grads_ref, back_ref, out_ref, back_sum, out_sum
):
    step = pl.program_id(0) * 3 + pl.program_id(1)
    x = x_ref[...].reshape(512, D)
    gate = mm(x, gate_ref[0])
    up = mm(x, up_ref[0])
    grad_active = mm(cot_ref[...].reshape(512, D), down_ref[0])
    sigmoid = jax.nn.sigmoid(gate)
    silu = gate * sigmoid
    active = (silu * up).astype(jnp.bfloat16)
    grad_gate = (grad_active * up * (sigmoid + silu * (1.0 - sigmoid))).astype(jnp.bfloat16)
    grad_up = (grad_active * silu).astype(jnp.bfloat16)
    grads = jnp.concatenate([grad_gate, grad_up], 1)
    active_ref[0] = active
    grads_ref[0] = grads
    back = mm(grads, jnp.concatenate([gate_ref[0], up_ref[0]], 1), 1, 1)
    out = mm(active, down_ref[0], 1, 1)

    @pl.when(step == 0)
    def _():
        back_sum[...] = back
        out_sum[...] = out

    @pl.when((step > 0) & (step < 5))
    def _():
        back_sum[...] += back
        out_sum[...] += out

    @pl.when(step == 5)
    def _():
        back_ref[...] = (back_sum[...] + back).astype(jnp.bfloat16).reshape(4, 128, D)
        out_ref[...] = (out_sum[...] + out).astype(jnp.bfloat16).reshape(4, 128, D)


def feed_forward_call(x, ring, rest):
    tokens = pl.BlockSpec((4, 128, D), lambda h, c: (0, 0, 0))
    weight = [pl.BlockSpec((1, D, 256), lambda h, c, first=first: (h, 0, first + c)) for first in (0, 3, 6)]
    ring_shape = jax.ShapeDtypeStruct((4, 128, D), jnp.bfloat16)
    return pl.pallas_call(
        feed_forward_kernel,
        grid=(2, 3),
        in_specs=[tokens, tokens] + weight,
        out_specs=[
            pl.BlockSpec((1, 512, 256), lambda h, c: (h, 0, c)),
            pl.BlockSpec((1, 512, 512), lambda h, c: (h, 0, c)),
            tokens,
            tokens,
        ],
        out_shape=[
            jax.ShapeDtypeStruct((2, 512, HID_PAD), jnp.bfloat16),
            jax.ShapeDtypeStruct((2, 512, 2 * HID_PAD), jnp.bfloat16),
            ring_shape,
            ring_shape,
        ],
        scratch_shapes=[pltpu.VMEM((512, D), jnp.float32), pltpu.VMEM((512, D), jnp.float32)],
        compiler_params=pltpu.CompilerParams(vmem_limit_bytes=VMEM_LIMIT),
        cost_estimate=TINY,
    )(x, ring, rest, rest, rest)


def plane_grad_kernel(core_ref, left_ref, left_other_ref, right_ref, right_other_ref, *refs):
    out_ref, left_t = refs[-2:]

    @pl.when((pl.program_id(0) == 0) & (pl.program_id(1) == 0))
    def _():
        left_t[:, :512] = jnp.transpose(core_columns(left_ref, core_ref[0], 4))
        left_t[:, 512:] = jnp.transpose(core_columns(left_other_ref, core_ref[0], 4))

    total = mm(left_t[...], jnp.concatenate([right_ref[0], right_other_ref[0]], 0)).astype(jnp.bfloat16)
    for z in range(4):
        for yl in range(2):
            row = (z * 2 + yl) * 128
            out_ref[0, yl, z] = total[row : row + 128]


def plane_grad_call(core, left, right, columns, first, shared=None):
    left_block = pl.BlockSpec((4, 128, D), lambda n, h: (0, 0, 0))
    right_block = pl.BlockSpec((1, 512, 256), lambda n, h: (h, 0, n))
    extra = [] if shared is None else [shared]
    return pl.pallas_call(
        plane_grad_kernel,
        grid=(columns // 256, 2),
        in_specs=[
            pl.BlockSpec(memory_space=pltpu.SMEM),
            left_block,
            left_block,
            right_block,
            right_block,
        ]
        + [pl.BlockSpec(memory_space=pl.ANY)] * len(extra),
        out_specs=pl.BlockSpec((1, 2, 4, 128, 256), lambda n, h: (h, 0, 0, 0, first // 256 + n)),
        out_shape=jax.ShapeDtypeStruct((2, 2, 4, 128, SHARED), jnp.bfloat16),
        input_output_aliases={5: 0} if extra else {},
        scratch_shapes=[pltpu.VMEM((1024, 1024), jnp.bfloat16)],
        compiler_params=pltpu.CompilerParams(vmem_limit_bytes=VMEM_LIMIT),
        cost_estimate=TINY,
    )(core, *left, *right, *extra)


def weight_grad_kernel(core_ref, place_ref, left_ref, left_other_ref, right_ref, right_other_ref, *refs):
    outs, left_t = refs[:4], refs[4]
    h = pl.program_id(1)

    @pl.when((h == 0) & (pl.program_id(0) == 0))
    def _():
        left_t[:, :512] = jnp.transpose(core_columns(left_ref, core_ref[0], 4))
        left_t[:, 512:] = jnp.transpose(core_columns(left_other_ref, core_ref[0], 4))

    total = mm(left_t[...], jnp.concatenate([right_ref[0], right_other_ref[0]], 0)).astype(jnp.bfloat16)
    for z in range(4):
        for yl in range(2):
            row = (z * 2 + yl) * 128
            chip = (h * 2 + yl) * 4 + z
            step, slot = place_ref[0, chip], place_ref[1, chip]
            for t in range(4):

                @pl.when(step == t)
                def _():
                    outs[t][slot] = total[row : row + 128]


def weight_grad_call(core, place, left, right, columns):
    smem = pl.BlockSpec(memory_space=pltpu.SMEM)
    left_block = pl.BlockSpec((4, 128, D), lambda n, h: (0, 0, 0))
    right_block = pl.BlockSpec((1, 512, 256), lambda n, h: (h, 0, n))
    return pl.pallas_call(
        weight_grad_kernel,
        grid=(columns // 256, 2),
        in_specs=[smem, smem, left_block, left_block, right_block, right_block],
        out_specs=[pl.BlockSpec((4, 128, 256), lambda n, h: (0, 0, n))] * 4,
        out_shape=[jax.ShapeDtypeStruct((4, 128, columns), jnp.bfloat16)] * 4,
        scratch_shapes=[pltpu.VMEM((1024, 1024), jnp.bfloat16)],
        compiler_params=pltpu.CompilerParams(vmem_limit_bytes=VMEM_LIMIT),
        cost_estimate=TINY,
    )(core, place, *left, *right)


def joint_grad_kernel(core_ref, place_ref, left_ref, left_other_ref, right_ref, right_other_ref, *refs):
    outs, left_t = refs[:8], refs[8]
    h = pl.program_id(0)

    @pl.when(h == 0)
    def _():
        left_t[:, :512] = jnp.transpose(core_columns(left_ref, core_ref[0], 4))
        left_t[:, 512:] = jnp.transpose(core_columns(left_other_ref, core_ref[0], 4))

    right = jnp.concatenate([right_ref[0], right_other_ref[0]], 0)
    total = mm(left_t[...], right).astype(jnp.bfloat16)
    for z in range(4):
        for yl in range(2):
            row = (z * 2 + yl) * 128
            chip = (h * 2 + yl) * 4 + z
            for j in range(2):
                step, slot = place_ref[2 * j, chip], place_ref[2 * j + 1, chip]
                for t in range(4):

                    @pl.when(step == t)
                    def _():
                        outs[4 * j + t][slot] = total[row : row + 128, j * 384 : j * 384 + 384]


def joint_grad_call(core, places, left, right):
    smem = pl.BlockSpec(memory_space=pltpu.SMEM)
    left_block = pl.BlockSpec((4, 128, D), lambda h: (0, 0, 0))
    right_block = pl.BlockSpec((1, 512, 768), lambda h: (h, 0, 0))
    return pl.pallas_call(
        joint_grad_kernel,
        grid=(2,),
        in_specs=[smem, smem, left_block, left_block, right_block, right_block],
        out_specs=[pl.BlockSpec((4, 128, 384), lambda h: (0, 0, 0))] * 8,
        out_shape=[jax.ShapeDtypeStruct((4, 128, 384), jnp.bfloat16)] * 8,
        scratch_shapes=[pltpu.VMEM((1024, 1024), jnp.bfloat16)],
        compiler_params=pltpu.CompilerParams(vmem_limit_bytes=VMEM_LIMIT),
        cost_estimate=TINY,
    )(core, jnp.concatenate(places, 0), *left, *right)


def split_sum_kernel(place_ref, a_ref, b_ref, c_ref, d_ref, *out_refs):
    for t in range(4):
        i = (place_ref[0] + t) % 4
        total = sum(ref[i].astype(jnp.float32) for ref in (a_ref, b_ref, c_ref, d_ref))
        out_refs[t][...] = total.astype(jnp.bfloat16)


def split_sum_call(place, parts):
    columns = parts[0].shape[2]
    width = 256 if columns % 256 == 0 else 384
    return pl.pallas_call(
        split_sum_kernel,
        grid=(columns // width,),
        in_specs=[pl.BlockSpec(memory_space=pltpu.SMEM)]
        + [pl.BlockSpec((4, 128, width), lambda n: (0, 0, n))] * 4,
        out_specs=[pl.BlockSpec((128, width), lambda n: (0, n))] * 4,
        out_shape=[jax.ShapeDtypeStruct((128, columns), jnp.bfloat16)] * 4,
        compiler_params=pltpu.CompilerParams(vmem_limit_bytes=VMEM_LIMIT),
        cost_estimate=TINY,
    )(place, *parts)


def chip_places(y_first):
    y, z = jnp.arange(16, dtype=jnp.int32) // 4, jnp.arange(16, dtype=jnp.int32) % 4
    if y_first:
        return jnp.stack([(y - lax.axis_index(Y)) % 4, z])
    return jnp.stack([(z - lax.axis_index("z")) % 4, y])


def plane_sum(parts):
    parts = parts.reshape(2048, parts.shape[-1])
    return lax.psum_scatter(parts, ("yh", "yl", "z"), scatter_dimension=0, tiled=True)


def with_other(value):
    return value, swap_core(value)


def first_send(parts, y_first):
    axes = Y if y_first else ("z",)
    return [parts[0]] + [send(parts[t], axes, t) for t in (1, 3, 2)]


def first_sum(parts, y_first):
    return split_sum_call(lax.axis_index(("z",) if y_first else Y).reshape(1), parts)


def second_send(parts, y_first):
    axes = ("z",) if y_first else Y
    return [parts[0]] + [send(parts[t], axes, t) for t in (1, 3, 2)]


def stack_heads(ref, *index):
    first = (lax.broadcasted_iota(jnp.int32, (128, 128), 1) < HEAD_DIM).astype(jnp.float32).astype(jnp.bfloat16)
    masks = (first, 1 - first)
    return jnp.concatenate([ref[i] * mask for i in index for mask in masks], 0)


def unstack_heads(values, block):
    low = lax.broadcasted_iota(jnp.int32, (128, 128), 1) < HEAD_DIM
    rows = values[block * 256 : block * 256 + 256]
    return jnp.where(low, rows[:128], rows[128:])


def key_blocks(r_ref, block, slot):
    rows = []
    for i in range(4):
        index = jnp.maximum(block + i, 0)
        rows.append(r_ref[index & 15, (index >> 4) * 2 + slot])
    return jnp.concatenate(rows, 0)


def masked(values, a, block, lo_a, lo_b, diagonal, fill):
    key_row = lax.broadcasted_iota(jnp.int32, (128, 256), 0)
    causal = key_row <= lax.broadcasted_iota(jnp.int32, (128, 256), 1) % 128
    rows = []
    for k in range(4):
        parts = []
        for i, lo in enumerate((lo_a, lo_b)):
            mask = block + k >= lo
            if diagonal and k == 2 + i:
                mask = causal
            part = values[k * 128 : k * 128 + 128, i * 256 : i * 256 + 256]
            if diagonal and k == 3 and i == 0:
                parts.append(jnp.full((128, 256), fill, jnp.float32))
            else:
                parts.append(jnp.where(mask, part, fill))
        rows.append(jnp.concatenate(parts, 1))
    return jnp.concatenate(rows, 0)


def attend_kernel(lo_ref, r_ref, o32_ref, o16_ref, lse_ref):
    def one_pair(a, _):
        lo_a, lo_b = lo_ref[2 * a], lo_ref[2 * a + 1]
        queries = stack_heads(r_ref, (2 * a, 4), (2 * a + 1, 4))

        def scores(block, diagonal):
            values = mm(key_blocks(r_ref, block, 0), queries, 1, 1)
            return masked(values, a, block, lo_a, lo_b, diagonal, masked_score)

        def add(scores, block, top):
            weights = jnp.exp(scores - top)
            sums = mm(key_blocks(r_ref, block, 1), weights.astype(jnp.bfloat16), 0, 0)
            return jnp.sum(weights, 0, keepdims=True), sums

        diagonal = scores(2 * a + 14, True)
        top = jnp.max(diagonal, 0, keepdims=True)
        total, sums = add(diagonal, 2 * a + 14, top)

        def earlier(i, carry):
            top, total, sums = carry
            block = 2 * a + 14 - 4 * i
            values = scores(block, False)
            new = jnp.maximum(top, jnp.max(values, 0, keepdims=True))
            scale = jnp.exp(top - new)
            more, more_sums = add(values, block, new)
            return new, total * scale + more, sums * scale + more_sums

        steps = (2 * a + 21 - lo_a) // 4
        top, total, sums = lax.fori_loop(1, steps, earlier, (top, total, sums))
        out = jnp.transpose(sums / total)
        for block in range(2):
            rows = unstack_heads(out, block)
            o32_ref[2 * a + block] = rows
            o16_ref[2 * a + block] = rows.astype(jnp.bfloat16)
        lse_ref[a] = top + jnp.log(total)
        return 0

    lax.fori_loop(0, 8, one_pair, 0)


def attend_call(lo, blocks):
    vmem = pl.BlockSpec(memory_space=pltpu.VMEM)
    return pl.pallas_call(
        attend_kernel,
        in_specs=[pl.BlockSpec(memory_space=pltpu.SMEM), vmem],
        out_specs=[vmem, vmem, vmem],
        out_shape=[
            jax.ShapeDtypeStruct((16, 128, 128), jnp.float32),
            jax.ShapeDtypeStruct((16, 128, 128), jnp.bfloat16),
            jax.ShapeDtypeStruct((8, 1, 512), jnp.float32),
        ],
        compiler_params=pltpu.CompilerParams(vmem_limit_bytes=VMEM_LIMIT),
        cost_estimate=TINY,
    )(lo, blocks)


def attend_back_kernel(lo_ref, r_ref, do_ref, o32_ref, lse_ref, out_ref, dk_ref, dv_ref):
    dk_ref[...] = jnp.zeros_like(dk_ref)
    dv_ref[...] = jnp.zeros_like(dv_ref)

    def one_pair(a, _):
        lo_a, lo_b = lo_ref[2 * a], lo_ref[2 * a + 1]
        queries = stack_heads(r_ref, (2 * a, 4), (2 * a + 1, 4))
        grads = stack_heads(do_ref, 2 * a, 2 * a + 1)
        out = jnp.concatenate([o32_ref[2 * a]] * 2 + [o32_ref[2 * a + 1]] * 2, 0)
        delta = jnp.sum(jnp.transpose(grads.astype(jnp.float32) * out), 0, keepdims=True)
        lse = lse_ref[a]

        def blocks_back(block, diagonal):
            keys, values = key_blocks(r_ref, block, 0), key_blocks(r_ref, block, 1)
            weights = jnp.exp(mm(keys, queries, 1, 1) - lse)
            weights = masked(weights, a, block, lo_a, lo_b, diagonal, 0.0)
            grad_scores = (weights * (mm(values, grads, 1, 1) - delta)).astype(jnp.bfloat16)
            grad_values = mm(weights.astype(jnp.bfloat16), grads)
            grad_keys = mm(grad_scores, queries)
            for k in range(4):
                index, rows = jnp.maximum(block + k, 0), slice(k * 128, k * 128 + 128)
                dv_ref[index] += grad_values[rows]
                dk_ref[index] += grad_keys[rows]
            return mm(grad_scores, keys, 0, 0)

        def earlier(i, grad_query):
            return grad_query + blocks_back(2 * a + 14 - 4 * i, False)

        steps = (2 * a + 21 - lo_a) // 4
        grad_query = blocks_back(2 * a + 14, True)
        grad_query = lax.fori_loop(1, steps, earlier, grad_query)
        for block in range(2):
            rows = unstack_heads(grad_query, block) * score_scale
            out_ref[2 * a + block, 4] = rows.astype(jnp.bfloat16)
        return 0

    lax.fori_loop(0, 8, one_pair, 0)

    def finish(c, _):
        out_ref[c, 0] = dk_ref[c].astype(jnp.bfloat16)
        out_ref[c, 1] = dv_ref[c].astype(jnp.bfloat16)
        out_ref[c, 2] = dk_ref[c + 16].astype(jnp.bfloat16)
        out_ref[c, 3] = dv_ref[c + 16].astype(jnp.bfloat16)
        return 0

    lax.fori_loop(0, 16, finish, 0)


def attend_back_call(lo, blocks, grads, out, lse):
    vmem = pl.BlockSpec(memory_space=pltpu.VMEM)
    return pl.pallas_call(
        attend_back_kernel,
        in_specs=[pl.BlockSpec(memory_space=pltpu.SMEM), vmem, vmem, vmem, vmem],
        out_specs=vmem,
        out_shape=jax.ShapeDtypeStruct((16, 5, 128, 128), jnp.bfloat16),
        scratch_shapes=[
            pltpu.VMEM((32, 128, 128), jnp.float32),
            pltpu.VMEM((32, 128, 128), jnp.float32),
        ],
        compiler_params=pltpu.CompilerParams(vmem_limit_bytes=VMEM_LIMIT),
        cost_estimate=TINY,
    )(lo, blocks, grads, out, lse)


def turn_back_kernel(r_ref, halo_ref, cos_ref, up_ref, down_ref, out_ref, bias_ref):
    for j in range(2):
        sums = [jnp.zeros((1, 128), jnp.float32) for _ in range(3)]
        for x in range(4):
            rows = slice(x * 128, (x + 1) * 128)

            def turned(grad):
                return (
                    grad * cos_ref[rows]
                    - pltpu.roll(grad, 120, 1) * up_ref[rows]
                    - pltpu.roll(grad, 8, 1) * down_ref[rows]
                )

            def read(slot):
                later = r_ref[x + 1, j, 0, slot] if x < 3 else halo_ref[j, 0, slot]
                return r_ref[x, j, 0, slot + 2].astype(jnp.float32) + later.astype(jnp.float32)

            parts = (
                turned(r_ref[x, j, 0, 4].astype(jnp.float32)),
                turned(read(0)),
                read(1),
            )
            for part in range(3):
                grad = parts[part].astype(jnp.bfloat16)
                column = (j * 3 + part) * 128
                out_ref[0, rows, column : column + 128] = grad
                sums[part] = sums[part] + jnp.sum(grad.astype(jnp.float32), 0, keepdims=True)
        for part in range(3):
            column = (j * 3 + part) * 128
            bias_ref[0, :, column : column + 128] = sums[part]


def turn_back_call(blocks, halo, tables):
    table = pl.BlockSpec((512, 128), lambda h: (0, 0))
    return pl.pallas_call(
        turn_back_kernel,
        grid=(2,),
        in_specs=[
            pl.BlockSpec((4, 2, 1, 5, 128, 128), lambda h: (0, 0, h, 0, 0, 0)),
            pl.BlockSpec((2, 1, 2, 128, 128), lambda h: (0, h, 0, 0, 0)),
            table,
            table,
            table,
        ],
        out_specs=[
            pl.BlockSpec((1, 512, 768), lambda h: (h, 0, 0)),
            pl.BlockSpec((1, 1, 768), lambda h: (h, 0, 0)),
        ],
        out_shape=[
            jax.ShapeDtypeStruct((2, 512, 768), jnp.bfloat16),
            jax.ShapeDtypeStruct((2, 1, 768), jnp.float32),
        ],
        compiler_params=pltpu.CompilerParams(vmem_limit_bytes=VMEM_LIMIT),
        cost_estimate=TINY,
    )(blocks, halo, *tables)


def normed_back_kernel(
    core_ref, g_ref, unit_ref, own0_ref, own1_ref, oth0_ref, oth1_ref, out_ref, gain_grad_ref, shift_grad_ref
):
    grads = jnp.concatenate([g_ref[0], g_ref[1]], 1)

    def rows(w0_ref, w1_ref, yl):
        return jnp.concatenate(
            [w[:, :384] for h in range(2) for w in (w0_ref[0, h, yl, :128], w1_ref[h, yl, 0])], 1
        )

    weights = jnp.concatenate(
        [ordered(core_ref, rows(own0_ref, own1_ref, yl), rows(oth0_ref, oth1_ref, yl)) for yl in range(2)], 0
    )
    total = mm(grads, weights, 1, 1)
    out_ref[...] = total.astype(jnp.bfloat16).reshape(4, 128, 512)
    unit = unit_ref[...].reshape(512, 512).astype(jnp.float32)
    gain_grad_ref[...] = jnp.sum(total * unit, 0, keepdims=True)
    shift_grad_ref[...] = jnp.sum(total, 0, keepdims=True)


def normed_back_call(core, grad_joint, unit, weights):
    first = pl.BlockSpec((1, 2, 2, 144, 512), lambda n: (n, 0, 0, 0, 0))
    second = pl.BlockSpec((2, 2, 1, 128, 512), lambda n: (0, 0, n, 0, 0))
    ring = pl.BlockSpec((4, 128, 512), lambda n: (0, 0, n))
    vector = pl.BlockSpec((1, 512), lambda n: (0, n))
    return pl.pallas_call(
        normed_back_kernel,
        grid=(4,),
        in_specs=[
            pl.BlockSpec(memory_space=pltpu.SMEM),
            pl.BlockSpec((2, 512, 768), lambda n: (0, 0, 0)),
            ring,
            first,
            second,
            first,
            second,
        ],
        out_specs=[ring, vector, vector],
        out_shape=[
            jax.ShapeDtypeStruct((4, 128, D), jnp.bfloat16),
            jax.ShapeDtypeStruct((1, D), jnp.float32),
            jax.ShapeDtypeStruct((1, D), jnp.float32),
        ],
        compiler_params=pltpu.CompilerParams(vmem_limit_bytes=VMEM_LIMIT),
        cost_estimate=TINY,
    )(core, grad_joint, unit, *weights)


def local(
    tokens,
    cotangent,
    doc_ids,
    ln1_gain,
    ln1_shift,
    w_qkv,
    b_qkv,
    w_out,
    ln2_gain,
    ln2_shift,
    w_gate,
    w_up,
    w_down,
):
    half = lax.axis_index("yh")
    blk = lax.axis_index(BLK)

    core = lax.axis_index("k").reshape(1)
    vectors = jnp.stack([ln1_gain, ln1_shift, ln2_gain, ln2_shift])
    first_pair, second_pair = pack_joint_call(w_qkv.transpose(1, 0, 2), w_out, vectors, b_qkv)
    ring = ring_gather(tokens)
    place = jnp.stack([lax.axis_index("x"), lax.axis_index("k")]).astype(jnp.int32)
    own0 = gather(gather(first_pair, Y), ("z",)).reshape(4, 2, 2, 144, 512)
    own1 = gather(gather(second_pair, ("z",)), Y).reshape(2, 2, 4, 128, 512)
    own0 = after(own0, ring)
    weights = (own0, own1, swap_core(own0), swap_core(own1))
    before = lax.ppermute(ring[3], ("yh",), [(0, 1)])
    rest = pack_hidden_call(w_gate.T, w_up.T, w_down)
    rest = after(rest, own0, own1, before)
    rest = lax.all_gather(rest, PLANE, axis=0, tiled=True).reshape(2, D, 3 * HID_PAD)

    small = jnp.stack([own0[:, :, :, 128:, :128], weights[2][:, :, :, 128:, :128]])
    small = jnp.where(core[0] == 0, small, small[::-1]).astype(jnp.float32)
    bias = small[..., 8:11, :16].transpose(2, 4, 1, 3, 0, 5).reshape(2, 3, 2, 128).reshape(2, 3, 1, 256)
    vectors = small[:, :, 0, :, :4].transpose(3, 1, 2, 0, 4).reshape(4, D)
    gain_one, shift_one, gain_two, shift_two = [vectors[i : i + 1] for i in range(4)]

    first_block = jnp.sum((doc_ids[None, :] < doc_ids[:, None]).astype(jnp.int32), axis=1)
    cycles = jnp.arange(4, dtype=jnp.int32) * 16 + half * 64 + blk
    cycles = jnp.concatenate([cycles, 48 + blk.reshape(1)])
    block_position = (cycles - first_block[cycles]) * BLK_TOK
    positions = (block_position[:, None] + jnp.arange(BLK_TOK, dtype=jnp.int32)).reshape(640)
    tables = rotary_tables(positions)
    first_query = half * 64 + (blk // 4) * 16
    lo = lax.dynamic_slice(first_block, (first_query,), (16,)) - (first_query - 16)

    payload, normed_one, unit_one = qkv_call(
        core, ring, before, gain_one, shift_one, weights, bias, tables
    )
    cot, own0, own1, payload = lax.optimization_barrier((cotangent, own0, own1, payload))
    ring_cot = gather(cot, ("x",))
    own_rows = out_rows_call(own0, own1)
    blocks = after(exchange(payload.reshape(16, 5, 128, 128), BLK), ring_cot)
    own_rows = [own_rows] + [send(own_rows, ("x",), t) for t in (1, 2, 3)]
    att32, att16, lse = attend_call(lo, blocks)
    own_rows = after(own_rows, att16)
    other_rows = [swap_core(rows) for rows in own_rows]
    attended = exchange(att16, BLK).reshape(4, 2, 2, 128, 128)
    middle, normed_two = project_call(
        place, exchange(attended, ("x",)), tokens, gain_two, shift_two, own_rows, other_rows
    )

    ring_two = exchange(normed_two, ("x",))
    active, grad_gu, ring_grad, ring_out = feed_forward_call(ring_two, ring_cot, rest)
    shared = plane_grad_call(core, with_other(ring_cot), with_other(active), HID_PAD, 2 * HID_PAD)
    came = after(exchange(ring_grad, ("x",)), shared)
    grad_middle, grad_branch, grad_gain_two, grad_shift_two, grad_att = project_back_call(
        place, came, middle, cotangent, gain_two, own_rows, other_rows
    )
    grad_att = exchange(grad_att, ("x",))
    ring_branch = lax.all_gather(after(grad_branch, grad_att), "x", axis=0)
    shared = plane_grad_call(core, with_other(ring_two), with_other(grad_gu), 2 * HID_PAD, 0, shared)
    grad_att = after(exchange(grad_att.reshape(16, 128, 128), BLK), shared)
    attended_pair = with_other(attended.transpose(2, 0, 3, 1, 4).reshape(2, 512, 256))

    mixed = lax.psum_scatter(
        after(ring_out, grad_att).reshape(512, D), "x", scatter_dimension=0, tiled=True
    )
    back = attend_back_call(lo, blocks, grad_att, att32, lse)
    branch_pair = with_other(after(ring_branch, back))
    shared = plane_grad_call(core, branch_pair, attended_pair, 256, 3 * HID_PAD, shared)
    back = exchange(back, BLK).reshape(4, 2, 2, 5, 128, 128)
    back, shared = lax.optimization_barrier((back, shared))
    shared = plane_sum(shared)
    mixed = (middle + after(mixed, back).astype(jnp.float32)).astype(jnp.bfloat16)
    halo_back = lax.ppermute(back[0, :, :, :2], ("yh",), [(1, 0)])
    back = after(back, mixed)
    grad_joint, grad_bias = turn_back_call(back, halo_back, tables)
    ring_one, grad_gain_one, grad_shift_one = normed_back_call(core, grad_joint, unit_one, weights)
    places = (chip_places(True), chip_places(False))
    parts = joint_grad_call(core, places, with_other(normed_one), with_other(grad_joint))
    pair_came = [first_send(parts[4 * j : 4 * j + 4], j == 0) for j in range(2)]
    pair_came = [second_send(first_sum(part, j == 0), j == 0) for j, part in enumerate(pair_came)]
    norms = jnp.concatenate([grad_gain_one, grad_shift_one, grad_gain_two, grad_shift_two], 0)
    norms = norms.reshape(4, 2, 4, 16, 16).transpose(1, 2, 3, 0, 4).reshape(2, 4, 16, 64)
    biases = grad_bias.reshape(2, 2, 3, 8, 16).transpose(0, 1, 3, 2, 4).reshape(2, 1, 16, 48)
    plane = jnp.arange(4).reshape(1, 4, 1, 1) == lax.axis_index("x")
    biases = jnp.where(plane, biases, 0.0)
    sums = jnp.concatenate([norms, biases, jnp.zeros((2, 4, 16, 16), jnp.float32)], 3)
    sums = jnp.sum(exchange(sums.reshape(128, 128), AXES), 0)
    norms = sums[:64].reshape(4, 16)

    ring_one = after(ring_one, norms, parts[0])
    came = after(exchange(ring_one, ("x",)), pair_came[0][0], pair_came[1][0])
    input_grad = whole_call(input_back_kernel, jax.ShapeDtypeStruct((128, D), jnp.float32), came, tokens, grad_middle, gain_one)

    def shape(*dims):
        return jax.ShapeDtypeStruct(dims, jnp.float32)

    grad_gate, grad_up, grad_down, grad_out = whole_call(
        shared_end_kernel, [shape(HID, 128)] * 3 + [shape(256, 128)], after(shared, input_grad)
    )
    grad_qkv = whole_call(joint_end_kernel, shape(3, 128, 256), *pair_came[0], *pair_came[1])

    return (
        mixed,
        input_grad,
        norms[0],
        norms[1],
        grad_qkv.transpose(1, 0, 2),
        sums[64:112].reshape(3, 16),
        grad_out,
        norms[2],
        norms[3],
        grad_gate.T,
        grad_up.T,
        grad_down,
    )


def solution(mesh):
    whole = Mesh(mesh.devices.reshape(2, 4, 4, 2, 2), AXES)
    ulysses, blk = ("yh", "x"), BLK
    both = ulysses + blk
    placed = (
        P(both, None),
        P(both, None),
        P(),
        P(blk),
        P(blk),
        P(blk, None, ulysses),
        P(None, both),
        P(ulysses, blk),
        P(blk),
        P(blk),
        P(blk, ulysses),
        P(blk, ulysses),
        P(ulysses, blk),
    )
    return jax.shard_map(
        local,
        mesh=whole,
        in_specs=placed,
        out_specs=(
            P(both, None),
            P(both, None),
            P(both),
            P(both),
            P(blk, None, ulysses),
            P(None, both),
            P(ulysses, blk),
            P(both),
            P(both),
            P(blk, ulysses),
            P(blk, ulysses),
            P(ulysses, blk),
        ),
        check_vma=False,
    )
```

```python
import functools

import jax
import jax.numpy as jnp
from jax import lax
from jax.experimental import pallas as pl
from jax.experimental.pallas import tpu as pltpu
from jax.sharding import Mesh
from jax.sharding import PartitionSpec as P

D = 2048
HEADS = 32
HEAD_DIM = 64
ROT = 16
BLK_TOK = 128
HID = 704
HID_PAD = 768
SHARED = 3 * HID_PAD + 256

eps = 1e-05
rope_base = 10000.0
masked_score = -1e30
score_scale = HEAD_DIM ** (-0.5)

AXES = ("yh", "x", "z", "yl", "k")
PLANE = ("z", "yh", "yl", "k")
BLK = ("z", "yl", "k")
Y = ("yh", "yl")

VMEM_LIMIT = 60 * 1024 * 1024
TINY = pl.CostEstimate(flops=1, bytes_accessed=1, transcendentals=0)


def mm(a, b, ca=1, cb=0):
    return lax.dot_general(a, b, (((ca,), (cb,)), ((), ())), preferred_element_type=jnp.float32)


def swap_core(value):
    return lax.ppermute(value, ("k",), [(0, 1), (1, 0)])


def exchange(parts, axes):
    return lax.all_to_all(parts, axes, 0, 0, tiled=True)


def send(value, axes, step):
    return lax.ppermute(value, axes, [(i, (i + step) % 4) for i in range(4)])


def ring_gather(value):
    return exchange(jnp.broadcast_to(value, (4,) + value.shape), ("x",))


def send(value, axes, step):
    return lax.ppermute(value, axes, [(i, (i + step) % 4) for i in range(4)])


def gather(value, axes, *others):
    me = lax.axis_index(axes)
    pieces = [send(value, axes, step) for step in (1, 3, 2)]
    if others:
        pieces = after(pieces, *others)
    buffer = jnp.zeros((4,) + value.shape, value.dtype)
    for step, piece in zip((0, 1, 3, 2), [value] + pieces):
        buffer = lax.dynamic_update_index_in_dim(buffer, piece, (me - step) % 4, 0)
    return buffer


def ring_gather(value):
    return exchange(jnp.broadcast_to(value, (4,) + value.shape), ("x",))


def after(value, *others):
    return lax.optimization_barrier((value,) + others)[0]


def rotary_tables(positions):
    halfway = ROT // 2
    counter = jnp.arange(halfway, dtype=jnp.float32)
    frequency = rope_base ** (-2.0 * counter / ROT)
    lane = jnp.arange(128) % HEAD_DIM
    frequency = jnp.where(lane < ROT, jnp.tile(frequency, 16), 0.0)
    angles = positions.astype(jnp.float32)[:, None] * frequency[None, :]
    sine = jnp.sin(angles)
    return (
        jnp.cos(angles),
        jnp.where(lane < halfway, -sine, 0.0),
        jnp.where((lane >= halfway) & (lane < ROT), sine, 0.0),
    )


def pack_joint_kernel(qkv_ref, out_ref, vectors_ref, bias_ref, w_ref, small_ref):
    out_t = jnp.transpose(out_ref[...])
    for j in range(2):
        pair = slice(j * 128, (j + 1) * 128)
        for part in range(3):
            column = j * 512 + part * 128
            w_ref[:128, column : column + 128] = qkv_ref[part, :, pair]
        w_ref[:128, j * 512 + 384 : j * 512 + 512] = out_t[:, pair]
    small_ref[...] = jnp.zeros_like(small_ref)
    small_ref[0:4, :128] = vectors_ref[...].astype(jnp.float32)
    small_ref[8:11, :16] = bias_ref[...].astype(jnp.float32)
    w_ref[128:, :] = small_ref[...].astype(jnp.bfloat16)


def pack_joint_call(qkv, out, vectors, bias):
    return whole_call(
        pack_joint_kernel,
        jax.ShapeDtypeStruct((144, 1024), jnp.bfloat16),
        qkv,
        out,
        vectors,
        bias,
        scratch=[pltpu.VMEM((16, 1024), jnp.float32)],
    )


def pack_hidden_kernel(gate_ref, up_ref, down_ref, rest_ref):
    for i, ref in enumerate((gate_ref, up_ref, down_ref)):
        first = i * HID_PAD
        rest_ref[:, first + HID_PAD - 128 : first + HID_PAD] = jnp.zeros((128, 128), jnp.bfloat16)
        rest_ref[:, first : first + HID] = jnp.transpose(ref[...])


def pack_hidden_call(gate, up, down):
    return whole_call(
        pack_hidden_kernel, jax.ShapeDtypeStruct((128, 3 * HID_PAD), jnp.bfloat16), gate, up, down
    )


def core_columns(ref, core, blocks):
    columns = [ref[:blocks, :, pl.ds(pl.multiple_of((2 * i + core) * 128, 128), 128)] for i in range(8)]
    return jnp.concatenate(columns, 2).reshape(blocks * 128, 1024)


def normalise(values):
    centred = values - jnp.mean(values, -1, keepdims=True)
    inverse = lax.rsqrt(jnp.mean(centred * centred, -1, keepdims=True) + eps)
    return centred * inverse, inverse


def qkv_kernel(
    x_ref,
    before_ref,
    gain_ref,
    shift_ref,
    w0_ref,
    w1_ref,
    bias_ref,
    cos_ref,
    up_ref,
    down_ref,
    out_ref,
    normed_ref,
    unit_ref,
    normed_rows,
):
    part = pl.program_id(1)

    @pl.when((pl.program_id(0) == 0) & (part == 0))
    def _():
        for b in range(5):
            block = x_ref[b] if b < 4 else before_ref[...]
            unit, _ = normalise(block.astype(jnp.float32))
            normed = (unit * gain_ref[...] + shift_ref[...]).astype(jnp.bfloat16)
            if b < 4:
                normed_ref[b] = normed
                unit_ref[b] = unit.astype(jnp.bfloat16)
            normed_rows[b * 128 : (b + 1) * 128] = normed

    def joint(rows):
        weights = [ref[:, 0, :, :128, :].reshape(D, 128) for ref in (w0_ref, w1_ref)]
        return mm(normed_rows[:rows], jnp.concatenate(weights, 1)) + bias_ref[0, 0]

    def turned(value):
        rows = value.shape[0]
        return (
            value * cos_ref[:rows]
            + pltpu.roll(value, 120, 1) * up_ref[:rows]
            + pltpu.roll(value, 8, 1) * down_ref[:rows]
        )

    @pl.when(part == 0)
    def _():
        value = joint(512)
        for j in range(2):
            query = turned(value[:, j * 128 : (j + 1) * 128]) * score_scale
            out_ref[:, j, 0, 4] = query.astype(jnp.bfloat16).reshape(4, 128, 128)

    @pl.when(part > 0)
    def _():
        value = joint(640)
        for j in range(2):
            block = value[:, j * 128 : (j + 1) * 128]
            block = jnp.where(part == 1, turned(block), block)
            block = block.astype(jnp.bfloat16).reshape(5, 128, 128)

            @pl.when(part == 1)
            def _():
                out_ref[:, j, 0, 2] = block[:4]
                out_ref[1:, j, 0, 0] = block[:3]
                out_ref[0, j, 0, 0] = block[4]

            @pl.when(part == 2)
            def _():
                out_ref[:, j, 0, 3] = block[:4]
                out_ref[1:, j, 0, 1] = block[:3]
                out_ref[0, j, 0, 1] = block[4]


def qkv_call(tokens, before, gain, shift, weights, bias, tables):
    table = pl.BlockSpec((640, 128), lambda h, p: (0, 0))
    vector = pl.BlockSpec((1, D), lambda h, p: (0, 0))
    return pl.pallas_call(
        qkv_kernel,
        grid=(2, 3),
        in_specs=[
            pl.BlockSpec((4, 128, D), lambda h, p: (0, 0, 0)),
            pl.BlockSpec((128, D), lambda h, p: (0, 0)),
            vector,
            vector,
            pl.BlockSpec((4, 1, 4, 144, 128), lambda h, p: (0, h, 0, 0, p)),
            pl.BlockSpec((4, 1, 4, 144, 128), lambda h, p: (0, h, 0, 0, p + 4)),
            pl.BlockSpec((1, 1, 1, 256), lambda h, p: (h, p, 0, 0)),
            table,
            table,
            table,
        ],
        out_specs=[
            pl.BlockSpec((4, 2, 1, 5, 128, 128), lambda h, p: (0, 0, h, 0, 0, 0)),
            pl.BlockSpec((4, 128, D), lambda h, p: (0, 0, 0)),
            pl.BlockSpec((4, 128, D), lambda h, p: (0, 0, 0)),
        ],
        out_shape=[
            jax.ShapeDtypeStruct((4, 2, 2, 5, 128, 128), jnp.bfloat16),
            jax.ShapeDtypeStruct((4, 128, D), jnp.bfloat16),
            jax.ShapeDtypeStruct((4, 128, D), jnp.bfloat16),
        ],
        scratch_shapes=[pltpu.VMEM((640, D), jnp.bfloat16)],
        compiler_params=pltpu.CompilerParams(vmem_limit_bytes=VMEM_LIMIT),
        cost_estimate=TINY,
    )(tokens, before, gain, shift, weights, weights, bias, *tables)


def whole_call(kernel, out_shape, *operands, scratch=()):
    vmem = pl.BlockSpec(memory_space=pltpu.VMEM)
    return pl.pallas_call(
        kernel,
        in_specs=[vmem] * len(operands),
        out_specs=jax.tree.map(lambda _: vmem, out_shape),
        out_shape=out_shape,
        scratch_shapes=list(scratch),
        compiler_params=pltpu.CompilerParams(vmem_limit_bytes=VMEM_LIMIT),
        cost_estimate=TINY,
    )(*operands)


def back_through(came_ref, values, gain):
    grad = came_ref[0].astype(jnp.float32)
    for i in range(1, 4):
        grad = grad + came_ref[i].astype(jnp.float32)
    unit, inverse = normalise(values)
    grad_unit = grad * gain
    centred_grad = (
        grad_unit
        - jnp.mean(grad_unit, -1, keepdims=True)
        - unit * jnp.mean(grad_unit * unit, -1, keepdims=True)
    )
    gain_grad = jnp.sum(grad * unit, 0, keepdims=True)
    return inverse * centred_grad, gain_grad, jnp.sum(grad, 0, keepdims=True)


def input_back_kernel(came_ref, tokens_ref, grad_ref, gain_ref, out_ref):
    values = tokens_ref[...].astype(jnp.float32)
    out_ref[...] = grad_ref[...] + back_through(came_ref, values, gain_ref[...])[0]


def shared_end_kernel(total_ref, gate_ref, up_ref, down_ref, out_ref):
    total = jnp.transpose(total_ref[...].astype(jnp.float32))
    for c in range(3):
        width = min(HID, c * 256 + 256) - c * 256
        gate_ref[c * 256 : c * 256 + width] = total[c * 512 : c * 512 + width]
        up_ref[c * 256 : c * 256 + width] = total[c * 512 + 256 : c * 512 + 256 + width]
    down_ref[...] = total[2 * HID_PAD : 2 * HID_PAD + HID]
    out_ref[...] = total[3 * HID_PAD :]


def joint_end_kernel(*refs):
    for j in range(2):
        total = sum(ref[...].astype(jnp.float32) for ref in refs[4 * j : 4 * j + 4])
        for part in range(3):
            refs[8][part, :, j * 128 : (j + 1) * 128] = total[:, part * 128 : part * 128 + 128]


def out_rows_kernel(place_ref, w0_ref, w1_ref, out_ref):
    for yl in range(2):
        for h in range(2):
            for j, ref in enumerate((w0_ref, w1_ref)):
                column = h * 256 + j * 128
                out_ref[yl, :, column : column + 128] = ref[0, h, 2 * yl + place_ref[1], :128]


def out_rows_call(place, weights):
    return pl.pallas_call(
        out_rows_kernel,
        grid=(4,),
        in_specs=[
            pl.BlockSpec(memory_space=pltpu.SMEM),
            pl.BlockSpec((1, 2, 4, 144, 128), lambda n: (n, 0, 0, 0, 3)),
            pl.BlockSpec((1, 2, 4, 144, 128), lambda n: (n, 0, 0, 0, 7)),
        ],
        out_specs=pl.BlockSpec((2, 128, 512), lambda n: (n, 0, 0)),
        out_shape=jax.ShapeDtypeStruct((8, 128, 512), jnp.bfloat16),
        compiler_params=pltpu.CompilerParams(vmem_limit_bytes=VMEM_LIMIT),
        cost_estimate=TINY,
    )(place, weights, weights)


def planes_columns(refs, yl):
    return jnp.concatenate([ref[yl] for ref in refs], 1)


def project_kernel(place_ref, att_ref, tokens_ref, gain_ref, shift_ref, *refs):
    own_refs, other_refs, (middle_ref, normed_ref, att_cols, total) = refs[:4], refs[4:8], refs[8:]
    n, me, core = pl.program_id(0), place_ref[0], place_ref[1]

    @pl.when(n == 0)
    def _():
        for t in range(4):
            x = (me + 4 - t) % 4
            for h in range(2):
                for j in range(2):
                    column = t * 512 + h * 256 + j * 128
                    att_cols[:, column : column + 128] = att_ref[x, j, h]

    weights = jnp.concatenate(
        [planes_columns(refs, yl) for refs in (own_refs, other_refs) for yl in range(2)], 0
    )
    values = mm(att_cols[...], weights, 1, 1)
    for i in range(4):
        holder = core if i < 2 else 1 - core
        column = pl.multiple_of((n * 4 + i % 2 * 2 + holder) * 128, 128)
        total[:, pl.ds(column, 128)] = values[:, i * 128 : i * 128 + 128]

    @pl.when(n == 3)
    def _():
        middle = tokens_ref[...].astype(jnp.float32) + total[...]
        middle_ref[...] = middle
        normed = (normalise(middle)[0] * gain_ref[...] + shift_ref[...]).astype(jnp.bfloat16)
        for i in range(4):
            normed_ref[i] = normed


def project_call(place, att, tokens, gain, shift, own, other):
    def whole(*dims):
        return pl.BlockSpec(dims, lambda n: (0,) * len(dims))

    rows = pl.BlockSpec((2, 128, 512), lambda n: (n, 0, 0))
    return pl.pallas_call(
        project_kernel,
        grid=(4,),
        in_specs=[
            pl.BlockSpec(memory_space=pltpu.SMEM),
            whole(4, 2, 2, 128, 128),
            whole(128, D),
            whole(1, D),
            whole(1, D),
        ]
        + [rows] * 8,
        out_specs=[whole(128, D), whole(4, 128, D)],
        out_shape=[
            jax.ShapeDtypeStruct((128, D), jnp.float32),
            jax.ShapeDtypeStruct((4, 128, D), jnp.bfloat16),
        ],
        scratch_shapes=[pltpu.VMEM((128, D), jnp.bfloat16), pltpu.VMEM((128, D), jnp.float32)],
        compiler_params=pltpu.CompilerParams(vmem_limit_bytes=VMEM_LIMIT),
        cost_estimate=TINY,
    )(place, att, tokens, gain, shift, *own, *other)


def project_back_kernel(place_ref, came_ref, middle_ref, cot_ref, gain_ref, *refs):
    own_refs, other_refs = refs[:4], refs[4:8]
    grad_ref, low_ref, gain_grad_ref, shift_grad_ref, out_ref, low, total = refs[8:]
    n, me, core = pl.program_id(0), place_ref[0], place_ref[1]

    @pl.when(n == 0)
    def _():
        grad, gain_grad_ref[...], shift_grad_ref[...] = back_through(came_ref, middle_ref[...], gain_ref[...])
        grad = grad + cot_ref[...].astype(jnp.float32)
        grad_ref[...] = grad
        low[...] = grad.astype(jnp.bfloat16)
        low_ref[...] = low[...]
        total[...] = jnp.zeros_like(total)

    columns = []
    for i in range(4):
        holder = core if i < 2 else 1 - core
        column = pl.multiple_of((n * 4 + i % 2 * 2 + holder) * 128, 128)
        columns.append(low[:, pl.ds(column, 128)])
    weights = jnp.concatenate(
        [planes_columns(refs, yl) for refs in (own_refs, other_refs) for yl in range(2)], 0
    )
    total[...] += mm(jnp.concatenate(columns, 1), weights)

    @pl.when(n == 3)
    def _():
        for t in range(4):
            x = (me + 4 - t) % 4
            for h in range(2):
                for j in range(2):
                    column = t * 512 + h * 256 + j * 128
                    out_ref[x, j, h] = total[:, column : column + 128].astype(jnp.bfloat16)


def project_back_call(place, came, middle, cot, gain, own, other):
    def whole(*dims):
        return pl.BlockSpec(dims, lambda n: (0,) * len(dims))

    rows = pl.BlockSpec((2, 128, 512), lambda n: (n, 0, 0))
    return pl.pallas_call(
        project_back_kernel,
        grid=(4,),
        in_specs=[
            pl.BlockSpec(memory_space=pltpu.SMEM),
            whole(4, 128, D),
            whole(128, D),
            whole(128, D),
            whole(1, D),
        ]
        + [rows] * 8,
        out_specs=[whole(128, D), whole(128, D), whole(1, D), whole(1, D), whole(4, 2, 2, 128, 128)],
        out_shape=[
            jax.ShapeDtypeStruct((128, D), jnp.float32),
            jax.ShapeDtypeStruct((128, D), jnp.bfloat16),
            jax.ShapeDtypeStruct((1, D), jnp.float32),
            jax.ShapeDtypeStruct((1, D), jnp.float32),
            jax.ShapeDtypeStruct((4, 2, 2, 128, 128), jnp.bfloat16),
        ],
        scratch_shapes=[pltpu.VMEM((128, D), jnp.bfloat16), pltpu.VMEM((128, D), jnp.float32)],
        compiler_params=pltpu.CompilerParams(vmem_limit_bytes=VMEM_LIMIT),
        cost_estimate=TINY,
    )(place, came, middle, cot, gain, *own, *other)


def feed_forward_kernel(
    x_ref, cot_ref, gate_ref, up_ref, down_ref, active_ref, grads_ref, back_ref, out_ref, back_sum, out_sum
):
    first_half = pl.program_id(0) == 0
    x = x_ref[...].reshape(512, D)
    cot = cot_ref[...].reshape(512, D)
    for c in range(3):
        columns = slice(c * 256, c * 256 + 256)
        gate = mm(x, gate_ref[:, 0, :, columns].reshape(D, 256))
        up = mm(x, up_ref[:, 0, :, columns].reshape(D, 256))
        grad_active = mm(cot, down_ref[:, 0, :, columns].reshape(D, 256))
        sigmoid = jax.nn.sigmoid(gate)
        silu = gate * sigmoid
        active_ref[0, :, columns] = (silu * up).astype(jnp.bfloat16)
        grad_gate = grad_active * up * (sigmoid + silu * (1.0 - sigmoid))
        grads_ref[0, :, c * 512 : c * 512 + 256] = grad_gate.astype(jnp.bfloat16)
        grads_ref[0, :, c * 512 + 256 : c * 512 + 512] = (grad_active * silu).astype(jnp.bfloat16)
    for n in range(4):
        rows = slice(n * 512, n * 512 + 512)
        weights = jnp.concatenate(
            [ref[n, 0, :, c * 256 : c * 256 + 256] for c in range(3) for ref in (gate_ref, up_ref)], 1
        )
        back = mm(grads_ref[0], weights, 1, 1)
        out = mm(active_ref[0], down_ref[n, 0], 1, 1)

        @pl.when(first_half)
        def _():
            back_sum[:, rows] = back
            out_sum[:, rows] = out

        @pl.when(~first_half)
        def _():
            back_ref[:, :, rows] = (back_sum[:, rows] + back).astype(jnp.bfloat16).reshape(4, 128, 512)
            out_ref[:, :, rows] = (out_sum[:, rows] + out).astype(jnp.bfloat16).reshape(4, 128, 512)


def feed_forward_call(x, ring, rest):
    tokens = pl.BlockSpec((4, 128, D), lambda h: (0, 0, 0))
    tokens_once = pl.BlockSpec((4, 128, D), lambda h: (0, 0, 0), pipeline_mode=pl.Buffered(1))
    weight = [pl.BlockSpec((4, 1, 512, HID_PAD), lambda h, i=i: (0, h, 0, i)) for i in range(3)]
    ring_shape = jax.ShapeDtypeStruct((4, 128, D), jnp.bfloat16)
    return pl.pallas_call(
        feed_forward_kernel,
        grid=(2,),
        in_specs=[tokens_once, tokens_once] + weight,
        out_specs=[
            pl.BlockSpec((1, 512, HID_PAD), lambda h: (h, 0, 0)),
            pl.BlockSpec((1, 512, 2 * HID_PAD), lambda h: (h, 0, 0)),
            tokens,
            tokens,
        ],
        out_shape=[
            jax.ShapeDtypeStruct((2, 512, HID_PAD), jnp.bfloat16),
            jax.ShapeDtypeStruct((2, 512, 2 * HID_PAD), jnp.bfloat16),
            ring_shape,
            ring_shape,
        ],
        scratch_shapes=[pltpu.VMEM((512, D), jnp.float32), pltpu.VMEM((512, D), jnp.float32)],
        compiler_params=pltpu.CompilerParams(vmem_limit_bytes=VMEM_LIMIT),
        cost_estimate=TINY,
    )(x, ring, rest, rest, rest)


def plane_grad_kernel(core_ref, left_ref, left_other_ref, right_ref, right_other_ref, *refs):
    out_ref, left_t = refs[-2:]

    @pl.when((pl.program_id(0) == 0) & (pl.program_id(1) == 0))
    def _():
        left_t[:, :512] = jnp.transpose(core_columns(left_ref, core_ref[0], 4))
        left_t[:, 512:] = jnp.transpose(core_columns(left_other_ref, core_ref[0], 4))

    total = mm(left_t[...], jnp.concatenate([right_ref[0], right_other_ref[0]], 0)).astype(jnp.bfloat16)
    for z in range(4):
        for yl in range(2):
            row = (z * 2 + yl) * 128
            out_ref[0, yl, z] = total[row : row + 128]


def plane_grad_call(core, left, right, columns, first, shared=None):
    left_block = pl.BlockSpec((4, 128, D), lambda n, h: (0, 0, 0))
    right_block = pl.BlockSpec((1, 512, 256), lambda n, h: (h, 0, n))
    extra = [] if shared is None else [shared]
    return pl.pallas_call(
        plane_grad_kernel,
        grid=(columns // 256, 2),
        in_specs=[
            pl.BlockSpec(memory_space=pltpu.SMEM),
            left_block,
            left_block,
            right_block,
            right_block,
        ]
        + [pl.BlockSpec(memory_space=pl.ANY)] * len(extra),
        out_specs=pl.BlockSpec((1, 2, 4, 128, 256), lambda n, h: (h, 0, 0, 0, first // 256 + n)),
        out_shape=jax.ShapeDtypeStruct((2, 2, 4, 128, SHARED), jnp.bfloat16),
        input_output_aliases={5: 0} if extra else {},
        scratch_shapes=[pltpu.VMEM((1024, 1024), jnp.bfloat16)],
        compiler_params=pltpu.CompilerParams(vmem_limit_bytes=VMEM_LIMIT),
        cost_estimate=TINY,
    )(core, *left, *right, *extra)


def weight_grad_kernel(core_ref, place_ref, left_ref, left_other_ref, right_ref, right_other_ref, *refs):
    outs, left_t = refs[:4], refs[4]
    h = pl.program_id(1)

    @pl.when((h == 0) & (pl.program_id(0) == 0))
    def _():
        left_t[:, :512] = jnp.transpose(core_columns(left_ref, core_ref[0], 4))
        left_t[:, 512:] = jnp.transpose(core_columns(left_other_ref, core_ref[0], 4))

    total = mm(left_t[...], jnp.concatenate([right_ref[0], right_other_ref[0]], 0)).astype(jnp.bfloat16)
    for z in range(4):
        for yl in range(2):
            row = (z * 2 + yl) * 128
            chip = (h * 2 + yl) * 4 + z
            step, slot = place_ref[0, chip], place_ref[1, chip]
            for t in range(4):

                @pl.when(step == t)
                def _():
                    outs[t][slot] = total[row : row + 128]


def weight_grad_call(core, place, left, right, columns):
    smem = pl.BlockSpec(memory_space=pltpu.SMEM)
    left_block = pl.BlockSpec((4, 128, D), lambda n, h: (0, 0, 0))
    right_block = pl.BlockSpec((1, 512, 256), lambda n, h: (h, 0, n))
    return pl.pallas_call(
        weight_grad_kernel,
        grid=(columns // 256, 2),
        in_specs=[smem, smem, left_block, left_block, right_block, right_block],
        out_specs=[pl.BlockSpec((4, 128, 256), lambda n, h: (0, 0, n))] * 4,
        out_shape=[jax.ShapeDtypeStruct((4, 128, columns), jnp.bfloat16)] * 4,
        scratch_shapes=[pltpu.VMEM((1024, 1024), jnp.bfloat16)],
        compiler_params=pltpu.CompilerParams(vmem_limit_bytes=VMEM_LIMIT),
        cost_estimate=TINY,
    )(core, place, *left, *right)


def joint_grad_kernel(core_ref, place_ref, left_ref, left_other_ref, right_ref, right_other_ref, *refs):
    outs, left_t = refs[:8], refs[8]
    h = pl.program_id(0)

    @pl.when(h == 0)
    def _():
        left_t[:, :512] = jnp.transpose(core_columns(left_ref, core_ref[0], 4))
        left_t[:, 512:] = jnp.transpose(core_columns(left_other_ref, core_ref[0], 4))

    right = jnp.concatenate([right_ref[0], right_other_ref[0]], 0)
    total = mm(left_t[...], right).astype(jnp.bfloat16)
    for z in range(4):
        for yl in range(2):
            row = (z * 2 + yl) * 128
            chip = (h * 2 + yl) * 4 + z
            for j in range(2):
                step, slot = place_ref[2 * j, chip], place_ref[2 * j + 1, chip]
                for t in range(4):

                    @pl.when(step == t)
                    def _():
                        outs[4 * j + t][slot] = total[row : row + 128, j * 384 : j * 384 + 384]


def joint_grad_call(core, places, left, right):
    smem = pl.BlockSpec(memory_space=pltpu.SMEM)
    left_block = pl.BlockSpec((4, 128, D), lambda h: (0, 0, 0))
    right_block = pl.BlockSpec((1, 512, 768), lambda h: (h, 0, 0))
    return pl.pallas_call(
        joint_grad_kernel,
        grid=(2,),
        in_specs=[smem, smem, left_block, left_block, right_block, right_block],
        out_specs=[pl.BlockSpec((4, 128, 384), lambda h: (0, 0, 0))] * 8,
        out_shape=[jax.ShapeDtypeStruct((4, 128, 384), jnp.bfloat16)] * 8,
        scratch_shapes=[pltpu.VMEM((1024, 1024), jnp.bfloat16)],
        compiler_params=pltpu.CompilerParams(vmem_limit_bytes=VMEM_LIMIT),
        cost_estimate=TINY,
    )(core, jnp.concatenate(places, 0), *left, *right)


def split_sum_kernel(place_ref, a_ref, b_ref, c_ref, d_ref, *out_refs):
    for t in range(4):
        i = (place_ref[0] + t) % 4
        total = sum(ref[i].astype(jnp.float32) for ref in (a_ref, b_ref, c_ref, d_ref))
        out_refs[t][...] = total.astype(jnp.bfloat16)


def split_sum_call(place, parts):
    columns = parts[0].shape[2]
    width = 256 if columns % 256 == 0 else 384
    return pl.pallas_call(
        split_sum_kernel,
        grid=(columns // width,),
        in_specs=[pl.BlockSpec(memory_space=pltpu.SMEM)]
        + [pl.BlockSpec((4, 128, width), lambda n: (0, 0, n))] * 4,
        out_specs=[pl.BlockSpec((128, width), lambda n: (0, n))] * 4,
        out_shape=[jax.ShapeDtypeStruct((128, columns), jnp.bfloat16)] * 4,
        compiler_params=pltpu.CompilerParams(vmem_limit_bytes=VMEM_LIMIT),
        cost_estimate=TINY,
    )(place, *parts)


def chip_places(y_first):
    y, z = jnp.arange(16, dtype=jnp.int32) // 4, jnp.arange(16, dtype=jnp.int32) % 4
    if y_first:
        return jnp.stack([(y - lax.axis_index(Y)) % 4, z])
    return jnp.stack([(z - lax.axis_index("z")) % 4, y])


def plane_sum(parts):
    parts = parts.reshape(2048, parts.shape[-1])
    return lax.psum_scatter(parts, ("yh", "yl", "z"), scatter_dimension=0, tiled=True)


def with_other(value):
    return value, swap_core(value)


def first_send(parts, y_first):
    axes = Y if y_first else ("z",)
    return [parts[0]] + [send(parts[t], axes, t) for t in (1, 3, 2)]


def first_sum(parts, y_first):
    return split_sum_call(lax.axis_index(("z",) if y_first else Y).reshape(1), parts)


def second_send(parts, y_first):
    axes = ("z",) if y_first else Y
    return [parts[0]] + [send(parts[t], axes, t) for t in (1, 3, 2)]


def stack_heads(ref, *index):
    first = (lax.broadcasted_iota(jnp.int32, (128, 128), 1) < HEAD_DIM).astype(jnp.float32).astype(jnp.bfloat16)
    masks = (first, 1 - first)
    return jnp.concatenate([ref[i] * mask for i in index for mask in masks], 0)


def unstack_heads(values, block):
    low = lax.broadcasted_iota(jnp.int32, (128, 128), 1) < HEAD_DIM
    rows = values[block * 256 : block * 256 + 256]
    return jnp.where(low, rows[:128], rows[128:])


def key_blocks(r_ref, block, slot):
    rows = []
    for i in range(4):
        index = jnp.maximum(block + i, 0)
        rows.append(r_ref[index & 15, (index >> 4) * 2 + slot])
    return jnp.concatenate(rows, 0)


def masked(values, a, block, lo_a, lo_b, diagonal, fill):
    key_row = lax.broadcasted_iota(jnp.int32, (128, 256), 0)
    causal = key_row <= lax.broadcasted_iota(jnp.int32, (128, 256), 1) % 128
    rows = []
    for k in range(4):
        parts = []
        for i, lo in enumerate((lo_a, lo_b)):
            mask = block + k >= lo
            if diagonal and k == 2 + i:
                mask = causal
            part = values[k * 128 : k * 128 + 128, i * 256 : i * 256 + 256]
            if diagonal and k == 3 and i == 0:
                parts.append(jnp.full((128, 256), fill, jnp.float32))
            else:
                parts.append(jnp.where(mask, part, fill))
        rows.append(jnp.concatenate(parts, 1))
    return jnp.concatenate(rows, 0)


def attend_kernel(lo_ref, r_ref, o32_ref, o16_ref, lse_ref):
    def one_pair(a, _):
        lo_a, lo_b = lo_ref[2 * a], lo_ref[2 * a + 1]
        queries = stack_heads(r_ref, (2 * a, 4), (2 * a + 1, 4))

        def scores(block, diagonal):
            values = mm(key_blocks(r_ref, block, 0), queries, 1, 1)
            return masked(values, a, block, lo_a, lo_b, diagonal, masked_score)

        def add(scores, block, top):
            weights = jnp.exp(scores - top)
            sums = mm(key_blocks(r_ref, block, 1), weights.astype(jnp.bfloat16), 0, 0)
            return jnp.sum(weights, 0, keepdims=True), sums

        diagonal = scores(2 * a + 14, True)
        top = jnp.max(diagonal, 0, keepdims=True)
        total, sums = add(diagonal, 2 * a + 14, top)

        def earlier(i, carry):
            top, total, sums = carry
            block = 2 * a + 14 - 4 * i
            values = scores(block, False)
            new = jnp.maximum(top, jnp.max(values, 0, keepdims=True))
            scale = jnp.exp(top - new)
            more, more_sums = add(values, block, new)
            return new, total * scale + more, sums * scale + more_sums

        steps = (2 * a + 21 - lo_a) // 4
        top, total, sums = lax.fori_loop(1, steps, earlier, (top, total, sums))
        out = jnp.transpose(sums / total)
        for block in range(2):
            rows = unstack_heads(out, block)
            o32_ref[2 * a + block] = rows
            o16_ref[2 * a + block] = rows.astype(jnp.bfloat16)
        lse_ref[a] = top + jnp.log(total)
        return 0

    lax.fori_loop(0, 8, one_pair, 0)


def attend_call(lo, blocks):
    vmem = pl.BlockSpec(memory_space=pltpu.VMEM)
    return pl.pallas_call(
        attend_kernel,
        in_specs=[pl.BlockSpec(memory_space=pltpu.SMEM), vmem],
        out_specs=[vmem, vmem, vmem],
        out_shape=[
            jax.ShapeDtypeStruct((16, 128, 128), jnp.float32),
            jax.ShapeDtypeStruct((16, 128, 128), jnp.bfloat16),
            jax.ShapeDtypeStruct((8, 1, 512), jnp.float32),
        ],
        compiler_params=pltpu.CompilerParams(vmem_limit_bytes=VMEM_LIMIT),
        cost_estimate=TINY,
    )(lo, blocks)


def attend_back_kernel(lo_ref, r_ref, do_ref, o32_ref, lse_ref, out_ref, dk_ref, dv_ref):
    dk_ref[...] = jnp.zeros_like(dk_ref)
    dv_ref[...] = jnp.zeros_like(dv_ref)

    def one_pair(a, _):
        lo_a, lo_b = lo_ref[2 * a], lo_ref[2 * a + 1]
        queries = stack_heads(r_ref, (2 * a, 4), (2 * a + 1, 4))
        grads = stack_heads(do_ref, 2 * a, 2 * a + 1)
        out = jnp.concatenate([o32_ref[2 * a]] * 2 + [o32_ref[2 * a + 1]] * 2, 0)
        delta = jnp.sum(jnp.transpose(grads.astype(jnp.float32) * out), 0, keepdims=True)
        lse = lse_ref[a]

        def blocks_back(block, diagonal):
            keys, values = key_blocks(r_ref, block, 0), key_blocks(r_ref, block, 1)
            weights = jnp.exp(mm(keys, queries, 1, 1) - lse)
            weights = masked(weights, a, block, lo_a, lo_b, diagonal, 0.0)
            grad_scores = (weights * (mm(values, grads, 1, 1) - delta)).astype(jnp.bfloat16)
            grad_values = mm(weights.astype(jnp.bfloat16), grads)
            grad_keys = mm(grad_scores, queries)
            for k in range(4):
                index, rows = jnp.maximum(block + k, 0), slice(k * 128, k * 128 + 128)
                dv_ref[index] += grad_values[rows]
                dk_ref[index] += grad_keys[rows]
            return mm(grad_scores, keys, 0, 0)

        def earlier(i, grad_query):
            return grad_query + blocks_back(2 * a + 14 - 4 * i, False)

        steps = (2 * a + 21 - lo_a) // 4
        grad_query = blocks_back(2 * a + 14, True)
        grad_query = lax.fori_loop(1, steps, earlier, grad_query)
        for block in range(2):
            rows = unstack_heads(grad_query, block) * score_scale
            out_ref[2 * a + block, 4] = rows.astype(jnp.bfloat16)
        return 0

    lax.fori_loop(0, 8, one_pair, 0)

    def finish(c, _):
        out_ref[c, 0] = dk_ref[c].astype(jnp.bfloat16)
        out_ref[c, 1] = dv_ref[c].astype(jnp.bfloat16)
        out_ref[c, 2] = dk_ref[c + 16].astype(jnp.bfloat16)
        out_ref[c, 3] = dv_ref[c + 16].astype(jnp.bfloat16)
        return 0

    lax.fori_loop(0, 16, finish, 0)


def attend_back_call(lo, blocks, grads, out, lse):
    vmem = pl.BlockSpec(memory_space=pltpu.VMEM)
    return pl.pallas_call(
        attend_back_kernel,
        in_specs=[pl.BlockSpec(memory_space=pltpu.SMEM), vmem, vmem, vmem, vmem],
        out_specs=vmem,
        out_shape=jax.ShapeDtypeStruct((16, 5, 128, 128), jnp.bfloat16),
        scratch_shapes=[
            pltpu.VMEM((32, 128, 128), jnp.float32),
            pltpu.VMEM((32, 128, 128), jnp.float32),
        ],
        compiler_params=pltpu.CompilerParams(vmem_limit_bytes=VMEM_LIMIT),
        cost_estimate=TINY,
    )(lo, blocks, grads, out, lse)


def turn_back_kernel(r_ref, halo_ref, cos_ref, up_ref, down_ref, out_ref, bias_ref):
    for j in range(2):
        sums = [jnp.zeros((1, 128), jnp.float32) for _ in range(3)]
        for x in range(4):
            rows = slice(x * 128, (x + 1) * 128)

            def turned(grad):
                return (
                    grad * cos_ref[rows]
                    - pltpu.roll(grad, 120, 1) * up_ref[rows]
                    - pltpu.roll(grad, 8, 1) * down_ref[rows]
                )

            def read(slot):
                later = r_ref[x + 1, j, 0, slot] if x < 3 else halo_ref[j, 0, slot]
                return r_ref[x, j, 0, slot + 2].astype(jnp.float32) + later.astype(jnp.float32)

            parts = (
                turned(r_ref[x, j, 0, 4].astype(jnp.float32)),
                turned(read(0)),
                read(1),
            )
            for part in range(3):
                grad = parts[part].astype(jnp.bfloat16)
                column = (j * 3 + part) * 128
                out_ref[0, rows, column : column + 128] = grad
                sums[part] = sums[part] + jnp.sum(grad.astype(jnp.float32), 0, keepdims=True)
        for part in range(3):
            column = (j * 3 + part) * 128
            bias_ref[0, :, column : column + 128] = sums[part]


def turn_back_call(blocks, halo, tables):
    table = pl.BlockSpec((512, 128), lambda h: (0, 0))
    return pl.pallas_call(
        turn_back_kernel,
        grid=(2,),
        in_specs=[
            pl.BlockSpec((4, 2, 1, 5, 128, 128), lambda h: (0, 0, h, 0, 0, 0)),
            pl.BlockSpec((2, 1, 2, 128, 128), lambda h: (0, h, 0, 0, 0)),
            table,
            table,
            table,
        ],
        out_specs=[
            pl.BlockSpec((1, 512, 768), lambda h: (h, 0, 0)),
            pl.BlockSpec((1, 1, 768), lambda h: (h, 0, 0)),
        ],
        out_shape=[
            jax.ShapeDtypeStruct((2, 512, 768), jnp.bfloat16),
            jax.ShapeDtypeStruct((2, 1, 768), jnp.float32),
        ],
        compiler_params=pltpu.CompilerParams(vmem_limit_bytes=VMEM_LIMIT),
        cost_estimate=TINY,
    )(blocks, halo, *tables)


def normed_back_kernel(g_ref, unit_ref, w_ref, out_ref, gain_grad_ref, shift_grad_ref):
    grads = jnp.concatenate([g_ref[0], g_ref[1]], 1)
    weights = jnp.concatenate(
        [
            w_ref[0, h, :, :128, j * 512 : j * 512 + 384].reshape(512, 384)
            for h in range(2)
            for j in range(2)
        ],
        1,
    )
    total = mm(grads, weights, 1, 1)
    out_ref[...] = total.astype(jnp.bfloat16).reshape(4, 128, 512)
    unit = unit_ref[...].reshape(512, 512).astype(jnp.float32)
    gain_grad_ref[...] = jnp.sum(total * unit, 0, keepdims=True)
    shift_grad_ref[...] = jnp.sum(total, 0, keepdims=True)


def normed_back_call(grad_joint, unit, weights):
    ring = pl.BlockSpec((4, 128, 512), lambda n: (0, 0, n))
    vector = pl.BlockSpec((1, 512), lambda n: (0, n))
    return pl.pallas_call(
        normed_back_kernel,
        grid=(4,),
        in_specs=[
            pl.BlockSpec((2, 512, 768), lambda n: (0, 0, 0)),
            ring,
            pl.BlockSpec((1, 2, 4, 144, 1024), lambda n: (n, 0, 0, 0, 0)),
        ],
        out_specs=[ring, vector, vector],
        out_shape=[
            jax.ShapeDtypeStruct((4, 128, D), jnp.bfloat16),
            jax.ShapeDtypeStruct((1, D), jnp.float32),
            jax.ShapeDtypeStruct((1, D), jnp.float32),
        ],
        compiler_params=pltpu.CompilerParams(vmem_limit_bytes=VMEM_LIMIT),
        cost_estimate=TINY,
    )(grad_joint, unit, weights)


def local(
    tokens,
    cotangent,
    doc_ids,
    ln1_gain,
    ln1_shift,
    w_qkv,
    b_qkv,
    w_out,
    ln2_gain,
    ln2_shift,
    w_gate,
    w_up,
    w_down,
):
    half = lax.axis_index("yh")
    blk = lax.axis_index(BLK)

    core = lax.axis_index("k").reshape(1)
    vectors = jnp.stack([ln1_gain, ln1_shift, ln2_gain, ln2_shift])
    joint_w = pack_joint_call(w_qkv.transpose(1, 0, 2), w_out, vectors, b_qkv)
    joint_w = lax.all_gather(joint_w, PLANE, axis=0).reshape(4, 2, 4, 144, 1024)
    ring = ring_gather(tokens)
    place = jnp.stack([lax.axis_index("x"), lax.axis_index("k")]).astype(jnp.int32)
    before = lax.ppermute(ring[3], ("yh",), [(0, 1)])
    ring_cot = lax.all_gather(after(cotangent, ring), "x", axis=0)
    rest = pack_hidden_call(w_gate.T, w_up.T, w_down)

    small = joint_w[:, :, :, 128:, :128].astype(jnp.float32)
    bias = small[:, :, :, 8:11, :16].transpose(1, 3, 0, 2, 4).reshape(2, 3, 1, 256)
    vectors = small[:, 0, :, :4].transpose(2, 0, 1, 3).reshape(4, D)
    gain_one, shift_one, gain_two, shift_two = [vectors[i : i + 1] for i in range(4)]

    first_block = jnp.sum((doc_ids[None, :] < doc_ids[:, None]).astype(jnp.int32), axis=1)
    cycles = jnp.arange(4, dtype=jnp.int32) * 16 + half * 64 + blk
    cycles = jnp.concatenate([cycles, 48 + blk.reshape(1)])
    block_position = (cycles - first_block[cycles]) * BLK_TOK
    positions = (block_position[:, None] + jnp.arange(BLK_TOK, dtype=jnp.int32)).reshape(640)
    tables = rotary_tables(positions)
    first_query = half * 64 + (blk // 4) * 16
    lo = lax.dynamic_slice(first_block, (first_query,), (16,)) - (first_query - 16)

    payload, normed_one, unit_one = qkv_call(
        ring, before, gain_one, shift_one, joint_w, bias, tables
    )
    out_w, payload = lax.optimization_barrier((joint_w, payload))
    own_rows = out_rows_call(place, out_w)
    near_rows = [send(own_rows, ("x",), t) for t in (1, 3)]
    blocks = after(exchange(payload.reshape(16, 5, 128, 128), BLK), near_rows)
    rest = lax.all_gather(after(rest, blocks), PLANE, axis=0).reshape(4, 2, 512, 3 * HID_PAD)
    att32, att16, lse = attend_call(lo, blocks)
    far_rows = send(after(own_rows, blocks), ("x",), 2)
    attended = exchange(att16, BLK).reshape(4, 2, 2, 128, 128)
    own_rows = [own_rows, near_rows[0], after(far_rows, attended), near_rows[1]]
    other_rows = [swap_core(rows) for rows in own_rows]
    middle, normed_two = project_call(
        place, exchange(attended, ("x",)), tokens, gain_two, shift_two, own_rows, other_rows
    )

    ring_two = exchange(normed_two, ("x",))
    active, grad_gu, ring_grad, ring_out = feed_forward_call(ring_two, ring_cot, rest)
    shared = plane_grad_call(core, with_other(ring_cot), with_other(active), HID_PAD, 2 * HID_PAD)
    came = after(exchange(ring_grad, ("x",)), shared)
    grad_middle, grad_branch, grad_gain_two, grad_shift_two, grad_att = project_back_call(
        place, came, middle, cotangent, gain_two, own_rows, other_rows
    )
    grad_att = exchange(grad_att, ("x",))
    ring_branch = lax.all_gather(after(grad_branch, grad_att), "x", axis=0)
    shared = plane_grad_call(core, with_other(ring_two), with_other(grad_gu), 2 * HID_PAD, 0, shared)
    grad_att = after(exchange(grad_att.reshape(16, 128, 128), BLK), shared)
    attended_pair = with_other(attended.transpose(2, 0, 3, 1, 4).reshape(2, 512, 256))

    mixed = lax.psum_scatter(
        after(ring_out, grad_att).reshape(512, D), "x", scatter_dimension=0, tiled=True
    )
    back = attend_back_call(lo, blocks, grad_att, att32, lse)
    branch_pair = with_other(after(ring_branch, back))
    shared = plane_grad_call(core, branch_pair, attended_pair, 256, 3 * HID_PAD, shared)
    back = exchange(back, BLK).reshape(4, 2, 2, 5, 128, 128)
    back, shared = lax.optimization_barrier((back, shared))
    shared = plane_sum(shared)
    mixed = (middle + after(mixed, back).astype(jnp.float32)).astype(jnp.bfloat16)
    halo_back = lax.ppermute(back[0, :, :, :2], ("yh",), [(1, 0)])
    back = after(back, mixed)
    grad_joint, grad_bias = turn_back_call(back, halo_back, tables)
    ring_one, grad_gain_one, grad_shift_one = normed_back_call(grad_joint, unit_one, joint_w)
    places = (chip_places(True), chip_places(False))
    parts = joint_grad_call(core, places, with_other(normed_one), with_other(grad_joint))
    pair_came = [first_send(parts[4 * j : 4 * j + 4], j == 0) for j in range(2)]

    norms = jnp.concatenate([grad_gain_one, grad_shift_one, grad_gain_two, grad_shift_two], 0)
    norms = norms.reshape(4, 2, 4, 16, 16).transpose(1, 2, 3, 0, 4).reshape(2, 4, 16, 64)
    biases = grad_bias.reshape(2, 2, 3, 8, 16).transpose(0, 1, 3, 2, 4).reshape(2, 1, 16, 48)
    plane = jnp.arange(4).reshape(1, 4, 1, 1) == lax.axis_index("x")
    biases = jnp.where(plane, biases, 0.0)
    sums = jnp.concatenate([norms, biases, jnp.zeros((2, 4, 16, 16), jnp.float32)], 3)
    sums = jnp.sum(exchange(sums.reshape(128, 128), AXES), 0)
    norms = sums[:64].reshape(4, 16)

    came = exchange(after(ring_one, norms, parts[0]), ("x",))
    input_grad = whole_call(
        input_back_kernel,
        jax.ShapeDtypeStruct((128, D), jnp.float32),
        came,
        tokens,
        grad_middle,
        gain_one,
    )
    pair_came[1] = after(pair_came[1], input_grad)
    pair_came = [second_send(first_sum(part, j == 0), j == 0) for j, part in enumerate(pair_came)]

    def shape(*dims):
        return jax.ShapeDtypeStruct(dims, jnp.float32)

    grad_gate, grad_up, grad_down, grad_out = whole_call(
        shared_end_kernel, [shape(HID, 128)] * 3 + [shape(256, 128)], after(shared, input_grad)
    )
    grad_qkv = whole_call(joint_end_kernel, shape(3, 128, 256), *pair_came[0], *pair_came[1])

    return (
        mixed,
        input_grad,
        norms[0],
        norms[1],
        grad_qkv.transpose(1, 0, 2),
        sums[64:112].reshape(3, 16),
        grad_out,
        norms[2],
        norms[3],
        grad_gate.T,
        grad_up.T,
        grad_down,
    )


def solution(mesh):
    whole = Mesh(mesh.devices.reshape(2, 4, 4, 2, 2), AXES)
    ulysses, blk = ("yh", "x"), BLK
    both = ulysses + blk
    placed = (
        P(both, None),
        P(both, None),
        P(),
        P(blk),
        P(blk),
        P(blk, None, ulysses),
        P(None, both),
        P(ulysses, blk),
        P(blk),
        P(blk),
        P(blk, ulysses),
        P(blk, ulysses),
        P(ulysses, blk),
    )
    return jax.shard_map(
        local,
        mesh=whole,
        in_specs=placed,
        out_specs=(
            P(both, None),
            P(both, None),
            P(both),
            P(both),
            P(blk, None, ulysses),
            P(None, both),
            P(ulysses, blk),
            P(both),
            P(both),
            P(blk, ulysses),
            P(blk, ulysses),
            P(ulysses, blk),
        ),
        check_vma=False,
    )
```

```python
import functools

import jax
import jax.numpy as jnp
from jax import lax
from jax.experimental import pallas as pl
from jax.experimental.pallas import tpu as pltpu
from jax.sharding import Mesh
from jax.sharding import PartitionSpec as P

D = 2048
HEADS = 32
HEAD_DIM = 64
ROT = 16
BLK_TOK = 128
HID = 704
HID_PAD = 768
SHARED = 3 * HID_PAD + 256

eps = 1e-05
rope_base = 10000.0
masked_score = -1e30
score_scale = HEAD_DIM ** (-0.5)

AXES = ("yh", "x", "z", "yl", "k")
PLANE = ("z", "yh", "yl", "k")
BLK = ("z", "yl", "k")
Y = ("yh", "yl")

VMEM_LIMIT = 60 * 1024 * 1024
TINY = pl.CostEstimate(flops=1, bytes_accessed=1, transcendentals=0)


def mm(a, b, ca=1, cb=0):
    return lax.dot_general(a, b, (((ca,), (cb,)), ((), ())), preferred_element_type=jnp.float32)


def swap_core(value):
    return lax.ppermute(value, ("k",), [(0, 1), (1, 0)])


def exchange(parts, axes):
    return lax.all_to_all(parts, axes, 0, 0, tiled=True)


def send(value, axes, step):
    return lax.ppermute(value, axes, [(i, (i + step) % 4) for i in range(4)])


def ring_gather(value):
    return exchange(jnp.broadcast_to(value, (4,) + value.shape), ("x",))


def send(value, axes, step):
    return lax.ppermute(value, axes, [(i, (i + step) % 4) for i in range(4)])


def gather(value, axes, *others):
    me = lax.axis_index(axes)
    pieces = [send(value, axes, step) for step in (1, 3, 2)]
    if others:
        pieces = after(pieces, *others)
    buffer = jnp.zeros((4,) + value.shape, value.dtype)
    for step, piece in zip((0, 1, 3, 2), [value] + pieces):
        buffer = lax.dynamic_update_index_in_dim(buffer, piece, (me - step) % 4, 0)
    return buffer


def ring_gather(value):
    return exchange(jnp.broadcast_to(value, (4,) + value.shape), ("x",))


def after(value, *others):
    return lax.optimization_barrier((value,) + others)[0]


def rotary_tables(positions):
    halfway = ROT // 2
    counter = jnp.arange(halfway, dtype=jnp.float32)
    frequency = rope_base ** (-2.0 * counter / ROT)
    lane = jnp.arange(128) % HEAD_DIM
    frequency = jnp.where(lane < ROT, jnp.tile(frequency, 16), 0.0)
    angles = positions.astype(jnp.float32)[:, None] * frequency[None, :]
    sine = jnp.sin(angles)
    return (
        jnp.cos(angles),
        jnp.where(lane < halfway, -sine, 0.0),
        jnp.where((lane >= halfway) & (lane < ROT), sine, 0.0),
    )


def pack_joint_kernel(qkv_ref, out_ref, vectors_ref, bias_ref, w_ref, small_ref):
    out_t = jnp.transpose(out_ref[...])
    for j in range(2):
        pair = slice(j * 128, (j + 1) * 128)
        for part in range(3):
            column = j * 512 + part * 128
            w_ref[:128, column : column + 128] = qkv_ref[part, :, pair]
        w_ref[:128, j * 512 + 384 : j * 512 + 512] = out_t[:, pair]
    small_ref[...] = jnp.zeros_like(small_ref)
    small_ref[0:4, :128] = vectors_ref[...].astype(jnp.float32)
    small_ref[8:11, :16] = bias_ref[...].astype(jnp.float32)
    w_ref[128:, :] = small_ref[...].astype(jnp.bfloat16)


def pack_joint_call(qkv, out, vectors, bias):
    return whole_call(
        pack_joint_kernel,
        jax.ShapeDtypeStruct((144, 1024), jnp.bfloat16),
        qkv,
        out,
        vectors,
        bias,
        scratch=[pltpu.VMEM((16, 1024), jnp.float32)],
    )


def pack_hidden_kernel(gate_ref, up_ref, down_ref, rest_ref):
    for i, ref in enumerate((gate_ref, up_ref, down_ref)):
        first = i * HID_PAD
        rest_ref[:, first + HID_PAD - 128 : first + HID_PAD] = jnp.zeros((128, 128), jnp.bfloat16)
        rest_ref[:, first : first + HID] = jnp.transpose(ref[...])


def pack_hidden_call(gate, up, down):
    return whole_call(
        pack_hidden_kernel, jax.ShapeDtypeStruct((128, 3 * HID_PAD), jnp.bfloat16), gate, up, down
    )


def core_columns(ref, core, blocks):
    columns = [ref[:blocks, :, pl.ds(pl.multiple_of((2 * i + core) * 128, 128), 128)] for i in range(8)]
    return jnp.concatenate(columns, 2).reshape(blocks * 128, 1024)


def normalise(values):
    centred = values - jnp.mean(values, -1, keepdims=True)
    inverse = lax.rsqrt(jnp.mean(centred * centred, -1, keepdims=True) + eps)
    return centred * inverse, inverse


def unit_kernel(x_ref, before_ref, out_ref):
    block = jnp.where(pl.program_id(0) < 4, x_ref[0], before_ref[...])
    out_ref[0] = normalise(block.astype(jnp.float32))[0].astype(jnp.bfloat16)


def unit_call(ring, before):
    return pl.pallas_call(
        unit_kernel,
        grid=(5,),
        in_specs=[
            pl.BlockSpec((1, 128, D), lambda b: (jnp.minimum(b, 3), 0, 0)),
            pl.BlockSpec((128, D), lambda b: (0, 0)),
        ],
        out_specs=pl.BlockSpec((1, 128, D), lambda b: (b, 0, 0)),
        out_shape=jax.ShapeDtypeStruct((5, 128, D), jnp.bfloat16),
        compiler_params=pltpu.CompilerParams(vmem_limit_bytes=VMEM_LIMIT),
        cost_estimate=TINY,
    )(ring, before)


def qkv_kernel(
    unit_ref,
    gain_ref,
    shift_ref,
    w0_ref,
    w1_ref,
    bias_ref,
    cos_ref,
    up_ref,
    down_ref,
    out_ref,
    normed_ref,
    normed_rows,
):
    part = pl.program_id(1)

    @pl.when((pl.program_id(0) == 0) & (part == 0))
    def _():
        for b in range(5):
            normed = unit_ref[b].astype(jnp.float32) * gain_ref[...] + shift_ref[...]
            normed = normed.astype(jnp.bfloat16)
            if b < 4:
                normed_ref[b] = normed
            normed_rows[b * 128 : (b + 1) * 128] = normed

    def joint(rows):
        weights = [ref[:, 0, :, :128, :].reshape(D, 128) for ref in (w0_ref, w1_ref)]
        return mm(normed_rows[:rows], jnp.concatenate(weights, 1)) + bias_ref[0, 0]

    def turned(value):
        rows = value.shape[0]
        return (
            value * cos_ref[:rows]
            + pltpu.roll(value, 120, 1) * up_ref[:rows]
            + pltpu.roll(value, 8, 1) * down_ref[:rows]
        )

    @pl.when(part == 0)
    def _():
        value = joint(512)
        for j in range(2):
            query = turned(value[:, j * 128 : (j + 1) * 128]) * score_scale
            out_ref[:, j, 0, 4] = query.astype(jnp.bfloat16).reshape(4, 128, 128)

    @pl.when(part > 0)
    def _():
        value = joint(640)
        for j in range(2):
            block = value[:, j * 128 : (j + 1) * 128]
            block = jnp.where(part == 1, turned(block), block)
            block = block.astype(jnp.bfloat16).reshape(5, 128, 128)

            @pl.when(part == 1)
            def _():
                out_ref[:, j, 0, 2] = block[:4]
                out_ref[1:, j, 0, 0] = block[:3]
                out_ref[0, j, 0, 0] = block[4]

            @pl.when(part == 2)
            def _():
                out_ref[:, j, 0, 3] = block[:4]
                out_ref[1:, j, 0, 1] = block[:3]
                out_ref[0, j, 0, 1] = block[4]


def qkv_call(unit, gain, shift, weights, bias, tables):
    table = pl.BlockSpec((640, 128), lambda h, p: (0, 0))
    vector = pl.BlockSpec((1, D), lambda h, p: (0, 0))
    return pl.pallas_call(
        qkv_kernel,
        grid=(2, 3),
        in_specs=[
            pl.BlockSpec((5, 128, D), lambda h, p: (0, 0, 0)),
            vector,
            vector,
            pl.BlockSpec((4, 1, 4, 144, 128), lambda h, p: (0, h, 0, 0, p)),
            pl.BlockSpec((4, 1, 4, 144, 128), lambda h, p: (0, h, 0, 0, p + 4)),
            pl.BlockSpec((1, 1, 1, 256), lambda h, p: (h, p, 0, 0)),
            table,
            table,
            table,
        ],
        out_specs=[
            pl.BlockSpec((4, 2, 1, 5, 128, 128), lambda h, p: (0, 0, h, 0, 0, 0)),
            pl.BlockSpec((4, 128, D), lambda h, p: (0, 0, 0)),
        ],
        out_shape=[
            jax.ShapeDtypeStruct((4, 2, 2, 5, 128, 128), jnp.bfloat16),
            jax.ShapeDtypeStruct((4, 128, D), jnp.bfloat16),
        ],
        scratch_shapes=[pltpu.VMEM((640, D), jnp.bfloat16)],
        compiler_params=pltpu.CompilerParams(vmem_limit_bytes=VMEM_LIMIT),
        cost_estimate=TINY,
    )(unit, gain, shift, weights, weights, bias, *tables)


def whole_call(kernel, out_shape, *operands, scratch=()):
    vmem = pl.BlockSpec(memory_space=pltpu.VMEM)
    return pl.pallas_call(
        kernel,
        in_specs=[vmem] * len(operands),
        out_specs=jax.tree.map(lambda _: vmem, out_shape),
        out_shape=out_shape,
        scratch_shapes=list(scratch),
        compiler_params=pltpu.CompilerParams(vmem_limit_bytes=VMEM_LIMIT),
        cost_estimate=TINY,
    )(*operands)


def back_through(came_ref, values, gain):
    grad = came_ref[0].astype(jnp.float32)
    for i in range(1, 4):
        grad = grad + came_ref[i].astype(jnp.float32)
    unit, inverse = normalise(values)
    grad_unit = grad * gain
    centred_grad = (
        grad_unit
        - jnp.mean(grad_unit, -1, keepdims=True)
        - unit * jnp.mean(grad_unit * unit, -1, keepdims=True)
    )
    gain_grad = jnp.sum(grad * unit, 0, keepdims=True)
    return inverse * centred_grad, gain_grad, jnp.sum(grad, 0, keepdims=True)


def input_back_kernel(came_ref, tokens_ref, grad_ref, gain_ref, out_ref):
    values = tokens_ref[...].astype(jnp.float32)
    out_ref[...] = grad_ref[...] + back_through(came_ref, values, gain_ref[...])[0]


def shared_end_kernel(total_ref, gate_ref, up_ref, down_ref, out_ref):
    total = jnp.transpose(total_ref[...].astype(jnp.float32))
    for c in range(3):
        width = min(HID, c * 256 + 256) - c * 256
        gate_ref[c * 256 : c * 256 + width] = total[c * 512 : c * 512 + width]
        up_ref[c * 256 : c * 256 + width] = total[c * 512 + 256 : c * 512 + 256 + width]
    down_ref[...] = total[2 * HID_PAD : 2 * HID_PAD + HID]
    out_ref[...] = total[3 * HID_PAD :]


def joint_end_kernel(*refs):
    for j in range(2):
        total = sum(ref[...].astype(jnp.float32) for ref in refs[4 * j : 4 * j + 4])
        for part in range(3):
            refs[8][part, :, j * 128 : (j + 1) * 128] = total[:, part * 128 : part * 128 + 128]


def out_rows_kernel(place_ref, w0_ref, w1_ref, out_ref):
    for yl in range(2):
        for h in range(2):
            for j, ref in enumerate((w0_ref, w1_ref)):
                column = h * 256 + j * 128
                out_ref[yl, :, column : column + 128] = ref[0, h, 2 * yl + place_ref[1], :128]


def out_rows_call(place, weights):
    return pl.pallas_call(
        out_rows_kernel,
        grid=(4,),
        in_specs=[
            pl.BlockSpec(memory_space=pltpu.SMEM),
            pl.BlockSpec((1, 2, 4, 144, 128), lambda n: (n, 0, 0, 0, 3)),
            pl.BlockSpec((1, 2, 4, 144, 128), lambda n: (n, 0, 0, 0, 7)),
        ],
        out_specs=pl.BlockSpec((2, 128, 512), lambda n: (n, 0, 0)),
        out_shape=jax.ShapeDtypeStruct((8, 128, 512), jnp.bfloat16),
        compiler_params=pltpu.CompilerParams(vmem_limit_bytes=VMEM_LIMIT),
        cost_estimate=TINY,
    )(place, weights, weights)


def planes_columns(refs, yl):
    return jnp.concatenate([ref[yl] for ref in refs], 1)


def project_kernel(place_ref, att_ref, tokens_ref, gain_ref, shift_ref, *refs):
    own_refs, other_refs, (middle_ref, normed_ref, att_cols, total) = refs[:4], refs[4:8], refs[8:]
    n, me, core = pl.program_id(0), place_ref[0], place_ref[1]

    @pl.when(n == 0)
    def _():
        for t in range(4):
            x = (me + 4 - t) % 4
            for h in range(2):
                for j in range(2):
                    column = t * 512 + h * 256 + j * 128
                    att_cols[:, column : column + 128] = att_ref[x, j, h]

    weights = jnp.concatenate(
        [planes_columns(refs, yl) for refs in (own_refs, other_refs) for yl in range(2)], 0
    )
    values = mm(att_cols[...], weights, 1, 1)
    for i in range(4):
        holder = core if i < 2 else 1 - core
        column = pl.multiple_of((n * 4 + i % 2 * 2 + holder) * 128, 128)
        total[:, pl.ds(column, 128)] = values[:, i * 128 : i * 128 + 128]

    @pl.when(n == 3)
    def _():
        middle = tokens_ref[...].astype(jnp.float32) + total[...]
        middle_ref[...] = middle
        normed = (normalise(middle)[0] * gain_ref[...] + shift_ref[...]).astype(jnp.bfloat16)
        for i in range(4):
            normed_ref[i] = normed


def project_call(place, att, tokens, gain, shift, own, other):
    def whole(*dims):
        return pl.BlockSpec(dims, lambda n: (0,) * len(dims))

    rows = pl.BlockSpec((2, 128, 512), lambda n: (n, 0, 0))
    return pl.pallas_call(
        project_kernel,
        grid=(4,),
        in_specs=[
            pl.BlockSpec(memory_space=pltpu.SMEM),
            whole(4, 2, 2, 128, 128),
            whole(128, D),
            whole(1, D),
            whole(1, D),
        ]
        + [rows] * 8,
        out_specs=[whole(128, D), whole(4, 128, D)],
        out_shape=[
            jax.ShapeDtypeStruct((128, D), jnp.float32),
            jax.ShapeDtypeStruct((4, 128, D), jnp.bfloat16),
        ],
        scratch_shapes=[pltpu.VMEM((128, D), jnp.bfloat16), pltpu.VMEM((128, D), jnp.float32)],
        compiler_params=pltpu.CompilerParams(vmem_limit_bytes=VMEM_LIMIT),
        cost_estimate=TINY,
    )(place, att, tokens, gain, shift, *own, *other)


def project_back_kernel(place_ref, came_ref, middle_ref, cot_ref, gain_ref, *refs):
    own_refs, other_refs = refs[:4], refs[4:8]
    grad_ref, low_ref, gain_grad_ref, shift_grad_ref, out_ref, low, total = refs[8:]
    n, me, core = pl.program_id(0), place_ref[0], place_ref[1]

    @pl.when(n == 0)
    def _():
        grad, gain_grad_ref[...], shift_grad_ref[...] = back_through(came_ref, middle_ref[...], gain_ref[...])
        grad = grad + cot_ref[...].astype(jnp.float32)
        grad_ref[...] = grad
        low[...] = grad.astype(jnp.bfloat16)
        low_ref[...] = low[...]
        total[...] = jnp.zeros_like(total)

    columns = []
    for i in range(4):
        holder = core if i < 2 else 1 - core
        column = pl.multiple_of((n * 4 + i % 2 * 2 + holder) * 128, 128)
        columns.append(low[:, pl.ds(column, 128)])
    weights = jnp.concatenate(
        [planes_columns(refs, yl) for refs in (own_refs, other_refs) for yl in range(2)], 0
    )
    total[...] += mm(jnp.concatenate(columns, 1), weights)

    @pl.when(n == 3)
    def _():
        for t in range(4):
            x = (me + 4 - t) % 4
            for h in range(2):
                for j in range(2):
                    column = t * 512 + h * 256 + j * 128
                    out_ref[x, j, h] = total[:, column : column + 128].astype(jnp.bfloat16)


def project_back_call(place, came, middle, cot, gain, own, other):
    def whole(*dims):
        return pl.BlockSpec(dims, lambda n: (0,) * len(dims))

    rows = pl.BlockSpec((2, 128, 512), lambda n: (n, 0, 0))
    return pl.pallas_call(
        project_back_kernel,
        grid=(4,),
        in_specs=[
            pl.BlockSpec(memory_space=pltpu.SMEM),
            whole(4, 128, D),
            whole(128, D),
            whole(128, D),
            whole(1, D),
        ]
        + [rows] * 8,
        out_specs=[whole(128, D), whole(128, D), whole(1, D), whole(1, D), whole(4, 2, 2, 128, 128)],
        out_shape=[
            jax.ShapeDtypeStruct((128, D), jnp.float32),
            jax.ShapeDtypeStruct((128, D), jnp.bfloat16),
            jax.ShapeDtypeStruct((1, D), jnp.float32),
            jax.ShapeDtypeStruct((1, D), jnp.float32),
            jax.ShapeDtypeStruct((4, 2, 2, 128, 128), jnp.bfloat16),
        ],
        scratch_shapes=[pltpu.VMEM((128, D), jnp.bfloat16), pltpu.VMEM((128, D), jnp.float32)],
        compiler_params=pltpu.CompilerParams(vmem_limit_bytes=VMEM_LIMIT),
        cost_estimate=TINY,
    )(place, came, middle, cot, gain, *own, *other)


def feed_forward_kernel(
    x_ref, cot_ref, gate_ref, up_ref, down_ref, active_ref, grads_ref, back_ref, out_ref, back_sum, out_sum
):
    first_half = pl.program_id(0) == 0
    x = x_ref[...].reshape(512, D)
    cot = cot_ref[...].reshape(512, D)
    for c in range(3):
        columns = slice(c * 256, c * 256 + 256)
        gate = mm(x, gate_ref[:, 0, :, columns].reshape(D, 256))
        up = mm(x, up_ref[:, 0, :, columns].reshape(D, 256))
        grad_active = mm(cot, down_ref[:, 0, :, columns].reshape(D, 256))
        sigmoid = jax.nn.sigmoid(gate)
        silu = gate * sigmoid
        active_ref[0, :, columns] = (silu * up).astype(jnp.bfloat16)
        grad_gate = grad_active * up * (sigmoid + silu * (1.0 - sigmoid))
        grads_ref[0, :, c * 512 : c * 512 + 256] = grad_gate.astype(jnp.bfloat16)
        grads_ref[0, :, c * 512 + 256 : c * 512 + 512] = (grad_active * silu).astype(jnp.bfloat16)
    for n in range(4):
        rows = slice(n * 512, n * 512 + 512)
        weights = jnp.concatenate(
            [ref[n, 0, :, c * 256 : c * 256 + 256] for c in range(3) for ref in (gate_ref, up_ref)], 1
        )
        back = mm(grads_ref[0], weights, 1, 1)
        out = mm(active_ref[0], down_ref[n, 0], 1, 1)

        @pl.when(first_half)
        def _():
            back_sum[:, rows] = back
            out_sum[:, rows] = out

        @pl.when(~first_half)
        def _():
            back_ref[:, :, rows] = (back_sum[:, rows] + back).astype(jnp.bfloat16).reshape(4, 128, 512)
            out_ref[:, :, rows] = (out_sum[:, rows] + out).astype(jnp.bfloat16).reshape(4, 128, 512)


def feed_forward_call(x, ring, rest):
    tokens = pl.BlockSpec((4, 128, D), lambda h: (0, 0, 0))
    tokens_once = pl.BlockSpec((4, 128, D), lambda h: (0, 0, 0), pipeline_mode=pl.Buffered(1))
    weight = [pl.BlockSpec((4, 1, 512, HID_PAD), lambda h, i=i: (0, h, 0, i)) for i in range(3)]
    ring_shape = jax.ShapeDtypeStruct((4, 128, D), jnp.bfloat16)
    return pl.pallas_call(
        feed_forward_kernel,
        grid=(2,),
        in_specs=[tokens_once, tokens_once] + weight,
        out_specs=[
            pl.BlockSpec((1, 512, HID_PAD), lambda h: (h, 0, 0)),
            pl.BlockSpec((1, 512, 2 * HID_PAD), lambda h: (h, 0, 0)),
            tokens,
            tokens,
        ],
        out_shape=[
            jax.ShapeDtypeStruct((2, 512, HID_PAD), jnp.bfloat16),
            jax.ShapeDtypeStruct((2, 512, 2 * HID_PAD), jnp.bfloat16),
            ring_shape,
            ring_shape,
        ],
        scratch_shapes=[pltpu.VMEM((512, D), jnp.float32), pltpu.VMEM((512, D), jnp.float32)],
        compiler_params=pltpu.CompilerParams(vmem_limit_bytes=VMEM_LIMIT),
        cost_estimate=TINY,
    )(x, ring, rest, rest, rest)


def plane_grad_kernel(core_ref, left_ref, left_other_ref, right_ref, right_other_ref, *refs):
    out_ref, left_t = refs[-2:]

    @pl.when((pl.program_id(0) == 0) & (pl.program_id(1) == 0))
    def _():
        left_t[:, :512] = jnp.transpose(core_columns(left_ref, core_ref[0], 4))
        left_t[:, 512:] = jnp.transpose(core_columns(left_other_ref, core_ref[0], 4))

    total = mm(left_t[...], jnp.concatenate([right_ref[0], right_other_ref[0]], 0)).astype(jnp.bfloat16)
    for z in range(4):
        for yl in range(2):
            row = (z * 2 + yl) * 128
            out_ref[0, yl, z] = total[row : row + 128]


def plane_grad_call(core, left, right, columns, first, shared=None):
    left_block = pl.BlockSpec((4, 128, D), lambda n, h: (0, 0, 0))
    right_block = pl.BlockSpec((1, 512, 256), lambda n, h: (h, 0, n))
    extra = [] if shared is None else [shared]
    return pl.pallas_call(
        plane_grad_kernel,
        grid=(columns // 256, 2),
        in_specs=[
            pl.BlockSpec(memory_space=pltpu.SMEM),
            left_block,
            left_block,
            right_block,
            right_block,
        ]
        + [pl.BlockSpec(memory_space=pl.ANY)] * len(extra),
        out_specs=pl.BlockSpec((1, 2, 4, 128, 256), lambda n, h: (h, 0, 0, 0, first // 256 + n)),
        out_shape=jax.ShapeDtypeStruct((2, 2, 4, 128, SHARED), jnp.bfloat16),
        input_output_aliases={5: 0} if extra else {},
        scratch_shapes=[pltpu.VMEM((1024, 1024), jnp.bfloat16)],
        compiler_params=pltpu.CompilerParams(vmem_limit_bytes=VMEM_LIMIT),
        cost_estimate=TINY,
    )(core, *left, *right, *extra)


def own_rows_kernel(place_ref, left_ref, left_other_ref, out_ref):
    out_ref[:, :512] = jnp.transpose(core_columns(left_ref, place_ref[1], 4))
    out_ref[:, 512:] = jnp.transpose(core_columns(left_other_ref, place_ref[1], 4))


def own_rows_call(place, left):
    vmem = pl.BlockSpec(memory_space=pltpu.VMEM)
    return pl.pallas_call(
        own_rows_kernel,
        in_specs=[pl.BlockSpec(memory_space=pltpu.SMEM), vmem, vmem],
        out_specs=vmem,
        out_shape=jax.ShapeDtypeStruct((1024, 1024), jnp.bfloat16),
        compiler_params=pltpu.CompilerParams(vmem_limit_bytes=VMEM_LIMIT),
        cost_estimate=TINY,
    )(place, *left)


def joint_grad_kernel(place_ref, left_ref, right_ref, right_other_ref, *outs):
    h = pl.program_id(0)
    right = jnp.concatenate([right_ref[0], right_other_ref[0]], 0)
    total = mm(left_ref[...], right).astype(jnp.bfloat16)
    for z in range(4):
        for yl in range(2):
            row = (z * 2 + yl) * 128
            chip = (h * 2 + yl) * 4 + z
            for j in range(2):
                step, slot = place_ref[2 * j, chip], place_ref[2 * j + 1, chip]
                for t in range(4):

                    @pl.when(step == t)
                    def _():
                        outs[4 * j + t][slot] = total[row : row + 128, j * 384 : j * 384 + 384]


def joint_grad_call(places, left, right):
    right_block = pl.BlockSpec((1, 512, 768), lambda h: (h, 0, 0))
    return pl.pallas_call(
        joint_grad_kernel,
        grid=(2,),
        in_specs=[
            pl.BlockSpec(memory_space=pltpu.SMEM),
            pl.BlockSpec((1024, 1024), lambda h: (0, 0)),
            right_block,
            right_block,
        ],
        out_specs=[pl.BlockSpec((4, 128, 384), lambda h: (0, 0, 0))] * 8,
        out_shape=[jax.ShapeDtypeStruct((4, 128, 384), jnp.bfloat16)] * 8,
        compiler_params=pltpu.CompilerParams(vmem_limit_bytes=VMEM_LIMIT),
        cost_estimate=TINY,
    )(jnp.concatenate(places, 0), left, *right)


def split_sum_kernel(place_ref, a_ref, b_ref, c_ref, d_ref, *out_refs):
    for t in range(4):
        i = (place_ref[0] + t) % 4
        total = sum(ref[i].astype(jnp.float32) for ref in (a_ref, b_ref, c_ref, d_ref))
        out_refs[t][...] = total.astype(jnp.bfloat16)


def split_sum_call(place, parts):
    columns = parts[0].shape[2]
    width = 256 if columns % 256 == 0 else 384
    return pl.pallas_call(
        split_sum_kernel,
        grid=(columns // width,),
        in_specs=[pl.BlockSpec(memory_space=pltpu.SMEM)]
        + [pl.BlockSpec((4, 128, width), lambda n: (0, 0, n))] * 4,
        out_specs=[pl.BlockSpec((128, width), lambda n: (0, n))] * 4,
        out_shape=[jax.ShapeDtypeStruct((128, columns), jnp.bfloat16)] * 4,
        compiler_params=pltpu.CompilerParams(vmem_limit_bytes=VMEM_LIMIT),
        cost_estimate=TINY,
    )(place, *parts)


def chip_places(y_first):
    y, z = jnp.arange(16, dtype=jnp.int32) // 4, jnp.arange(16, dtype=jnp.int32) % 4
    if y_first:
        return jnp.stack([(y - lax.axis_index(Y)) % 4, z])
    return jnp.stack([(z - lax.axis_index("z")) % 4, y])


def plane_sum(parts):
    parts = parts.reshape(2048, parts.shape[-1])
    return lax.psum_scatter(parts, ("yh", "yl", "z"), scatter_dimension=0, tiled=True)


def with_other(value):
    return value, swap_core(value)


def first_send(parts, y_first):
    axes = Y if y_first else ("z",)
    return [parts[0]] + [send(parts[t], axes, t) for t in (1, 3, 2)]


def first_sum(parts, y_first):
    return split_sum_call(lax.axis_index(("z",) if y_first else Y).reshape(1), parts)


def second_send(parts, y_first):
    axes = ("z",) if y_first else Y
    return [parts[0]] + [send(parts[t], axes, t) for t in (1, 3, 2)]


def stack_heads(ref, *index):
    first = (lax.broadcasted_iota(jnp.int32, (128, 128), 1) < HEAD_DIM).astype(jnp.float32).astype(jnp.bfloat16)
    masks = (first, 1 - first)
    return jnp.concatenate([ref[i] * mask for i in index for mask in masks], 0)


def unstack_heads(values, block):
    low = lax.broadcasted_iota(jnp.int32, (128, 128), 1) < HEAD_DIM
    rows = values[block * 256 : block * 256 + 256]
    return jnp.where(low, rows[:128], rows[128:])


def key_blocks(r_ref, block, slot):
    rows = []
    for i in range(4):
        index = jnp.maximum(block + i, 0)
        rows.append(r_ref[index & 15, (index >> 4) * 2 + slot])
    return jnp.concatenate(rows, 0)


def masked(values, a, block, lo_a, lo_b, diagonal, fill):
    key_row = lax.broadcasted_iota(jnp.int32, (128, 256), 0)
    causal = key_row <= lax.broadcasted_iota(jnp.int32, (128, 256), 1) % 128
    rows = []
    for k in range(4):
        parts = []
        for i, lo in enumerate((lo_a, lo_b)):
            mask = block + k >= lo
            if diagonal and k == 2 + i:
                mask = causal
            part = values[k * 128 : k * 128 + 128, i * 256 : i * 256 + 256]
            if diagonal and k == 3 and i == 0:
                parts.append(jnp.full((128, 256), fill, jnp.float32))
            else:
                parts.append(jnp.where(mask, part, fill))
        rows.append(jnp.concatenate(parts, 1))
    return jnp.concatenate(rows, 0)


def attend_kernel(lo_ref, r_ref, o32_ref, o16_ref, lse_ref):
    def one_pair(a, _):
        lo_a, lo_b = lo_ref[2 * a], lo_ref[2 * a + 1]
        queries = stack_heads(r_ref, (2 * a, 4), (2 * a + 1, 4))

        def scores(block, diagonal):
            values = mm(key_blocks(r_ref, block, 0), queries, 1, 1)
            return masked(values, a, block, lo_a, lo_b, diagonal, masked_score)

        def add(scores, block, top):
            weights = jnp.exp(scores - top)
            sums = mm(key_blocks(r_ref, block, 1), weights.astype(jnp.bfloat16), 0, 0)
            return jnp.sum(weights, 0, keepdims=True), sums

        diagonal = scores(2 * a + 14, True)
        top = jnp.max(diagonal, 0, keepdims=True)
        total, sums = add(diagonal, 2 * a + 14, top)

        def earlier(i, carry):
            top, total, sums = carry
            block = 2 * a + 14 - 4 * i
            values = scores(block, False)
            new = jnp.maximum(top, jnp.max(values, 0, keepdims=True))
            scale = jnp.exp(top - new)
            more, more_sums = add(values, block, new)
            return new, total * scale + more, sums * scale + more_sums

        steps = (2 * a + 21 - lo_a) // 4
        top, total, sums = lax.fori_loop(1, steps, earlier, (top, total, sums))
        out = jnp.transpose(sums / total)
        for block in range(2):
            rows = unstack_heads(out, block)
            o32_ref[2 * a + block] = rows
            o16_ref[2 * a + block] = rows.astype(jnp.bfloat16)
        lse_ref[a] = top + jnp.log(total)
        return 0

    lax.fori_loop(0, 8, one_pair, 0)


def attend_call(lo, blocks):
    vmem = pl.BlockSpec(memory_space=pltpu.VMEM)
    return pl.pallas_call(
        attend_kernel,
        in_specs=[pl.BlockSpec(memory_space=pltpu.SMEM), vmem],
        out_specs=[vmem, vmem, vmem],
        out_shape=[
            jax.ShapeDtypeStruct((16, 128, 128), jnp.float32),
            jax.ShapeDtypeStruct((16, 128, 128), jnp.bfloat16),
            jax.ShapeDtypeStruct((8, 1, 512), jnp.float32),
        ],
        compiler_params=pltpu.CompilerParams(vmem_limit_bytes=VMEM_LIMIT),
        cost_estimate=TINY,
    )(lo, blocks)


def attend_back_kernel(lo_ref, r_ref, do_ref, o32_ref, lse_ref, out_ref, dk_ref, dv_ref):
    dk_ref[...] = jnp.zeros_like(dk_ref)
    dv_ref[...] = jnp.zeros_like(dv_ref)

    def one_pair(a, _):
        lo_a, lo_b = lo_ref[2 * a], lo_ref[2 * a + 1]
        queries = stack_heads(r_ref, (2 * a, 4), (2 * a + 1, 4))
        grads = stack_heads(do_ref, 2 * a, 2 * a + 1)
        out = jnp.concatenate([o32_ref[2 * a]] * 2 + [o32_ref[2 * a + 1]] * 2, 0)
        delta = jnp.sum(jnp.transpose(grads.astype(jnp.float32) * out), 0, keepdims=True)
        lse = lse_ref[a]

        def blocks_back(block, diagonal):
            keys, values = key_blocks(r_ref, block, 0), key_blocks(r_ref, block, 1)
            weights = jnp.exp(mm(keys, queries, 1, 1) - lse)
            weights = masked(weights, a, block, lo_a, lo_b, diagonal, 0.0)
            grad_scores = (weights * (mm(values, grads, 1, 1) - delta)).astype(jnp.bfloat16)
            grad_values = mm(weights.astype(jnp.bfloat16), grads)
            grad_keys = mm(grad_scores, queries)
            for k in range(4):
                index, rows = jnp.maximum(block + k, 0), slice(k * 128, k * 128 + 128)
                dv_ref[index] += grad_values[rows]
                dk_ref[index] += grad_keys[rows]
            return mm(grad_scores, keys, 0, 0)

        def earlier(i, grad_query):
            return grad_query + blocks_back(2 * a + 14 - 4 * i, False)

        steps = (2 * a + 21 - lo_a) // 4
        grad_query = blocks_back(2 * a + 14, True)
        grad_query = lax.fori_loop(1, steps, earlier, grad_query)
        for block in range(2):
            rows = unstack_heads(grad_query, block) * score_scale
            out_ref[2 * a + block, 4] = rows.astype(jnp.bfloat16)
        return 0

    lax.fori_loop(0, 8, one_pair, 0)

    def finish(c, _):
        out_ref[c, 0] = dk_ref[c].astype(jnp.bfloat16)
        out_ref[c, 1] = dv_ref[c].astype(jnp.bfloat16)
        out_ref[c, 2] = dk_ref[c + 16].astype(jnp.bfloat16)
        out_ref[c, 3] = dv_ref[c + 16].astype(jnp.bfloat16)
        return 0

    lax.fori_loop(0, 16, finish, 0)


def attend_back_call(lo, blocks, grads, out, lse):
    vmem = pl.BlockSpec(memory_space=pltpu.VMEM)
    return pl.pallas_call(
        attend_back_kernel,
        in_specs=[pl.BlockSpec(memory_space=pltpu.SMEM), vmem, vmem, vmem, vmem],
        out_specs=vmem,
        out_shape=jax.ShapeDtypeStruct((16, 5, 128, 128), jnp.bfloat16),
        scratch_shapes=[
            pltpu.VMEM((32, 128, 128), jnp.float32),
            pltpu.VMEM((32, 128, 128), jnp.float32),
        ],
        compiler_params=pltpu.CompilerParams(vmem_limit_bytes=VMEM_LIMIT),
        cost_estimate=TINY,
    )(lo, blocks, grads, out, lse)


def turn_back_kernel(r_ref, halo_ref, cos_ref, up_ref, down_ref, out_ref, bias_ref):
    for j in range(2):
        sums = [jnp.zeros((1, 128), jnp.float32) for _ in range(3)]
        for x in range(4):
            rows = slice(x * 128, (x + 1) * 128)

            def turned(grad):
                return (
                    grad * cos_ref[rows]
                    - pltpu.roll(grad, 120, 1) * up_ref[rows]
                    - pltpu.roll(grad, 8, 1) * down_ref[rows]
                )

            def read(slot):
                later = r_ref[x + 1, j, 0, slot] if x < 3 else halo_ref[j, 0, slot]
                return r_ref[x, j, 0, slot + 2].astype(jnp.float32) + later.astype(jnp.float32)

            parts = (
                turned(r_ref[x, j, 0, 4].astype(jnp.float32)),
                turned(read(0)),
                read(1),
            )
            for part in range(3):
                grad = parts[part].astype(jnp.bfloat16)
                column = (j * 3 + part) * 128
                out_ref[0, rows, column : column + 128] = grad
                sums[part] = sums[part] + jnp.sum(grad.astype(jnp.float32), 0, keepdims=True)
        for part in range(3):
            column = (j * 3 + part) * 128
            bias_ref[0, :, column : column + 128] = sums[part]


def turn_back_call(blocks, halo, tables):
    table = pl.BlockSpec((512, 128), lambda h: (0, 0))
    return pl.pallas_call(
        turn_back_kernel,
        grid=(2,),
        in_specs=[
            pl.BlockSpec((4, 2, 1, 5, 128, 128), lambda h: (0, 0, h, 0, 0, 0)),
            pl.BlockSpec((2, 1, 2, 128, 128), lambda h: (0, h, 0, 0, 0)),
            table,
            table,
            table,
        ],
        out_specs=[
            pl.BlockSpec((1, 512, 768), lambda h: (h, 0, 0)),
            pl.BlockSpec((1, 1, 768), lambda h: (h, 0, 0)),
        ],
        out_shape=[
            jax.ShapeDtypeStruct((2, 512, 768), jnp.bfloat16),
            jax.ShapeDtypeStruct((2, 1, 768), jnp.float32),
        ],
        compiler_params=pltpu.CompilerParams(vmem_limit_bytes=VMEM_LIMIT),
        cost_estimate=TINY,
    )(blocks, halo, *tables)


def normed_back_kernel(g_ref, unit_ref, w_ref, out_ref, gain_grad_ref, shift_grad_ref):
    grads = jnp.concatenate([g_ref[0], g_ref[1]], 1)
    weights = jnp.concatenate(
        [
            w_ref[0, h, :, :128, j * 512 : j * 512 + 384].reshape(512, 384)
            for h in range(2)
            for j in range(2)
        ],
        1,
    )
    total = mm(grads, weights, 1, 1)
    out_ref[...] = total.astype(jnp.bfloat16).reshape(4, 128, 512)
    unit = unit_ref[...].reshape(512, 512).astype(jnp.float32)
    gain_grad_ref[...] = jnp.sum(total * unit, 0, keepdims=True)
    shift_grad_ref[...] = jnp.sum(total, 0, keepdims=True)


def normed_back_call(grad_joint, unit, weights):
    ring = pl.BlockSpec((4, 128, 512), lambda n: (0, 0, n))
    vector = pl.BlockSpec((1, 512), lambda n: (0, n))
    return pl.pallas_call(
        normed_back_kernel,
        grid=(4,),
        in_specs=[
            pl.BlockSpec((2, 512, 768), lambda n: (0, 0, 0)),
            ring,
            pl.BlockSpec((1, 2, 4, 144, 1024), lambda n: (n, 0, 0, 0, 0)),
        ],
        out_specs=[ring, vector, vector],
        out_shape=[
            jax.ShapeDtypeStruct((4, 128, D), jnp.bfloat16),
            jax.ShapeDtypeStruct((1, D), jnp.float32),
            jax.ShapeDtypeStruct((1, D), jnp.float32),
        ],
        compiler_params=pltpu.CompilerParams(vmem_limit_bytes=VMEM_LIMIT),
        cost_estimate=TINY,
    )(grad_joint, unit, weights)


def local(
    tokens,
    cotangent,
    doc_ids,
    ln1_gain,
    ln1_shift,
    w_qkv,
    b_qkv,
    w_out,
    ln2_gain,
    ln2_shift,
    w_gate,
    w_up,
    w_down,
):
    half = lax.axis_index("yh")
    blk = lax.axis_index(BLK)

    core = lax.axis_index("k").reshape(1)
    vectors = jnp.stack([ln1_gain, ln1_shift, ln2_gain, ln2_shift])
    joint_w = pack_joint_call(w_qkv.transpose(1, 0, 2), w_out, vectors, b_qkv)
    joint_w = lax.all_gather(joint_w, PLANE, axis=0).reshape(4, 2, 4, 144, 1024)
    ring = ring_gather(tokens)
    place = jnp.stack([lax.axis_index("x"), lax.axis_index("k")]).astype(jnp.int32)
    before = lax.ppermute(ring[3], ("yh",), [(0, 1)])
    ring_cot = lax.all_gather(after(cotangent, ring), "x", axis=0)
    rest = pack_hidden_call(w_gate.T, w_up.T, w_down)

    small = joint_w[:, :, :, 128:, :128].astype(jnp.float32)
    bias = small[:, :, :, 8:11, :16].transpose(1, 3, 0, 2, 4).reshape(2, 3, 1, 256)
    vectors = small[:, 0, :, :4].transpose(2, 0, 1, 3).reshape(4, D)
    gain_one, shift_one, gain_two, shift_two = [vectors[i : i + 1] for i in range(4)]

    first_block = jnp.sum((doc_ids[None, :] < doc_ids[:, None]).astype(jnp.int32), axis=1)
    cycles = jnp.arange(4, dtype=jnp.int32) * 16 + half * 64 + blk
    cycles = jnp.concatenate([cycles, 48 + blk.reshape(1)])
    block_position = (cycles - first_block[cycles]) * BLK_TOK
    positions = (block_position[:, None] + jnp.arange(BLK_TOK, dtype=jnp.int32)).reshape(640)
    tables = rotary_tables(positions)
    first_query = half * 64 + (blk // 4) * 16
    lo = lax.dynamic_slice(first_block, (first_query,), (16,)) - (first_query - 16)

    unit_one = unit_call(ring, before)
    payload, normed_one = qkv_call(unit_one, gain_one, shift_one, joint_w, bias, tables)
    out_w, payload = lax.optimization_barrier((joint_w, payload))
    own_rows = out_rows_call(place, out_w)
    near_rows = [send(own_rows, ("x",), t) for t in (1, 3)]
    blocks = after(exchange(payload.reshape(16, 5, 128, 128), BLK), near_rows)
    rest = lax.all_gather(after(rest, blocks), PLANE, axis=0).reshape(4, 2, 512, 3 * HID_PAD)
    att32, att16, lse = attend_call(lo, blocks)
    far_rows = send(after(own_rows, blocks), ("x",), 2)
    attended = exchange(att16, BLK).reshape(4, 2, 2, 128, 128)
    own_rows = [own_rows, near_rows[0], after(far_rows, attended), near_rows[1]]
    other_rows = [swap_core(rows) for rows in own_rows]
    middle, normed_two = project_call(
        place, exchange(attended, ("x",)), tokens, gain_two, shift_two, own_rows, other_rows
    )

    ring_two = exchange(normed_two, ("x",))
    active, grad_gu, ring_grad, ring_out = feed_forward_call(ring_two, ring_cot, rest)
    shared = plane_grad_call(core, with_other(ring_cot), with_other(active), HID_PAD, 2 * HID_PAD)
    came = after(exchange(ring_grad, ("x",)), shared)
    grad_middle, grad_branch, grad_gain_two, grad_shift_two, grad_att = project_back_call(
        place, came, middle, cotangent, gain_two, own_rows, other_rows
    )
    grad_att = exchange(grad_att, ("x",))
    ring_branch = lax.all_gather(after(grad_branch, grad_att), "x", axis=0)
    joint_left = own_rows_call(place, with_other(normed_one))
    grad_att = after(exchange(grad_att.reshape(16, 128, 128), BLK), joint_left)
    attended_pair = with_other(attended.transpose(2, 0, 3, 1, 4).reshape(2, 512, 256))

    mixed = lax.psum_scatter(
        after(ring_out, grad_att).reshape(512, D), "x", scatter_dimension=0, tiled=True
    )
    back = attend_back_call(lo, blocks, grad_att, att32, lse)
    hidden_pair = with_other(ring_two), with_other(grad_gu)
    shared = plane_grad_call(core, *after(hidden_pair, back), 2 * HID_PAD, 0, shared)
    branch_pair = with_other(after(ring_branch, back))
    shared = plane_grad_call(core, branch_pair, attended_pair, 256, 3 * HID_PAD, shared)
    back = exchange(back, BLK).reshape(4, 2, 2, 5, 128, 128)
    back, shared = lax.optimization_barrier((back, shared))
    shared = plane_sum(shared)
    mixed = (middle + after(mixed, back).astype(jnp.float32)).astype(jnp.bfloat16)
    halo_back = lax.ppermute(back[0, :, :, :2], ("yh",), [(1, 0)])
    back = after(back, mixed)
    grad_joint, grad_bias = turn_back_call(back, halo_back, tables)
    places = (chip_places(True), chip_places(False))
    parts = joint_grad_call(places, joint_left, with_other(grad_joint))
    ring_one, grad_gain_one, grad_shift_one = normed_back_call(grad_joint, unit_one, joint_w)
    pair_came = [first_send(parts[4 * j : 4 * j + 4], j == 0) for j in range(2)]

    norms = jnp.concatenate([grad_gain_one, grad_shift_one, grad_gain_two, grad_shift_two], 0)
    norms = norms.reshape(4, 2, 4, 16, 16).transpose(1, 2, 3, 0, 4).reshape(2, 4, 16, 64)
    biases = grad_bias.reshape(2, 2, 3, 8, 16).transpose(0, 1, 3, 2, 4).reshape(2, 1, 16, 48)
    plane = jnp.arange(4).reshape(1, 4, 1, 1) == lax.axis_index("x")
    biases = jnp.where(plane, biases, 0.0)
    sums = jnp.concatenate([norms, biases, jnp.zeros((2, 4, 16, 16), jnp.float32)], 3)
    sums = jnp.sum(exchange(sums.reshape(128, 128), AXES), 0)
    norms = sums[:64].reshape(4, 16)

    came = exchange(after(ring_one, norms, parts[0]), ("x",))
    input_grad = whole_call(
        input_back_kernel,
        jax.ShapeDtypeStruct((128, D), jnp.float32),
        came,
        tokens,
        grad_middle,
        gain_one,
    )
    pair_came[1] = after(pair_came[1], input_grad)
    pair_came = [second_send(first_sum(part, j == 0), j == 0) for j, part in enumerate(pair_came)]

    def shape(*dims):
        return jax.ShapeDtypeStruct(dims, jnp.float32)

    grad_gate, grad_up, grad_down, grad_out = whole_call(
        shared_end_kernel, [shape(HID, 128)] * 3 + [shape(256, 128)], after(shared, input_grad)
    )
    grad_qkv = whole_call(joint_end_kernel, shape(3, 128, 256), *pair_came[0], *pair_came[1])

    return (
        mixed,
        input_grad,
        norms[0],
        norms[1],
        grad_qkv.transpose(1, 0, 2),
        sums[64:112].reshape(3, 16),
        grad_out,
        norms[2],
        norms[3],
        grad_gate.T,
        grad_up.T,
        grad_down,
    )


def solution(mesh):
    whole = Mesh(mesh.devices.reshape(2, 4, 4, 2, 2), AXES)
    ulysses, blk = ("yh", "x"), BLK
    both = ulysses + blk
    placed = (
        P(both, None),
        P(both, None),
        P(),
        P(blk),
        P(blk),
        P(blk, None, ulysses),
        P(None, both),
        P(ulysses, blk),
        P(blk),
        P(blk),
        P(blk, ulysses),
        P(blk, ulysses),
        P(ulysses, blk),
    )
    return jax.shard_map(
        local,
        mesh=whole,
        in_specs=placed,
        out_specs=(
            P(both, None),
            P(both, None),
            P(both),
            P(both),
            P(blk, None, ulysses),
            P(None, both),
            P(ulysses, blk),
            P(both),
            P(both),
            P(blk, ulysses),
            P(blk, ulysses),
            P(ulysses, blk),
        ),
        check_vma=False,
    )
```

```python
import functools

import jax
import jax.numpy as jnp
from jax import lax
from jax.experimental import pallas as pl
from jax.experimental.pallas import tpu as pltpu
from jax.sharding import Mesh
from jax.sharding import PartitionSpec as P

D = 2048
HEADS = 32
HEAD_DIM = 64
ROT = 16
BLK_TOK = 128
HID = 704
HID_PAD = 768
SHARED = 3 * HID_PAD + 256

eps = 1e-05
rope_base = 10000.0
masked_score = -1e30
score_scale = HEAD_DIM ** (-0.5)

AXES = ("yh", "x", "z", "yl", "k")
PLANE = ("z", "yh", "yl", "k")
BLK = ("z", "yl", "k")
Y = ("yh", "yl")

VMEM_LIMIT = 60 * 1024 * 1024
TINY = pl.CostEstimate(flops=1, bytes_accessed=1, transcendentals=0)


def mm(a, b, ca=1, cb=0):
    return lax.dot_general(a, b, (((ca,), (cb,)), ((), ())), preferred_element_type=jnp.float32)


def swap_core(value):
    return lax.ppermute(value, ("k",), [(0, 1), (1, 0)])


def exchange(parts, axes):
    return lax.all_to_all(parts, axes, 0, 0, tiled=True)


def send(value, axes, step):
    return lax.ppermute(value, axes, [(i, (i + step) % 4) for i in range(4)])


def ring_gather(value):
    return exchange(jnp.broadcast_to(value, (4,) + value.shape), ("x",))


def send(value, axes, step):
    return lax.ppermute(value, axes, [(i, (i + step) % 4) for i in range(4)])


def gather(value, axes, *others):
    me = lax.axis_index(axes)
    pieces = [send(value, axes, step) for step in (1, 3, 2)]
    if others:
        pieces = after(pieces, *others)
    buffer = jnp.zeros((4,) + value.shape, value.dtype)
    for step, piece in zip((0, 1, 3, 2), [value] + pieces):
        buffer = lax.dynamic_update_index_in_dim(buffer, piece, (me - step) % 4, 0)
    return buffer


def ring_gather(value):
    return exchange(jnp.broadcast_to(value, (4,) + value.shape), ("x",))


def after(value, *others):
    return lax.optimization_barrier((value,) + others)[0]


def rotary_tables(positions):
    halfway = ROT // 2
    counter = jnp.arange(halfway, dtype=jnp.float32)
    frequency = rope_base ** (-2.0 * counter / ROT)
    lane = jnp.arange(128) % HEAD_DIM
    frequency = jnp.where(lane < ROT, jnp.tile(frequency, 16), 0.0)
    angles = positions.astype(jnp.float32)[:, None] * frequency[None, :]
    sine = jnp.sin(angles)
    return (
        jnp.cos(angles),
        jnp.where(lane < halfway, -sine, 0.0),
        jnp.where((lane >= halfway) & (lane < ROT), sine, 0.0),
    )


def pack_joint_kernel(qkv_ref, out_ref, vectors_ref, bias_ref, w_ref, small_ref):
    out_t = jnp.transpose(out_ref[...])
    for j in range(2):
        pair = slice(j * 128, (j + 1) * 128)
        for part in range(3):
            column = j * 512 + part * 128
            w_ref[:128, column : column + 128] = qkv_ref[part, :, pair]
        w_ref[:128, j * 512 + 384 : j * 512 + 512] = out_t[:, pair]
    small_ref[...] = jnp.zeros_like(small_ref)
    small_ref[0:4, :128] = vectors_ref[...].astype(jnp.float32)
    bias = bias_ref[...].astype(jnp.float32)
    for part in range(3):
        small_ref[8:9, part * 128 : part * 128 + 16] = bias[part : part + 1]
    w_ref[128:, :] = small_ref[...].astype(jnp.bfloat16)


def pack_joint_call(qkv, out, vectors, bias):
    return whole_call(
        pack_joint_kernel,
        jax.ShapeDtypeStruct((144, 1024), jnp.bfloat16),
        qkv,
        out,
        vectors,
        bias,
        scratch=[pltpu.VMEM((16, 1024), jnp.float32)],
    )


def pack_hidden_kernel(gate_ref, up_ref, down_ref, rest_ref):
    for i, ref in enumerate((gate_ref, up_ref, down_ref)):
        first = i * HID_PAD
        rest_ref[:, first + HID_PAD - 128 : first + HID_PAD] = jnp.zeros((128, 128), jnp.bfloat16)
        rest_ref[:, first : first + HID] = jnp.transpose(ref[...])


def pack_hidden_call(gate, up, down):
    return whole_call(
        pack_hidden_kernel, jax.ShapeDtypeStruct((128, 3 * HID_PAD), jnp.bfloat16), gate, up, down
    )


def core_columns(ref, core, blocks):
    columns = [ref[:blocks, :, pl.ds(pl.multiple_of((2 * i + core) * 128, 128), 128)] for i in range(8)]
    return jnp.concatenate(columns, 2).reshape(blocks * 128, 1024)


def normalise(values):
    centred = values - jnp.mean(values, -1, keepdims=True)
    inverse = lax.rsqrt(jnp.mean(centred * centred, -1, keepdims=True) + eps)
    return centred * inverse, inverse


def unit_kernel(x_ref, before_ref, out_ref):
    block = jnp.where(pl.program_id(0) < 4, x_ref[0], before_ref[...])
    out_ref[0] = normalise(block.astype(jnp.float32))[0].astype(jnp.bfloat16)


def unit_call(ring, before):
    return pl.pallas_call(
        unit_kernel,
        grid=(5,),
        in_specs=[
            pl.BlockSpec((1, 128, D), lambda b: (jnp.minimum(b, 3), 0, 0)),
            pl.BlockSpec((128, D), lambda b: (0, 0)),
        ],
        out_specs=pl.BlockSpec((1, 128, D), lambda b: (b, 0, 0)),
        out_shape=jax.ShapeDtypeStruct((5, 128, D), jnp.bfloat16),
        compiler_params=pltpu.CompilerParams(vmem_limit_bytes=VMEM_LIMIT),
        cost_estimate=TINY,
    )(ring, before)


def qkv_kernel(
    unit_ref,
    w0_ref,
    w1_ref,
    cos_ref,
    up_ref,
    down_ref,
    out_ref,
    normed_ref,
    normed_rows,
):
    part = pl.program_id(1)
    chips = [(z, i) for z in range(4) for i in range(4)]
    extras = [w0_ref[z, 0, i, 128:144, :].astype(jnp.float32) for z, i in chips]

    held = jnp.concatenate([rows[8:9] for rows in extras], 0).astype(jnp.bfloat16)
    lane = lax.broadcasted_iota(jnp.int32, (128, 256), 1)
    spread = lax.broadcasted_iota(jnp.int32, (128, 256), 0) == lane % 16
    spread = mm(held, spread.astype(jnp.float32).astype(jnp.bfloat16))
    owner = lax.broadcasted_iota(jnp.int32, (16, 256), 0) == lane[:16] // 16
    bias = jnp.sum(jnp.where(owner, spread, 0.0), 0, keepdims=True)

    @pl.when((pl.program_id(0) == 0) & (part == 0))
    def _():
        gain = jnp.concatenate([rows[0:1] for rows in extras], 1)
        shift = jnp.concatenate([rows[1:2] for rows in extras], 1)
        for b in range(5):
            normed = unit_ref[b].astype(jnp.float32) * gain + shift
            normed = normed.astype(jnp.bfloat16)
            if b < 4:
                normed_ref[b] = normed
            normed_rows[b * 128 : (b + 1) * 128] = normed

    def joint(rows):
        weights = [ref[:, 0, :, :128, :].reshape(D, 128) for ref in (w0_ref, w1_ref)]
        return mm(normed_rows[:rows], jnp.concatenate(weights, 1)) + bias

    def turned(value):
        rows = value.shape[0]
        return (
            value * cos_ref[:rows]
            + pltpu.roll(value, 120, 1) * up_ref[:rows]
            + pltpu.roll(value, 8, 1) * down_ref[:rows]
        )

    @pl.when(part == 0)
    def _():
        value = joint(512)
        for j in range(2):
            query = turned(value[:, j * 128 : (j + 1) * 128]) * score_scale
            out_ref[:, j, 0, 4] = query.astype(jnp.bfloat16).reshape(4, 128, 128)

    @pl.when(part > 0)
    def _():
        value = joint(640)
        for j in range(2):
            block = value[:, j * 128 : (j + 1) * 128]
            block = jnp.where(part == 1, turned(block), block)
            block = block.astype(jnp.bfloat16).reshape(5, 128, 128)

            @pl.when(part == 1)
            def _():
                out_ref[:, j, 0, 2] = block[:4]
                out_ref[1:, j, 0, 0] = block[:3]
                out_ref[0, j, 0, 0] = block[4]

            @pl.when(part == 2)
            def _():
                out_ref[:, j, 0, 3] = block[:4]
                out_ref[1:, j, 0, 1] = block[:3]
                out_ref[0, j, 0, 1] = block[4]


def qkv_call(unit, weights, tables):
    table = pl.BlockSpec((640, 128), lambda h, p: (0, 0))
    return pl.pallas_call(
        qkv_kernel,
        grid=(2, 3),
        in_specs=[
            pl.BlockSpec((5, 128, D), lambda h, p: (0, 0, 0)),
            pl.BlockSpec((4, 1, 4, 144, 128), lambda h, p: (0, h, 0, 0, p)),
            pl.BlockSpec((4, 1, 4, 144, 128), lambda h, p: (0, h, 0, 0, p + 4)),
            table,
            table,
            table,
        ],
        out_specs=[
            pl.BlockSpec((4, 2, 1, 5, 128, 128), lambda h, p: (0, 0, h, 0, 0, 0)),
            pl.BlockSpec((4, 128, D), lambda h, p: (0, 0, 0)),
        ],
        out_shape=[
            jax.ShapeDtypeStruct((4, 2, 2, 5, 128, 128), jnp.bfloat16),
            jax.ShapeDtypeStruct((4, 128, D), jnp.bfloat16),
        ],
        scratch_shapes=[pltpu.VMEM((640, D), jnp.bfloat16)],
        compiler_params=pltpu.CompilerParams(vmem_limit_bytes=VMEM_LIMIT),
        cost_estimate=TINY,
    )(unit, weights, weights, *tables)


def whole_call(kernel, out_shape, *operands, scratch=()):
    vmem = pl.BlockSpec(memory_space=pltpu.VMEM)
    return pl.pallas_call(
        kernel,
        in_specs=[vmem] * len(operands),
        out_specs=jax.tree.map(lambda _: vmem, out_shape),
        out_shape=out_shape,
        scratch_shapes=list(scratch),
        compiler_params=pltpu.CompilerParams(vmem_limit_bytes=VMEM_LIMIT),
        cost_estimate=TINY,
    )(*operands)


def back_through(came_ref, values, gain):
    grad = came_ref[0].astype(jnp.float32)
    for i in range(1, 4):
        grad = grad + came_ref[i].astype(jnp.float32)
    unit, inverse = normalise(values)
    grad_unit = grad * gain
    centred_grad = (
        grad_unit
        - jnp.mean(grad_unit, -1, keepdims=True)
        - unit * jnp.mean(grad_unit * unit, -1, keepdims=True)
    )
    gain_grad = jnp.sum(grad * unit, 0, keepdims=True)
    return inverse * centred_grad, gain_grad, jnp.sum(grad, 0, keepdims=True)


def input_back_kernel(came_ref, tokens_ref, grad_ref, gain_ref, out_ref):
    values = tokens_ref[...].astype(jnp.float32)
    out_ref[...] = grad_ref[...] + back_through(came_ref, values, gain_ref[...])[0]


def shared_end_kernel(total_ref, gate_ref, up_ref, down_ref, out_ref):
    total = jnp.transpose(total_ref[...].astype(jnp.float32))
    for c in range(3):
        width = min(HID, c * 256 + 256) - c * 256
        gate_ref[c * 256 : c * 256 + width] = total[c * 512 : c * 512 + width]
        up_ref[c * 256 : c * 256 + width] = total[c * 512 + 256 : c * 512 + 256 + width]
    down_ref[...] = total[2 * HID_PAD : 2 * HID_PAD + HID]
    out_ref[...] = total[3 * HID_PAD :]


def joint_end_kernel(*refs):
    for j in range(2):
        total = sum(ref[...].astype(jnp.float32) for ref in refs[4 * j : 4 * j + 4])
        for part in range(3):
            refs[8][part, :, j * 128 : (j + 1) * 128] = total[:, part * 128 : part * 128 + 128]


def out_rows_kernel(place_ref, w0_ref, w1_ref, out_ref):
    for yl in range(2):
        for h in range(2):
            for j, ref in enumerate((w0_ref, w1_ref)):
                column = h * 256 + j * 128
                out_ref[yl, :, column : column + 128] = ref[0, h, 2 * yl + place_ref[1], :128]


def out_rows_call(place, weights):
    return pl.pallas_call(
        out_rows_kernel,
        grid=(4,),
        in_specs=[
            pl.BlockSpec(memory_space=pltpu.SMEM),
            pl.BlockSpec((1, 2, 4, 144, 128), lambda n: (n, 0, 0, 0, 3)),
            pl.BlockSpec((1, 2, 4, 144, 128), lambda n: (n, 0, 0, 0, 7)),
        ],
        out_specs=pl.BlockSpec((2, 128, 512), lambda n: (n, 0, 0)),
        out_shape=jax.ShapeDtypeStruct((8, 128, 512), jnp.bfloat16),
        compiler_params=pltpu.CompilerParams(vmem_limit_bytes=VMEM_LIMIT),
        cost_estimate=TINY,
    )(place, weights, weights)


def planes_columns(refs, yl):
    return jnp.concatenate([ref[yl] for ref in refs], 1)


def project_kernel(place_ref, att_ref, tokens_ref, gain_ref, shift_ref, *refs):
    own_refs, other_refs, (middle_ref, normed_ref, att_cols, total) = refs[:4], refs[4:8], refs[8:]
    n, me, core = pl.program_id(0), place_ref[0], place_ref[1]

    @pl.when(n == 0)
    def _():
        for t in range(4):
            x = (me + 4 - t) % 4
            for h in range(2):
                for j in range(2):
                    column = t * 512 + h * 256 + j * 128
                    att_cols[:, column : column + 128] = att_ref[x, j, h]

    weights = jnp.concatenate(
        [planes_columns(refs, yl) for refs in (own_refs, other_refs) for yl in range(2)], 0
    )
    values = mm(att_cols[...], weights, 1, 1)
    for i in range(4):
        holder = core if i < 2 else 1 - core
        column = pl.multiple_of((n * 4 + i % 2 * 2 + holder) * 128, 128)
        total[:, pl.ds(column, 128)] = values[:, i * 128 : i * 128 + 128]

    @pl.when(n == 3)
    def _():
        middle = tokens_ref[...].astype(jnp.float32) + total[...]
        middle_ref[...] = middle
        normed = (normalise(middle)[0] * gain_ref[...] + shift_ref[...]).astype(jnp.bfloat16)
        for i in range(4):
            normed_ref[i] = normed


def project_call(place, att, tokens, gain, shift, own, other):
    def whole(*dims):
        return pl.BlockSpec(dims, lambda n: (0,) * len(dims))

    rows = pl.BlockSpec((2, 128, 512), lambda n: (n, 0, 0))
    return pl.pallas_call(
        project_kernel,
        grid=(4,),
        in_specs=[
            pl.BlockSpec(memory_space=pltpu.SMEM),
            whole(4, 2, 2, 128, 128),
            whole(128, D),
            whole(1, D),
            whole(1, D),
        ]
        + [rows] * 8,
        out_specs=[whole(128, D), whole(4, 128, D)],
        out_shape=[
            jax.ShapeDtypeStruct((128, D), jnp.float32),
            jax.ShapeDtypeStruct((4, 128, D), jnp.bfloat16),
        ],
        scratch_shapes=[pltpu.VMEM((128, D), jnp.bfloat16), pltpu.VMEM((128, D), jnp.float32)],
        compiler_params=pltpu.CompilerParams(vmem_limit_bytes=VMEM_LIMIT),
        cost_estimate=TINY,
    )(place, att, tokens, gain, shift, *own, *other)


def project_back_kernel(place_ref, came_ref, middle_ref, cot_ref, gain_ref, *refs):
    own_refs, other_refs = refs[:4], refs[4:8]
    grad_ref, low_ref, gain_grad_ref, shift_grad_ref, out_ref, low, total = refs[8:]
    n, me, core = pl.program_id(0), place_ref[0], place_ref[1]

    @pl.when(n == 0)
    def _():
        grad, gain_grad_ref[...], shift_grad_ref[...] = back_through(came_ref, middle_ref[...], gain_ref[...])
        grad = grad + cot_ref[...].astype(jnp.float32)
        grad_ref[...] = grad
        low[...] = grad.astype(jnp.bfloat16)
        low_ref[...] = low[...]
        total[...] = jnp.zeros_like(total)

    columns = []
    for i in range(4):
        holder = core if i < 2 else 1 - core
        column = pl.multiple_of((n * 4 + i % 2 * 2 + holder) * 128, 128)
        columns.append(low[:, pl.ds(column, 128)])
    weights = jnp.concatenate(
        [planes_columns(refs, yl) for refs in (own_refs, other_refs) for yl in range(2)], 0
    )
    total[...] += mm(jnp.concatenate(columns, 1), weights)

    @pl.when(n == 3)
    def _():
        for t in range(4):
            x = (me + 4 - t) % 4
            for h in range(2):
                for j in range(2):
                    column = t * 512 + h * 256 + j * 128
                    out_ref[x, j, h] = total[:, column : column + 128].astype(jnp.bfloat16)


def project_back_call(place, came, middle, cot, gain, own, other):
    def whole(*dims):
        return pl.BlockSpec(dims, lambda n: (0,) * len(dims))

    rows = pl.BlockSpec((2, 128, 512), lambda n: (n, 0, 0))
    return pl.pallas_call(
        project_back_kernel,
        grid=(4,),
        in_specs=[
            pl.BlockSpec(memory_space=pltpu.SMEM),
            whole(4, 128, D),
            whole(128, D),
            whole(128, D),
            whole(1, D),
        ]
        + [rows] * 8,
        out_specs=[whole(128, D), whole(128, D), whole(1, D), whole(1, D), whole(4, 2, 2, 128, 128)],
        out_shape=[
            jax.ShapeDtypeStruct((128, D), jnp.float32),
            jax.ShapeDtypeStruct((128, D), jnp.bfloat16),
            jax.ShapeDtypeStruct((1, D), jnp.float32),
            jax.ShapeDtypeStruct((1, D), jnp.float32),
            jax.ShapeDtypeStruct((4, 2, 2, 128, 128), jnp.bfloat16),
        ],
        scratch_shapes=[pltpu.VMEM((128, D), jnp.bfloat16), pltpu.VMEM((128, D), jnp.float32)],
        compiler_params=pltpu.CompilerParams(vmem_limit_bytes=VMEM_LIMIT),
        cost_estimate=TINY,
    )(place, came, middle, cot, gain, *own, *other)


def feed_forward_kernel(
    x_ref, cot_ref, gate_ref, up_ref, down_ref, active_ref, grads_ref, back_ref, out_ref, back_sum, out_sum
):
    first_half = pl.program_id(0) == 0
    x = x_ref[...].reshape(512, D)
    cot = cot_ref[...].reshape(512, D)
    for c in range(3):
        columns = slice(c * 256, c * 256 + 256)
        gate = mm(x, gate_ref[:, 0, :, columns].reshape(D, 256))
        up = mm(x, up_ref[:, 0, :, columns].reshape(D, 256))
        grad_active = mm(cot, down_ref[:, 0, :, columns].reshape(D, 256))
        sigmoid = jax.nn.sigmoid(gate)
        silu = gate * sigmoid
        active_ref[0, :, columns] = (silu * up).astype(jnp.bfloat16)
        grad_gate = grad_active * up * (sigmoid + silu * (1.0 - sigmoid))
        grads_ref[0, :, c * 512 : c * 512 + 256] = grad_gate.astype(jnp.bfloat16)
        grads_ref[0, :, c * 512 + 256 : c * 512 + 512] = (grad_active * silu).astype(jnp.bfloat16)
    for n in range(4):
        rows = slice(n * 512, n * 512 + 512)
        weights = jnp.concatenate(
            [ref[n, 0, :, c * 256 : c * 256 + 256] for c in range(3) for ref in (gate_ref, up_ref)], 1
        )
        back = mm(grads_ref[0], weights, 1, 1)
        out = mm(active_ref[0], down_ref[n, 0], 1, 1)

        @pl.when(first_half)
        def _():
            back_sum[:, rows] = back
            out_sum[:, rows] = out

        @pl.when(~first_half)
        def _():
            back_ref[:, :, rows] = (back_sum[:, rows] + back).astype(jnp.bfloat16).reshape(4, 128, 512)
            out_ref[:, :, rows] = (out_sum[:, rows] + out).astype(jnp.bfloat16).reshape(4, 128, 512)


def feed_forward_call(x, ring, rest):
    tokens = pl.BlockSpec((4, 128, D), lambda h: (0, 0, 0))
    tokens_once = pl.BlockSpec((4, 128, D), lambda h: (0, 0, 0), pipeline_mode=pl.Buffered(1))
    weight = [pl.BlockSpec((4, 1, 512, HID_PAD), lambda h, i=i: (0, h, 0, i)) for i in range(3)]
    ring_shape = jax.ShapeDtypeStruct((4, 128, D), jnp.bfloat16)
    return pl.pallas_call(
        feed_forward_kernel,
        grid=(2,),
        in_specs=[tokens_once, tokens_once] + weight,
        out_specs=[
            pl.BlockSpec((1, 512, HID_PAD), lambda h: (h, 0, 0)),
            pl.BlockSpec((1, 512, 2 * HID_PAD), lambda h: (h, 0, 0)),
            tokens,
            tokens,
        ],
        out_shape=[
            jax.ShapeDtypeStruct((2, 512, HID_PAD), jnp.bfloat16),
            jax.ShapeDtypeStruct((2, 512, 2 * HID_PAD), jnp.bfloat16),
            ring_shape,
            ring_shape,
        ],
        scratch_shapes=[pltpu.VMEM((512, D), jnp.float32), pltpu.VMEM((512, D), jnp.float32)],
        compiler_params=pltpu.CompilerParams(vmem_limit_bytes=VMEM_LIMIT),
        cost_estimate=TINY,
    )(x, ring, rest, rest, rest)


def plane_grad_kernel(core_ref, left_ref, left_other_ref, right_ref, right_other_ref, *refs):
    out_ref, left_t = refs[-2:]

    @pl.when((pl.program_id(0) == 0) & (pl.program_id(1) == 0))
    def _():
        left_t[:, :512] = jnp.transpose(core_columns(left_ref, core_ref[0], 4))
        left_t[:, 512:] = jnp.transpose(core_columns(left_other_ref, core_ref[0], 4))

    total = mm(left_t[...], jnp.concatenate([right_ref[0], right_other_ref[0]], 0)).astype(jnp.bfloat16)
    for z in range(4):
        for yl in range(2):
            row = (z * 2 + yl) * 128
            out_ref[0, yl, z] = total[row : row + 128]


def plane_grad_call(core, left, right, columns, first, shared=None):
    left_block = pl.BlockSpec((4, 128, D), lambda n, h: (0, 0, 0))
    right_block = pl.BlockSpec((1, 512, 256), lambda n, h: (h, 0, n))
    extra = [] if shared is None else [shared]
    return pl.pallas_call(
        plane_grad_kernel,
        grid=(columns // 256, 2),
        in_specs=[
            pl.BlockSpec(memory_space=pltpu.SMEM),
            left_block,
            left_block,
            right_block,
            right_block,
        ]
        + [pl.BlockSpec(memory_space=pl.ANY)] * len(extra),
        out_specs=pl.BlockSpec((1, 2, 4, 128, 256), lambda n, h: (h, 0, 0, 0, first // 256 + n)),
        out_shape=jax.ShapeDtypeStruct((2, 2, 4, 128, SHARED), jnp.bfloat16),
        input_output_aliases={5: 0} if extra else {},
        scratch_shapes=[pltpu.VMEM((1024, 1024), jnp.bfloat16)],
        compiler_params=pltpu.CompilerParams(vmem_limit_bytes=VMEM_LIMIT),
        cost_estimate=TINY,
    )(core, *left, *right, *extra)


def own_rows_kernel(place_ref, left_ref, left_other_ref, out_ref):
    out_ref[:, :512] = jnp.transpose(core_columns(left_ref, place_ref[1], 4))
    out_ref[:, 512:] = jnp.transpose(core_columns(left_other_ref, place_ref[1], 4))


def own_rows_call(place, left):
    vmem = pl.BlockSpec(memory_space=pltpu.VMEM)
    return pl.pallas_call(
        own_rows_kernel,
        in_specs=[pl.BlockSpec(memory_space=pltpu.SMEM), vmem, vmem],
        out_specs=vmem,
        out_shape=jax.ShapeDtypeStruct((1024, 1024), jnp.bfloat16),
        compiler_params=pltpu.CompilerParams(vmem_limit_bytes=VMEM_LIMIT),
        cost_estimate=TINY,
    )(place, *left)


def joint_grad_kernel(place_ref, left_ref, right_ref, right_other_ref, *outs):
    h = pl.program_id(0)
    right = jnp.concatenate([right_ref[0], right_other_ref[0]], 0)
    total = mm(left_ref[...], right).astype(jnp.bfloat16)
    for z in range(4):
        for yl in range(2):
            row = (z * 2 + yl) * 128
            chip = (h * 2 + yl) * 4 + z
            for j in range(2):
                step, slot = place_ref[2 * j, chip], place_ref[2 * j + 1, chip]
                for t in range(4):

                    @pl.when(step == t)
                    def _():
                        outs[4 * j + t][slot] = total[row : row + 128, j * 384 : j * 384 + 384]


def joint_grad_call(places, left, right):
    right_block = pl.BlockSpec((1, 512, 768), lambda h: (h, 0, 0))
    return pl.pallas_call(
        joint_grad_kernel,
        grid=(2,),
        in_specs=[
            pl.BlockSpec(memory_space=pltpu.SMEM),
            pl.BlockSpec((1024, 1024), lambda h: (0, 0)),
            right_block,
            right_block,
        ],
        out_specs=[pl.BlockSpec((4, 128, 384), lambda h: (0, 0, 0))] * 8,
        out_shape=[jax.ShapeDtypeStruct((4, 128, 384), jnp.bfloat16)] * 8,
        compiler_params=pltpu.CompilerParams(vmem_limit_bytes=VMEM_LIMIT),
        cost_estimate=TINY,
    )(jnp.concatenate(places, 0), left, *right)


def split_sum_kernel(place_ref, a_ref, b_ref, c_ref, d_ref, *out_refs):
    for t in range(4):
        i = (place_ref[0] + t) % 4
        total = sum(ref[i].astype(jnp.float32) for ref in (a_ref, b_ref, c_ref, d_ref))
        out_refs[t][...] = total.astype(jnp.bfloat16)


def split_sum_call(place, parts):
    columns = parts[0].shape[2]
    width = 256 if columns % 256 == 0 else 384
    return pl.pallas_call(
        split_sum_kernel,
        grid=(columns // width,),
        in_specs=[pl.BlockSpec(memory_space=pltpu.SMEM)]
        + [pl.BlockSpec((4, 128, width), lambda n: (0, 0, n))] * 4,
        out_specs=[pl.BlockSpec((128, width), lambda n: (0, n))] * 4,
        out_shape=[jax.ShapeDtypeStruct((128, columns), jnp.bfloat16)] * 4,
        compiler_params=pltpu.CompilerParams(vmem_limit_bytes=VMEM_LIMIT),
        cost_estimate=TINY,
    )(place, *parts)


def chip_places(y_first):
    y, z = jnp.arange(16, dtype=jnp.int32) // 4, jnp.arange(16, dtype=jnp.int32) % 4
    if y_first:
        return jnp.stack([(y - lax.axis_index(Y)) % 4, z])
    return jnp.stack([(z - lax.axis_index("z")) % 4, y])


def plane_sum(parts):
    parts = parts.reshape(2048, parts.shape[-1])
    return lax.psum_scatter(parts, ("yh", "yl", "z"), scatter_dimension=0, tiled=True)


def with_other(value):
    return value, swap_core(value)


def first_send(parts, y_first):
    axes = Y if y_first else ("z",)
    return [parts[0]] + [send(parts[t], axes, t) for t in (1, 3, 2)]


def first_sum(parts, y_first):
    return split_sum_call(lax.axis_index(("z",) if y_first else Y).reshape(1), parts)


def second_send(parts, y_first):
    axes = ("z",) if y_first else Y
    return [parts[0]] + [send(parts[t], axes, t) for t in (1, 3, 2)]


def stack_heads(ref, *index):
    first = (lax.broadcasted_iota(jnp.int32, (128, 128), 1) < HEAD_DIM).astype(jnp.float32).astype(jnp.bfloat16)
    masks = (first, 1 - first)
    return jnp.concatenate([ref[i] * mask for i in index for mask in masks], 0)


def unstack_heads(values, block):
    low = lax.broadcasted_iota(jnp.int32, (128, 128), 1) < HEAD_DIM
    rows = values[block * 256 : block * 256 + 256]
    return jnp.where(low, rows[:128], rows[128:])


def key_blocks(r_ref, block, slot):
    rows = []
    for i in range(4):
        index = jnp.maximum(block + i, 0)
        rows.append(r_ref[index & 15, (index >> 4) * 2 + slot])
    return jnp.concatenate(rows, 0)


def masked(values, a, block, lo_a, lo_b, diagonal, fill):
    key_row = lax.broadcasted_iota(jnp.int32, (128, 256), 0)
    causal = key_row <= lax.broadcasted_iota(jnp.int32, (128, 256), 1) % 128
    rows = []
    for k in range(4):
        parts = []
        for i, lo in enumerate((lo_a, lo_b)):
            mask = block + k >= lo
            if diagonal and k == 2 + i:
                mask = causal
            part = values[k * 128 : k * 128 + 128, i * 256 : i * 256 + 256]
            if diagonal and k == 3 and i == 0:
                parts.append(jnp.full((128, 256), fill, jnp.float32))
            else:
                parts.append(jnp.where(mask, part, fill))
        rows.append(jnp.concatenate(parts, 1))
    return jnp.concatenate(rows, 0)


def attend_kernel(lo_ref, r_ref, o32_ref, o16_ref, lse_ref):
    def one_pair(a, _):
        lo_a, lo_b = lo_ref[2 * a], lo_ref[2 * a + 1]
        queries = stack_heads(r_ref, (2 * a, 4), (2 * a + 1, 4))

        def scores(block, diagonal):
            values = mm(key_blocks(r_ref, block, 0), queries, 1, 1)
            return masked(values, a, block, lo_a, lo_b, diagonal, masked_score)

        def add(scores, block, top):
            weights = jnp.exp(scores - top)
            sums = mm(key_blocks(r_ref, block, 1), weights.astype(jnp.bfloat16), 0, 0)
            return jnp.sum(weights, 0, keepdims=True), sums

        diagonal = scores(2 * a + 14, True)
        top = jnp.max(diagonal, 0, keepdims=True)
        total, sums = add(diagonal, 2 * a + 14, top)

        def earlier(i, carry):
            top, total, sums = carry
            block = 2 * a + 14 - 4 * i
            values = scores(block, False)
            new = jnp.maximum(top, jnp.max(values, 0, keepdims=True))
            scale = jnp.exp(top - new)
            more, more_sums = add(values, block, new)
            return new, total * scale + more, sums * scale + more_sums

        steps = (2 * a + 21 - lo_a) // 4
        top, total, sums = lax.fori_loop(1, steps, earlier, (top, total, sums))
        out = jnp.transpose(sums / total)
        for block in range(2):
            rows = unstack_heads(out, block)
            o32_ref[2 * a + block] = rows
            o16_ref[2 * a + block] = rows.astype(jnp.bfloat16)
        lse_ref[a] = top + jnp.log(total)
        return 0

    lax.fori_loop(0, 8, one_pair, 0)


def attend_call(lo, blocks):
    vmem = pl.BlockSpec(memory_space=pltpu.VMEM)
    return pl.pallas_call(
        attend_kernel,
        in_specs=[pl.BlockSpec(memory_space=pltpu.SMEM), vmem],
        out_specs=[vmem, vmem, vmem],
        out_shape=[
            jax.ShapeDtypeStruct((16, 128, 128), jnp.float32),
            jax.ShapeDtypeStruct((16, 128, 128), jnp.bfloat16),
            jax.ShapeDtypeStruct((8, 1, 512), jnp.float32),
        ],
        compiler_params=pltpu.CompilerParams(vmem_limit_bytes=VMEM_LIMIT),
        cost_estimate=TINY,
    )(lo, blocks)


def attend_back_kernel(lo_ref, r_ref, do_ref, o32_ref, lse_ref, out_ref, dk_ref, dv_ref):
    dk_ref[...] = jnp.zeros_like(dk_ref)
    dv_ref[...] = jnp.zeros_like(dv_ref)

    def one_pair(a, _):
        lo_a, lo_b = lo_ref[2 * a], lo_ref[2 * a + 1]
        queries = stack_heads(r_ref, (2 * a, 4), (2 * a + 1, 4))
        grads = stack_heads(do_ref, 2 * a, 2 * a + 1)
        out = jnp.concatenate([o32_ref[2 * a]] * 2 + [o32_ref[2 * a + 1]] * 2, 0)
        delta = jnp.sum(jnp.transpose(grads.astype(jnp.float32) * out), 0, keepdims=True)
        lse = lse_ref[a]

        def blocks_back(block, diagonal):
            keys, values = key_blocks(r_ref, block, 0), key_blocks(r_ref, block, 1)
            weights = jnp.exp(mm(keys, queries, 1, 1) - lse)
            weights = masked(weights, a, block, lo_a, lo_b, diagonal, 0.0)
            grad_scores = (weights * (mm(values, grads, 1, 1) - delta)).astype(jnp.bfloat16)
            grad_values = mm(weights.astype(jnp.bfloat16), grads)
            grad_keys = mm(grad_scores, queries)
            for k in range(4):
                index, rows = jnp.maximum(block + k, 0), slice(k * 128, k * 128 + 128)
                dv_ref[index] += grad_values[rows]
                dk_ref[index] += grad_keys[rows]
            return mm(grad_scores, keys, 0, 0)

        def earlier(i, grad_query):
            return grad_query + blocks_back(2 * a + 14 - 4 * i, False)

        steps = (2 * a + 21 - lo_a) // 4
        grad_query = blocks_back(2 * a + 14, True)
        grad_query = lax.fori_loop(1, steps, earlier, grad_query)
        for block in range(2):
            rows = unstack_heads(grad_query, block) * score_scale
            out_ref[2 * a + block, 4] = rows.astype(jnp.bfloat16)
        return 0

    lax.fori_loop(0, 8, one_pair, 0)

    def finish(c, _):
        out_ref[c, 0] = dk_ref[c].astype(jnp.bfloat16)
        out_ref[c, 1] = dv_ref[c].astype(jnp.bfloat16)
        out_ref[c, 2] = dk_ref[c + 16].astype(jnp.bfloat16)
        out_ref[c, 3] = dv_ref[c + 16].astype(jnp.bfloat16)
        return 0

    lax.fori_loop(0, 16, finish, 0)


def attend_back_call(lo, blocks, grads, out, lse):
    vmem = pl.BlockSpec(memory_space=pltpu.VMEM)
    return pl.pallas_call(
        attend_back_kernel,
        in_specs=[pl.BlockSpec(memory_space=pltpu.SMEM), vmem, vmem, vmem, vmem],
        out_specs=vmem,
        out_shape=jax.ShapeDtypeStruct((16, 5, 128, 128), jnp.bfloat16),
        scratch_shapes=[
            pltpu.VMEM((32, 128, 128), jnp.float32),
            pltpu.VMEM((32, 128, 128), jnp.float32),
        ],
        compiler_params=pltpu.CompilerParams(vmem_limit_bytes=VMEM_LIMIT),
        cost_estimate=TINY,
    )(lo, blocks, grads, out, lse)


def turn_back_kernel(r_ref, halo_ref, cos_ref, up_ref, down_ref, out_ref, bias_ref):
    for j in range(2):
        sums = [jnp.zeros((1, 128), jnp.float32) for _ in range(3)]
        for x in range(4):
            rows = slice(x * 128, (x + 1) * 128)

            def turned(grad):
                return (
                    grad * cos_ref[rows]
                    - pltpu.roll(grad, 120, 1) * up_ref[rows]
                    - pltpu.roll(grad, 8, 1) * down_ref[rows]
                )

            def read(slot):
                later = r_ref[x + 1, j, 0, slot] if x < 3 else halo_ref[j, 0, slot]
                return r_ref[x, j, 0, slot + 2].astype(jnp.float32) + later.astype(jnp.float32)

            parts = (
                turned(r_ref[x, j, 0, 4].astype(jnp.float32)),
                turned(read(0)),
                read(1),
            )
            for part in range(3):
                grad = parts[part].astype(jnp.bfloat16)
                column = (j * 3 + part) * 128
                out_ref[0, rows, column : column + 128] = grad
                sums[part] = sums[part] + jnp.sum(grad.astype(jnp.float32), 0, keepdims=True)
        for part in range(3):
            column = (j * 3 + part) * 128
            bias_ref[0, :, column : column + 128] = sums[part]


def turn_back_call(blocks, halo, tables):
    table = pl.BlockSpec((512, 128), lambda h: (0, 0))
    return pl.pallas_call(
        turn_back_kernel,
        grid=(2,),
        in_specs=[
            pl.BlockSpec((4, 2, 1, 5, 128, 128), lambda h: (0, 0, h, 0, 0, 0)),
            pl.BlockSpec((2, 1, 2, 128, 128), lambda h: (0, h, 0, 0, 0)),
            table,
            table,
            table,
        ],
        out_specs=[
            pl.BlockSpec((1, 512, 768), lambda h: (h, 0, 0)),
            pl.BlockSpec((1, 1, 768), lambda h: (h, 0, 0)),
        ],
        out_shape=[
            jax.ShapeDtypeStruct((2, 512, 768), jnp.bfloat16),
            jax.ShapeDtypeStruct((2, 1, 768), jnp.float32),
        ],
        compiler_params=pltpu.CompilerParams(vmem_limit_bytes=VMEM_LIMIT),
        cost_estimate=TINY,
    )(blocks, halo, *tables)


def normed_back_kernel(g_ref, unit_ref, w_ref, out_ref, gain_grad_ref, shift_grad_ref):
    grads = jnp.concatenate([g_ref[0], g_ref[1]], 1)
    weights = jnp.concatenate(
        [
            w_ref[0, h, :, :128, j * 512 : j * 512 + 384].reshape(512, 384)
            for h in range(2)
            for j in range(2)
        ],
        1,
    )
    total = mm(grads, weights, 1, 1)
    out_ref[...] = total.astype(jnp.bfloat16).reshape(4, 128, 512)
    unit = unit_ref[...].reshape(512, 512).astype(jnp.float32)
    gain_grad_ref[...] = jnp.sum(total * unit, 0, keepdims=True)
    shift_grad_ref[...] = jnp.sum(total, 0, keepdims=True)


def normed_back_call(grad_joint, unit, weights):
    ring = pl.BlockSpec((4, 128, 512), lambda n: (0, 0, n))
    vector = pl.BlockSpec((1, 512), lambda n: (0, n))
    return pl.pallas_call(
        normed_back_kernel,
        grid=(4,),
        in_specs=[
            pl.BlockSpec((2, 512, 768), lambda n: (0, 0, 0)),
            ring,
            pl.BlockSpec((1, 2, 4, 144, 1024), lambda n: (n, 0, 0, 0, 0)),
        ],
        out_specs=[ring, vector, vector],
        out_shape=[
            jax.ShapeDtypeStruct((4, 128, D), jnp.bfloat16),
            jax.ShapeDtypeStruct((1, D), jnp.float32),
            jax.ShapeDtypeStruct((1, D), jnp.float32),
        ],
        compiler_params=pltpu.CompilerParams(vmem_limit_bytes=VMEM_LIMIT),
        cost_estimate=TINY,
    )(grad_joint, unit, weights)


def local(
    tokens,
    cotangent,
    doc_ids,
    ln1_gain,
    ln1_shift,
    w_qkv,
    b_qkv,
    w_out,
    ln2_gain,
    ln2_shift,
    w_gate,
    w_up,
    w_down,
):
    half = lax.axis_index("yh")
    blk = lax.axis_index(BLK)

    core = lax.axis_index("k").reshape(1)
    vectors = jnp.stack([ln1_gain, ln1_shift, ln2_gain, ln2_shift])
    joint_w = pack_joint_call(w_qkv.transpose(1, 0, 2), w_out, vectors, b_qkv)
    joint_w = lax.all_gather(joint_w, PLANE, axis=0).reshape(4, 2, 4, 144, 1024)
    ring = ring_gather(tokens)
    place = jnp.stack([lax.axis_index("x"), lax.axis_index("k")]).astype(jnp.int32)
    before = lax.ppermute(ring[3], ("yh",), [(0, 1)])
    ring_cot = lax.all_gather(after(cotangent, ring), "x", axis=0)
    rest = pack_hidden_call(w_gate.T, w_up.T, w_down)


    first_block = jnp.sum((doc_ids[None, :] < doc_ids[:, None]).astype(jnp.int32), axis=1)
    cycles = jnp.arange(4, dtype=jnp.int32) * 16 + half * 64 + blk
    cycles = jnp.concatenate([cycles, 48 + blk.reshape(1)])
    block_position = (cycles - first_block[cycles]) * BLK_TOK
    positions = (block_position[:, None] + jnp.arange(BLK_TOK, dtype=jnp.int32)).reshape(640)
    tables = rotary_tables(positions)
    first_query = half * 64 + (blk // 4) * 16
    lo = lax.dynamic_slice(first_block, (first_query,), (16,)) - (first_query - 16)

    unit_one = unit_call(ring, before)
    payload, normed_one = qkv_call(unit_one, joint_w, tables)
    out_w, payload = lax.optimization_barrier((joint_w, payload))
    vectors = out_w[:, 0, :, 128:132, :128].astype(jnp.float32).transpose(2, 0, 1, 3).reshape(4, D)
    gain_one, _, gain_two, shift_two = [vectors[i : i + 1] for i in range(4)]
    own_rows = out_rows_call(place, out_w)
    near_rows = [send(own_rows, ("x",), t) for t in (1, 3)]
    blocks = after(exchange(payload.reshape(16, 5, 128, 128), BLK), near_rows)
    rest = lax.all_gather(after(rest, blocks), PLANE, axis=0).reshape(4, 2, 512, 3 * HID_PAD)
    att32, att16, lse = attend_call(lo, blocks)
    far_rows = send(after(own_rows, blocks), ("x",), 2)
    attended = exchange(att16, BLK).reshape(4, 2, 2, 128, 128)
    own_rows = [own_rows, near_rows[0], after(far_rows, attended), near_rows[1]]
    other_rows = [swap_core(rows) for rows in own_rows]
    middle, normed_two = project_call(
        place, exchange(attended, ("x",)), tokens, gain_two, shift_two, own_rows, other_rows
    )

    ring_two = exchange(normed_two, ("x",))
    active, grad_gu, ring_grad, ring_out = feed_forward_call(ring_two, ring_cot, rest)
    shared = plane_grad_call(core, with_other(ring_cot), with_other(active), HID_PAD, 2 * HID_PAD)
    came = after(exchange(ring_grad, ("x",)), shared)
    grad_middle, grad_branch, grad_gain_two, grad_shift_two, grad_att = project_back_call(
        place, came, middle, cotangent, gain_two, own_rows, other_rows
    )
    grad_att = exchange(grad_att, ("x",))
    ring_branch = lax.all_gather(after(grad_branch, grad_att), "x", axis=0)
    joint_left = own_rows_call(place, with_other(normed_one))
    grad_att = after(exchange(grad_att.reshape(16, 128, 128), BLK), joint_left)
    attended_pair = with_other(attended.transpose(2, 0, 3, 1, 4).reshape(2, 512, 256))

    mixed = lax.psum_scatter(
        after(ring_out, grad_att).reshape(512, D), "x", scatter_dimension=0, tiled=True
    )
    back = attend_back_call(lo, blocks, grad_att, att32, lse)
    hidden_pair = with_other(ring_two), with_other(grad_gu)
    shared = plane_grad_call(core, *after(hidden_pair, back), 2 * HID_PAD, 0, shared)
    branch_pair = with_other(after(ring_branch, back))
    shared = plane_grad_call(core, branch_pair, attended_pair, 256, 3 * HID_PAD, shared)
    back = exchange(back, BLK).reshape(4, 2, 2, 5, 128, 128)
    back, shared = lax.optimization_barrier((back, shared))
    shared = plane_sum(shared)
    mixed = (middle + after(mixed, back).astype(jnp.float32)).astype(jnp.bfloat16)
    halo_back = lax.ppermute(back[0, :, :, :2], ("yh",), [(1, 0)])
    back = after(back, mixed)
    grad_joint, grad_bias = turn_back_call(back, halo_back, tables)
    places = (chip_places(True), chip_places(False))
    parts = joint_grad_call(places, joint_left, with_other(grad_joint))
    ring_one, grad_gain_one, grad_shift_one = normed_back_call(grad_joint, unit_one, joint_w)
    pair_came = [first_send(parts[4 * j : 4 * j + 4], j == 0) for j in range(2)]

    norms = jnp.concatenate([grad_gain_one, grad_shift_one, grad_gain_two, grad_shift_two], 0)
    norms = norms.reshape(4, 2, 4, 16, 16).transpose(1, 2, 3, 0, 4).reshape(2, 4, 16, 64)
    biases = grad_bias.reshape(2, 2, 3, 8, 16).transpose(0, 1, 3, 2, 4).reshape(2, 1, 16, 48)
    plane = jnp.arange(4).reshape(1, 4, 1, 1) == lax.axis_index("x")
    biases = jnp.where(plane, biases, 0.0)
    sums = jnp.concatenate([norms, biases, jnp.zeros((2, 4, 16, 16), jnp.float32)], 3)
    sums = jnp.sum(exchange(sums.reshape(128, 128), AXES), 0)
    norms = sums[:64].reshape(4, 16)

    came = exchange(after(ring_one, norms, parts[0]), ("x",))
    input_grad = whole_call(
        input_back_kernel,
        jax.ShapeDtypeStruct((128, D), jnp.float32),
        came,
        tokens,
        grad_middle,
        gain_one,
    )
    pair_came[1] = after(pair_came[1], input_grad)
    pair_came = [second_send(first_sum(part, j == 0), j == 0) for j, part in enumerate(pair_came)]

    def shape(*dims):
        return jax.ShapeDtypeStruct(dims, jnp.float32)

    grad_gate, grad_up, grad_down, grad_out = whole_call(
        shared_end_kernel, [shape(HID, 128)] * 3 + [shape(256, 128)], after(shared, input_grad)
    )
    grad_qkv = whole_call(joint_end_kernel, shape(3, 128, 256), *pair_came[0], *pair_came[1])

    return (
        mixed,
        input_grad,
        norms[0],
        norms[1],
        grad_qkv.transpose(1, 0, 2),
        sums[64:112].reshape(3, 16),
        grad_out,
        norms[2],
        norms[3],
        grad_gate.T,
        grad_up.T,
        grad_down,
    )


def solution(mesh):
    whole = Mesh(mesh.devices.reshape(2, 4, 4, 2, 2), AXES)
    ulysses, blk = ("yh", "x"), BLK
    both = ulysses + blk
    placed = (
        P(both, None),
        P(both, None),
        P(),
        P(blk),
        P(blk),
        P(blk, None, ulysses),
        P(None, both),
        P(ulysses, blk),
        P(blk),
        P(blk),
        P(blk, ulysses),
        P(blk, ulysses),
        P(ulysses, blk),
    )
    return jax.shard_map(
        local,
        mesh=whole,
        in_specs=placed,
        out_specs=(
            P(both, None),
            P(both, None),
            P(both),
            P(both),
            P(blk, None, ulysses),
            P(None, both),
            P(ulysses, blk),
            P(both),
            P(both),
            P(blk, ulysses),
            P(blk, ulysses),
            P(ulysses, blk),
        ),
        check_vma=False,
    )
```

```python
import functools

import jax
import jax.numpy as jnp
from jax import lax
from jax.experimental import pallas as pl
from jax.experimental.pallas import tpu as pltpu
from jax.sharding import Mesh
from jax.sharding import PartitionSpec as P

D = 2048
HEADS = 32
HEAD_DIM = 64
ROT = 16
BLK_TOK = 128
HID = 704
HID_PAD = 768
SHARED = 3 * HID_PAD + 256

eps = 1e-05
rope_base = 10000.0
masked_score = -1e30
score_scale = HEAD_DIM ** (-0.5)

AXES = ("yh", "x", "z", "yl", "k")
PLANE = ("z", "yh", "yl", "k")
BLK = ("z", "yl", "k")
Y = ("yh", "yl")

VMEM_LIMIT = 63 * 1024 * 1024
TINY = pl.CostEstimate(flops=1, bytes_accessed=1, transcendentals=0)


def mm(a, b, ca=1, cb=0):
    return lax.dot_general(a, b, (((ca,), (cb,)), ((), ())), preferred_element_type=jnp.float32)


def swap_core(value):
    return lax.ppermute(value, ("k",), [(0, 1), (1, 0)])


def exchange(parts, axes):
    return lax.all_to_all(parts, axes, 0, 0, tiled=True)


def send(value, axes, step):
    return lax.ppermute(value, axes, [(i, (i + step) % 4) for i in range(4)])


def ring_gather(value):
    return exchange(jnp.broadcast_to(value, (4,) + value.shape), ("x",))


def send(value, axes, step):
    return lax.ppermute(value, axes, [(i, (i + step) % 4) for i in range(4)])


def gather(value, axes, *others):
    me = lax.axis_index(axes)
    pieces = [send(value, axes, step) for step in (1, 3, 2)]
    if others:
        pieces = after(pieces, *others)
    buffer = jnp.zeros((4,) + value.shape, value.dtype)
    for step, piece in zip((0, 1, 3, 2), [value] + pieces):
        buffer = lax.dynamic_update_index_in_dim(buffer, piece, (me - step) % 4, 0)
    return buffer


def ring_gather(value):
    return exchange(jnp.broadcast_to(value, (4,) + value.shape), ("x",))


def after(value, *others):
    return lax.optimization_barrier((value,) + others)[0]


def rotary_tables(positions):
    halfway = ROT // 2
    counter = jnp.arange(halfway, dtype=jnp.float32)
    frequency = rope_base ** (-2.0 * counter / ROT)
    lane = jnp.arange(128) % HEAD_DIM
    frequency = jnp.where(lane < ROT, jnp.tile(frequency, 16), 0.0)
    angles = positions.astype(jnp.float32)[:, None] * frequency[None, :]
    sine = jnp.sin(angles)
    return (
        jnp.cos(angles),
        jnp.where(lane < halfway, -sine, 0.0),
        jnp.where((lane >= halfway) & (lane < ROT), sine, 0.0),
    )


def pack_joint_kernel(qkv_ref, out_ref, vectors_ref, bias_ref, w_ref, small_ref):
    out_t = jnp.transpose(out_ref[...])
    for j in range(2):
        pair = slice(j * 128, (j + 1) * 128)
        for part in range(3):
            column = j * 512 + part * 128
            w_ref[:128, column : column + 128] = qkv_ref[part, :, pair]
        w_ref[:128, j * 512 + 384 : j * 512 + 512] = out_t[:, pair]
    small_ref[...] = jnp.zeros_like(small_ref)
    small_ref[0:4, :128] = vectors_ref[...].astype(jnp.float32)
    bias = bias_ref[...].astype(jnp.float32)
    for part in range(3):
        small_ref[8:9, part * 128 : part * 128 + 16] = bias[part : part + 1]
    w_ref[128:, :] = small_ref[...].astype(jnp.bfloat16)


def pack_joint_call(qkv, out, vectors, bias):
    return whole_call(
        pack_joint_kernel,
        jax.ShapeDtypeStruct((144, 1024), jnp.bfloat16),
        qkv,
        out,
        vectors,
        bias,
        scratch=[pltpu.VMEM((16, 1024), jnp.float32)],
    )


def pack_hidden_kernel(gate_ref, up_ref, down_ref, rest_ref):
    for i, ref in enumerate((gate_ref, up_ref, down_ref)):
        first = i * HID_PAD
        rest_ref[:, first + HID_PAD - 128 : first + HID_PAD] = jnp.zeros((128, 128), jnp.bfloat16)
        rest_ref[:, first : first + HID] = jnp.transpose(ref[...])


def pack_hidden_call(gate, up, down):
    return whole_call(
        pack_hidden_kernel, jax.ShapeDtypeStruct((128, 3 * HID_PAD), jnp.bfloat16), gate, up, down
    )


def core_columns(ref, core, blocks):
    columns = [ref[:blocks, :, pl.ds(pl.multiple_of((2 * i + core) * 128, 128), 128)] for i in range(8)]
    return jnp.concatenate(columns, 2).reshape(blocks * 128, 1024)


def normalise(values):
    centred = values - jnp.mean(values, -1, keepdims=True)
    inverse = lax.rsqrt(jnp.mean(centred * centred, -1, keepdims=True) + eps)
    return centred * inverse, inverse


def unit_kernel(x_ref, before_ref, out_ref):
    block = jnp.where(pl.program_id(0) < 4, x_ref[0], before_ref[...])
    out_ref[0] = normalise(block.astype(jnp.float32))[0].astype(jnp.bfloat16)


def unit_call(ring, before):
    return pl.pallas_call(
        unit_kernel,
        grid=(5,),
        in_specs=[
            pl.BlockSpec((1, 128, D), lambda b: (jnp.minimum(b, 3), 0, 0)),
            pl.BlockSpec((128, D), lambda b: (0, 0)),
        ],
        out_specs=pl.BlockSpec((1, 128, D), lambda b: (b, 0, 0)),
        out_shape=jax.ShapeDtypeStruct((5, 128, D), jnp.bfloat16),
        compiler_params=pltpu.CompilerParams(vmem_limit_bytes=VMEM_LIMIT),
        cost_estimate=TINY,
    )(ring, before)


def qkv_kernel(
    unit_ref,
    w0_ref,
    w1_ref,
    cos_ref,
    up_ref,
    down_ref,
    out_ref,
    normed_ref,
    normed_rows,
):
    part = pl.program_id(1)
    chips = [(z, i) for z in range(4) for i in range(4)]
    extras = [w0_ref[z, 0, i, 128:144, :].astype(jnp.float32) for z, i in chips]

    held = jnp.concatenate([rows[8:9] for rows in extras], 0).astype(jnp.bfloat16)
    lane = lax.broadcasted_iota(jnp.int32, (128, 256), 1)
    spread = lax.broadcasted_iota(jnp.int32, (128, 256), 0) == lane % 16
    spread = mm(held, spread.astype(jnp.float32).astype(jnp.bfloat16))
    owner = lax.broadcasted_iota(jnp.int32, (16, 256), 0) == lane[:16] // 16
    bias = jnp.sum(jnp.where(owner, spread, 0.0), 0, keepdims=True)

    @pl.when((pl.program_id(0) == 0) & (part == 0))
    def _():
        gain = jnp.concatenate([rows[0:1] for rows in extras], 1)
        shift = jnp.concatenate([rows[1:2] for rows in extras], 1)
        for b in range(5):
            normed = unit_ref[b].astype(jnp.float32) * gain + shift
            normed = normed.astype(jnp.bfloat16)
            if b < 4:
                normed_ref[b] = normed
            normed_rows[b * 128 : (b + 1) * 128] = normed

    def joint(rows):
        weights = [ref[:, 0, :, :128, :].reshape(D, 128) for ref in (w0_ref, w1_ref)]
        return mm(normed_rows[:rows], jnp.concatenate(weights, 1)) + bias

    def turned(value):
        rows = value.shape[0]
        return (
            value * cos_ref[:rows]
            + pltpu.roll(value, 120, 1) * up_ref[:rows]
            + pltpu.roll(value, 8, 1) * down_ref[:rows]
        )

    @pl.when(part == 0)
    def _():
        value = joint(512)
        for j in range(2):
            query = turned(value[:, j * 128 : (j + 1) * 128]) * score_scale
            out_ref[:, j, 0, 4] = query.astype(jnp.bfloat16).reshape(4, 128, 128)

    @pl.when(part > 0)
    def _():
        value = joint(640)
        for j in range(2):
            block = value[:, j * 128 : (j + 1) * 128]
            block = jnp.where(part == 1, turned(block), block)
            block = block.astype(jnp.bfloat16).reshape(5, 128, 128)

            @pl.when(part == 1)
            def _():
                out_ref[:, j, 0, 2] = block[:4]
                out_ref[1:, j, 0, 0] = block[:3]
                out_ref[0, j, 0, 0] = block[4]

            @pl.when(part == 2)
            def _():
                out_ref[:, j, 0, 3] = block[:4]
                out_ref[1:, j, 0, 1] = block[:3]
                out_ref[0, j, 0, 1] = block[4]


def qkv_call(unit, weights, tables):
    table = pl.BlockSpec((640, 128), lambda h, p: (0, 0))
    return pl.pallas_call(
        qkv_kernel,
        grid=(2, 3),
        in_specs=[
            pl.BlockSpec((5, 128, D), lambda h, p: (0, 0, 0)),
            pl.BlockSpec((4, 1, 4, 144, 128), lambda h, p: (0, h, 0, 0, p)),
            pl.BlockSpec((4, 1, 4, 144, 128), lambda h, p: (0, h, 0, 0, p + 4)),
            table,
            table,
            table,
        ],
        out_specs=[
            pl.BlockSpec((4, 2, 1, 5, 128, 128), lambda h, p: (0, 0, h, 0, 0, 0)),
            pl.BlockSpec((4, 128, D), lambda h, p: (0, 0, 0)),
        ],
        out_shape=[
            jax.ShapeDtypeStruct((4, 2, 2, 5, 128, 128), jnp.bfloat16),
            jax.ShapeDtypeStruct((4, 128, D), jnp.bfloat16),
        ],
        scratch_shapes=[pltpu.VMEM((640, D), jnp.bfloat16)],
        compiler_params=pltpu.CompilerParams(vmem_limit_bytes=VMEM_LIMIT),
        cost_estimate=TINY,
    )(unit, weights, weights, *tables)


def whole_call(kernel, out_shape, *operands, scratch=()):
    vmem = pl.BlockSpec(memory_space=pltpu.VMEM)
    return pl.pallas_call(
        kernel,
        in_specs=[vmem] * len(operands),
        out_specs=jax.tree.map(lambda _: vmem, out_shape),
        out_shape=out_shape,
        scratch_shapes=list(scratch),
        compiler_params=pltpu.CompilerParams(vmem_limit_bytes=VMEM_LIMIT),
        cost_estimate=TINY,
    )(*operands)


def back_through(came_ref, values, gain):
    grad = came_ref[0].astype(jnp.float32)
    for i in range(1, 4):
        grad = grad + came_ref[i].astype(jnp.float32)
    unit, inverse = normalise(values)
    grad_unit = grad * gain
    centred_grad = (
        grad_unit
        - jnp.mean(grad_unit, -1, keepdims=True)
        - unit * jnp.mean(grad_unit * unit, -1, keepdims=True)
    )
    gain_grad = jnp.sum(grad * unit, 0, keepdims=True)
    return inverse * centred_grad, gain_grad, jnp.sum(grad, 0, keepdims=True)


def input_back_kernel(came_ref, tokens_ref, grad_ref, gain_ref, out_ref):
    values = tokens_ref[...].astype(jnp.float32)
    out_ref[...] = grad_ref[...] + back_through(came_ref, values, gain_ref[...])[0]


def shared_end_kernel(total_ref, gate_ref, up_ref, down_ref, out_ref):
    total = jnp.transpose(total_ref[...].astype(jnp.float32))
    for c in range(3):
        width = min(HID, c * 256 + 256) - c * 256
        gate_ref[c * 256 : c * 256 + width] = total[c * 512 : c * 512 + width]
        up_ref[c * 256 : c * 256 + width] = total[c * 512 + 256 : c * 512 + 256 + width]
    down_ref[...] = total[2 * HID_PAD : 2 * HID_PAD + HID]
    out_ref[...] = total[3 * HID_PAD :]


def joint_end_kernel(*refs):
    for j in range(2):
        total = sum(ref[...].astype(jnp.float32) for ref in refs[4 * j : 4 * j + 4])
        for part in range(3):
            refs[8][part, :, j * 128 : (j + 1) * 128] = total[:, part * 128 : part * 128 + 128]


def out_rows_kernel(place_ref, w0_ref, w1_ref, out_ref):
    for yl in range(2):
        for h in range(2):
            for j, ref in enumerate((w0_ref, w1_ref)):
                column = h * 256 + j * 128
                out_ref[yl, :, column : column + 128] = ref[0, h, 2 * yl + place_ref[1], :128]


def out_rows_call(place, weights):
    return pl.pallas_call(
        out_rows_kernel,
        grid=(4,),
        in_specs=[
            pl.BlockSpec(memory_space=pltpu.SMEM),
            pl.BlockSpec((1, 2, 4, 144, 128), lambda n: (n, 0, 0, 0, 3)),
            pl.BlockSpec((1, 2, 4, 144, 128), lambda n: (n, 0, 0, 0, 7)),
        ],
        out_specs=pl.BlockSpec((2, 128, 512), lambda n: (n, 0, 0)),
        out_shape=jax.ShapeDtypeStruct((8, 128, 512), jnp.bfloat16),
        compiler_params=pltpu.CompilerParams(vmem_limit_bytes=VMEM_LIMIT),
        cost_estimate=TINY,
    )(place, weights, weights)


def planes_columns(refs, yl):
    return jnp.concatenate([ref[yl] for ref in refs], 1)


def project_kernel(place_ref, att_ref, tokens_ref, gain_ref, shift_ref, *refs):
    own_refs, other_refs, (middle_ref, normed_ref, att_cols, total) = refs[:4], refs[4:8], refs[8:]
    n, me, core = pl.program_id(0), place_ref[0], place_ref[1]

    @pl.when(n == 0)
    def _():
        for t in range(4):
            x = (me + 4 - t) % 4
            for h in range(2):
                for j in range(2):
                    column = t * 512 + h * 256 + j * 128
                    att_cols[:, column : column + 128] = att_ref[x, j, h]

    weights = jnp.concatenate(
        [planes_columns(refs, yl) for refs in (own_refs, other_refs) for yl in range(2)], 0
    )
    values = mm(att_cols[...], weights, 1, 1)
    for i in range(4):
        holder = core if i < 2 else 1 - core
        column = pl.multiple_of((n * 4 + i % 2 * 2 + holder) * 128, 128)
        total[:, pl.ds(column, 128)] = values[:, i * 128 : i * 128 + 128]

    @pl.when(n == 3)
    def _():
        middle = tokens_ref[...].astype(jnp.float32) + total[...]
        middle_ref[...] = middle
        normed = (normalise(middle)[0] * gain_ref[...] + shift_ref[...]).astype(jnp.bfloat16)
        for i in range(4):
            normed_ref[i] = normed


def project_call(place, att, tokens, gain, shift, own, other):
    def whole(*dims):
        return pl.BlockSpec(dims, lambda n: (0,) * len(dims))

    rows = pl.BlockSpec((2, 128, 512), lambda n: (n, 0, 0))
    return pl.pallas_call(
        project_kernel,
        grid=(4,),
        in_specs=[
            pl.BlockSpec(memory_space=pltpu.SMEM),
            whole(4, 2, 2, 128, 128),
            whole(128, D),
            whole(1, D),
            whole(1, D),
        ]
        + [rows] * 8,
        out_specs=[whole(128, D), whole(4, 128, D)],
        out_shape=[
            jax.ShapeDtypeStruct((128, D), jnp.float32),
            jax.ShapeDtypeStruct((4, 128, D), jnp.bfloat16),
        ],
        scratch_shapes=[pltpu.VMEM((128, D), jnp.bfloat16), pltpu.VMEM((128, D), jnp.float32)],
        compiler_params=pltpu.CompilerParams(vmem_limit_bytes=VMEM_LIMIT),
        cost_estimate=TINY,
    )(place, att, tokens, gain, shift, *own, *other)


def project_back_kernel(place_ref, came_ref, middle_ref, cot_ref, gain_ref, *refs):
    own_refs, other_refs = refs[:4], refs[4:8]
    grad_ref, low_ref, gain_grad_ref, shift_grad_ref, out_ref, low, total = refs[8:]
    n, me, core = pl.program_id(0), place_ref[0], place_ref[1]

    @pl.when(n == 0)
    def _():
        grad, gain_grad_ref[...], shift_grad_ref[...] = back_through(came_ref, middle_ref[...], gain_ref[...])
        grad = grad + cot_ref[...].astype(jnp.float32)
        grad_ref[...] = grad
        low[...] = grad.astype(jnp.bfloat16)
        low_ref[...] = low[...]
        total[...] = jnp.zeros_like(total)

    columns = []
    for i in range(4):
        holder = core if i < 2 else 1 - core
        column = pl.multiple_of((n * 4 + i % 2 * 2 + holder) * 128, 128)
        columns.append(low[:, pl.ds(column, 128)])
    weights = jnp.concatenate(
        [planes_columns(refs, yl) for refs in (own_refs, other_refs) for yl in range(2)], 0
    )
    total[...] += mm(jnp.concatenate(columns, 1), weights)

    @pl.when(n == 3)
    def _():
        for t in range(4):
            x = (me + 4 - t) % 4
            for h in range(2):
                for j in range(2):
                    column = t * 512 + h * 256 + j * 128
                    out_ref[x, j, h] = total[:, column : column + 128].astype(jnp.bfloat16)


def project_back_call(place, came, middle, cot, gain, own, other):
    def whole(*dims):
        return pl.BlockSpec(dims, lambda n: (0,) * len(dims))

    rows = pl.BlockSpec((2, 128, 512), lambda n: (n, 0, 0))
    return pl.pallas_call(
        project_back_kernel,
        grid=(4,),
        in_specs=[
            pl.BlockSpec(memory_space=pltpu.SMEM),
            whole(4, 128, D),
            whole(128, D),
            whole(128, D),
            whole(1, D),
        ]
        + [rows] * 8,
        out_specs=[whole(128, D), whole(128, D), whole(1, D), whole(1, D), whole(4, 2, 2, 128, 128)],
        out_shape=[
            jax.ShapeDtypeStruct((128, D), jnp.float32),
            jax.ShapeDtypeStruct((128, D), jnp.bfloat16),
            jax.ShapeDtypeStruct((1, D), jnp.float32),
            jax.ShapeDtypeStruct((1, D), jnp.float32),
            jax.ShapeDtypeStruct((4, 2, 2, 128, 128), jnp.bfloat16),
        ],
        scratch_shapes=[pltpu.VMEM((128, D), jnp.bfloat16), pltpu.VMEM((128, D), jnp.float32)],
        compiler_params=pltpu.CompilerParams(vmem_limit_bytes=VMEM_LIMIT),
        cost_estimate=TINY,
    )(place, came, middle, cot, gain, *own, *other)


def feed_forward_kernel(
    x_ref, cot_ref, gate_ref, up_ref, down_ref, active_ref, grads_ref, back_ref, out_ref, back_sum, out_sum
):
    first_half = pl.program_id(0) == 0
    x = x_ref[...].reshape(512, D)
    cot = cot_ref[...].reshape(512, D)
    for c in range(3):
        columns = slice(c * 256, c * 256 + 256)
        gate = mm(x, gate_ref[:, 0, :, columns].reshape(D, 256))
        up = mm(x, up_ref[:, 0, :, columns].reshape(D, 256))
        grad_active = mm(cot, down_ref[:, 0, :, columns].reshape(D, 256))
        sigmoid = jax.nn.sigmoid(gate)
        silu = gate * sigmoid
        active_ref[0, :, columns] = (silu * up).astype(jnp.bfloat16)
        grad_gate = grad_active * up * (sigmoid + silu * (1.0 - sigmoid))
        grads_ref[0, :, c * 512 : c * 512 + 256] = grad_gate.astype(jnp.bfloat16)
        grads_ref[0, :, c * 512 + 256 : c * 512 + 512] = (grad_active * silu).astype(jnp.bfloat16)
    for n in range(4):
        rows = slice(n * 512, n * 512 + 512)
        weights = jnp.concatenate(
            [ref[n, 0, :, c * 256 : c * 256 + 256] for c in range(3) for ref in (gate_ref, up_ref)], 1
        )
        back = mm(grads_ref[0], weights, 1, 1)
        out = mm(active_ref[0], down_ref[n, 0], 1, 1)

        @pl.when(first_half)
        def _():
            back_sum[:, rows] = back
            out_sum[:, rows] = out

        @pl.when(~first_half)
        def _():
            back_ref[:, :, rows] = (back_sum[:, rows] + back).astype(jnp.bfloat16).reshape(4, 128, 512)
            out_ref[:, :, rows] = (out_sum[:, rows] + out).astype(jnp.bfloat16).reshape(4, 128, 512)


def feed_forward_call(x, ring, rest):
    tokens = pl.BlockSpec((4, 128, D), lambda h: (0, 0, 0))
    tokens_once = pl.BlockSpec((4, 128, D), lambda h: (0, 0, 0), pipeline_mode=pl.Buffered(1))
    weight = [pl.BlockSpec((4, 1, 512, HID_PAD), lambda h, i=i: (0, h, 0, i)) for i in range(3)]
    ring_shape = jax.ShapeDtypeStruct((4, 128, D), jnp.bfloat16)
    return pl.pallas_call(
        feed_forward_kernel,
        grid=(2,),
        in_specs=[tokens_once, tokens_once] + weight,
        out_specs=[
            pl.BlockSpec((1, 512, HID_PAD), lambda h: (h, 0, 0)),
            pl.BlockSpec((1, 512, 2 * HID_PAD), lambda h: (h, 0, 0)),
            tokens,
            tokens,
        ],
        out_shape=[
            jax.ShapeDtypeStruct((2, 512, HID_PAD), jnp.bfloat16),
            jax.ShapeDtypeStruct((2, 512, 2 * HID_PAD), jnp.bfloat16),
            ring_shape,
            ring_shape,
        ],
        scratch_shapes=[pltpu.VMEM((512, D), jnp.float32), pltpu.VMEM((512, D), jnp.float32)],
        compiler_params=pltpu.CompilerParams(vmem_limit_bytes=VMEM_LIMIT),
        cost_estimate=TINY,
    )(x, ring, rest, rest, rest)


def plane_grad_kernel(core_ref, left_ref, left_other_ref, right_ref, right_other_ref, *refs):
    out_ref, left_t = refs[-2:]

    @pl.when((pl.program_id(0) == 0) & (pl.program_id(1) == 0))
    def _():
        left_t[:, :512] = jnp.transpose(core_columns(left_ref, core_ref[0], 4))
        left_t[:, 512:] = jnp.transpose(core_columns(left_other_ref, core_ref[0], 4))

    total = mm(left_t[...], jnp.concatenate([right_ref[0], right_other_ref[0]], 0)).astype(jnp.bfloat16)
    for z in range(4):
        for yl in range(2):
            row = (z * 2 + yl) * 128
            out_ref[0, yl, z] = total[row : row + 128]


def plane_grad_call(core, left, right, columns, first, shared=None):
    left_block = pl.BlockSpec((4, 128, D), lambda n, h: (0, 0, 0))
    right_block = pl.BlockSpec((1, 512, 256), lambda n, h: (h, 0, n))
    extra = [] if shared is None else [shared]
    return pl.pallas_call(
        plane_grad_kernel,
        grid=(columns // 256, 2),
        in_specs=[
            pl.BlockSpec(memory_space=pltpu.SMEM),
            left_block,
            left_block,
            right_block,
            right_block,
        ]
        + [pl.BlockSpec(memory_space=pl.ANY)] * len(extra),
        out_specs=pl.BlockSpec((1, 2, 4, 128, 256), lambda n, h: (h, 0, 0, 0, first // 256 + n)),
        out_shape=jax.ShapeDtypeStruct((2, 2, 4, 128, SHARED), jnp.bfloat16),
        input_output_aliases={5: 0} if extra else {},
        scratch_shapes=[pltpu.VMEM((1024, 1024), jnp.bfloat16)],
        compiler_params=pltpu.CompilerParams(vmem_limit_bytes=VMEM_LIMIT),
        cost_estimate=TINY,
    )(core, *left, *right, *extra)


def own_rows_kernel(place_ref, left_ref, left_other_ref, out_ref):
    out_ref[:, :512] = jnp.transpose(core_columns(left_ref, place_ref[1], 4))
    out_ref[:, 512:] = jnp.transpose(core_columns(left_other_ref, place_ref[1], 4))


def own_rows_call(place, left):
    vmem = pl.BlockSpec(memory_space=pltpu.VMEM)
    return pl.pallas_call(
        own_rows_kernel,
        in_specs=[pl.BlockSpec(memory_space=pltpu.SMEM), vmem, vmem],
        out_specs=vmem,
        out_shape=jax.ShapeDtypeStruct((1024, 1024), jnp.bfloat16),
        compiler_params=pltpu.CompilerParams(vmem_limit_bytes=VMEM_LIMIT),
        cost_estimate=TINY,
    )(place, *left)


def joint_grad_kernel(place_ref, left_ref, right_ref, right_other_ref, *outs):
    h = pl.program_id(0)
    right = jnp.concatenate([right_ref[0], right_other_ref[0]], 0)
    total = mm(left_ref[...], right).astype(jnp.bfloat16)
    for z in range(4):
        for yl in range(2):
            row = (z * 2 + yl) * 128
            chip = (h * 2 + yl) * 4 + z
            for j in range(2):
                step, slot = place_ref[2 * j, chip], place_ref[2 * j + 1, chip]
                for t in range(4):

                    @pl.when(step == t)
                    def _():
                        outs[4 * j + t][slot] = total[row : row + 128, j * 384 : j * 384 + 384]


def joint_grad_call(places, left, right):
    right_block = pl.BlockSpec((1, 512, 768), lambda h: (h, 0, 0))
    return pl.pallas_call(
        joint_grad_kernel,
        grid=(2,),
        in_specs=[
            pl.BlockSpec(memory_space=pltpu.SMEM),
            pl.BlockSpec((1024, 1024), lambda h: (0, 0)),
            right_block,
            right_block,
        ],
        out_specs=[pl.BlockSpec((4, 128, 384), lambda h: (0, 0, 0))] * 8,
        out_shape=[jax.ShapeDtypeStruct((4, 128, 384), jnp.bfloat16)] * 8,
        compiler_params=pltpu.CompilerParams(vmem_limit_bytes=VMEM_LIMIT),
        cost_estimate=TINY,
    )(jnp.concatenate(places, 0), left, *right)


def split_sum_kernel(place_ref, a_ref, b_ref, c_ref, d_ref, *out_refs):
    for t in range(4):
        i = (place_ref[0] + t) % 4
        total = sum(ref[i].astype(jnp.float32) for ref in (a_ref, b_ref, c_ref, d_ref))
        out_refs[t][...] = total.astype(jnp.bfloat16)


def split_sum_call(place, parts):
    columns = parts[0].shape[2]
    width = 256 if columns % 256 == 0 else 384
    return pl.pallas_call(
        split_sum_kernel,
        grid=(columns // width,),
        in_specs=[pl.BlockSpec(memory_space=pltpu.SMEM)]
        + [pl.BlockSpec((4, 128, width), lambda n: (0, 0, n))] * 4,
        out_specs=[pl.BlockSpec((128, width), lambda n: (0, n))] * 4,
        out_shape=[jax.ShapeDtypeStruct((128, columns), jnp.bfloat16)] * 4,
        compiler_params=pltpu.CompilerParams(vmem_limit_bytes=VMEM_LIMIT),
        cost_estimate=TINY,
    )(place, *parts)


def chip_places(y_first):
    y, z = jnp.arange(16, dtype=jnp.int32) // 4, jnp.arange(16, dtype=jnp.int32) % 4
    if y_first:
        return jnp.stack([(y - lax.axis_index(Y)) % 4, z])
    return jnp.stack([(z - lax.axis_index("z")) % 4, y])


def plane_sum(parts):
    parts = parts.reshape(2048, parts.shape[-1])
    return lax.psum_scatter(parts, ("yh", "yl", "z"), scatter_dimension=0, tiled=True)


def with_other(value):
    return value, swap_core(value)


def first_send(parts, y_first):
    axes = Y if y_first else ("z",)
    return [parts[0]] + [send(parts[t], axes, t) for t in (1, 3, 2)]


def first_sum(parts, y_first):
    return split_sum_call(lax.axis_index(("z",) if y_first else Y).reshape(1), parts)


def second_send(parts, y_first):
    axes = ("z",) if y_first else Y
    return [parts[0]] + [send(parts[t], axes, t) for t in (1, 3, 2)]


def stack_heads(ref, *index):
    first = (lax.broadcasted_iota(jnp.int32, (128, 128), 1) < HEAD_DIM).astype(jnp.float32).astype(jnp.bfloat16)
    masks = (first, 1 - first)
    return jnp.concatenate([ref[i] * mask for i in index for mask in masks], 0)


def unstack_heads(values, block):
    low = lax.broadcasted_iota(jnp.int32, (128, 128), 1) < HEAD_DIM
    rows = values[block * 256 : block * 256 + 256]
    return jnp.where(low, rows[:128], rows[128:])


def key_blocks(r_ref, block, slot):
    rows = []
    for i in range(4):
        index = jnp.maximum(block + i, 0)
        rows.append(r_ref[index & 15, (index >> 4) * 2 + slot])
    return jnp.concatenate(rows, 0)


def masked(values, a, block, lo_a, lo_b, diagonal, fill):
    key_row = lax.broadcasted_iota(jnp.int32, (128, 256), 0)
    causal = key_row <= lax.broadcasted_iota(jnp.int32, (128, 256), 1) % 128
    rows = []
    for k in range(4):
        parts = []
        for i, lo in enumerate((lo_a, lo_b)):
            mask = block + k >= lo
            if diagonal and k == 2 + i:
                mask = causal
            part = values[k * 128 : k * 128 + 128, i * 256 : i * 256 + 256]
            if diagonal and k == 3 and i == 0:
                parts.append(jnp.full((128, 256), fill, jnp.float32))
            else:
                parts.append(jnp.where(mask, part, fill))
        rows.append(jnp.concatenate(parts, 1))
    return jnp.concatenate(rows, 0)


def attend_kernel(lo_ref, r_ref, o32_ref, o16_ref, lse_ref):
    def one_pair(a, _):
        lo_a, lo_b = lo_ref[2 * a], lo_ref[2 * a + 1]
        queries = stack_heads(r_ref, (2 * a, 4), (2 * a + 1, 4))

        def scores(block, diagonal):
            values = mm(key_blocks(r_ref, block, 0), queries, 1, 1)
            return masked(values, a, block, lo_a, lo_b, diagonal, masked_score)

        def add(scores, block, top):
            weights = jnp.exp(scores - top)
            sums = mm(key_blocks(r_ref, block, 1), weights.astype(jnp.bfloat16), 0, 0)
            return jnp.sum(weights, 0, keepdims=True), sums

        diagonal = scores(2 * a + 14, True)
        top = jnp.max(diagonal, 0, keepdims=True)
        total, sums = add(diagonal, 2 * a + 14, top)

        def earlier(i, carry):
            top, total, sums = carry
            block = 2 * a + 14 - 4 * i
            values = scores(block, False)
            new = jnp.maximum(top, jnp.max(values, 0, keepdims=True))
            scale = jnp.exp(top - new)
            more, more_sums = add(values, block, new)
            return new, total * scale + more, sums * scale + more_sums

        steps = (2 * a + 21 - lo_a) // 4
        top, total, sums = lax.fori_loop(1, steps, earlier, (top, total, sums))
        out = jnp.transpose(sums / total)
        for block in range(2):
            rows = unstack_heads(out, block)
            o32_ref[2 * a + block] = rows
            o16_ref[2 * a + block] = rows.astype(jnp.bfloat16)
        lse_ref[a] = top + jnp.log(total)
        return 0

    lax.fori_loop(0, 8, one_pair, 0)


def attend_call(lo, blocks):
    vmem = pl.BlockSpec(memory_space=pltpu.VMEM)
    return pl.pallas_call(
        attend_kernel,
        in_specs=[pl.BlockSpec(memory_space=pltpu.SMEM), vmem],
        out_specs=[vmem, vmem, vmem],
        out_shape=[
            jax.ShapeDtypeStruct((16, 128, 128), jnp.float32),
            jax.ShapeDtypeStruct((16, 128, 128), jnp.bfloat16),
            jax.ShapeDtypeStruct((8, 1, 512), jnp.float32),
        ],
        compiler_params=pltpu.CompilerParams(vmem_limit_bytes=VMEM_LIMIT),
        cost_estimate=TINY,
    )(lo, blocks)


def attend_back_kernel(lo_ref, r_ref, do_ref, o32_ref, lse_ref, out_ref, dk_ref, dv_ref):
    dk_ref[...] = jnp.zeros_like(dk_ref)
    dv_ref[...] = jnp.zeros_like(dv_ref)

    def one_pair(a, _):
        lo_a, lo_b = lo_ref[2 * a], lo_ref[2 * a + 1]
        queries = stack_heads(r_ref, (2 * a, 4), (2 * a + 1, 4))
        grads = stack_heads(do_ref, 2 * a, 2 * a + 1)
        out = jnp.concatenate([o32_ref[2 * a]] * 2 + [o32_ref[2 * a + 1]] * 2, 0)
        delta = jnp.sum(jnp.transpose(grads.astype(jnp.float32) * out), 0, keepdims=True)
        lse = lse_ref[a]

        def blocks_back(block, diagonal):
            keys, values = key_blocks(r_ref, block, 0), key_blocks(r_ref, block, 1)
            weights = jnp.exp(mm(keys, queries, 1, 1) - lse)
            weights = masked(weights, a, block, lo_a, lo_b, diagonal, 0.0)
            grad_scores = (weights * (mm(values, grads, 1, 1) - delta)).astype(jnp.bfloat16)
            grad_values = mm(weights.astype(jnp.bfloat16), grads)
            grad_keys = mm(grad_scores, queries)
            for k in range(4):
                index, rows = jnp.maximum(block + k, 0), slice(k * 128, k * 128 + 128)
                dv_ref[index] += grad_values[rows]
                dk_ref[index] += grad_keys[rows]
            return mm(grad_scores, keys, 0, 0)

        def earlier(i, grad_query):
            return grad_query + blocks_back(2 * a + 14 - 4 * i, False)

        steps = (2 * a + 21 - lo_a) // 4
        grad_query = blocks_back(2 * a + 14, True)
        grad_query = lax.fori_loop(1, steps, earlier, grad_query)
        for block in range(2):
            rows = unstack_heads(grad_query, block) * score_scale
            out_ref[2 * a + block, 4] = rows.astype(jnp.bfloat16)
        return 0

    lax.fori_loop(0, 8, one_pair, 0)

    def finish(c, _):
        out_ref[c, 0] = dk_ref[c].astype(jnp.bfloat16)
        out_ref[c, 1] = dv_ref[c].astype(jnp.bfloat16)
        out_ref[c, 2] = dk_ref[c + 16].astype(jnp.bfloat16)
        out_ref[c, 3] = dv_ref[c + 16].astype(jnp.bfloat16)
        return 0

    lax.fori_loop(0, 16, finish, 0)


def attend_back_call(lo, blocks, grads, out, lse):
    vmem = pl.BlockSpec(memory_space=pltpu.VMEM)
    return pl.pallas_call(
        attend_back_kernel,
        in_specs=[pl.BlockSpec(memory_space=pltpu.SMEM), vmem, vmem, vmem, vmem],
        out_specs=vmem,
        out_shape=jax.ShapeDtypeStruct((16, 5, 128, 128), jnp.bfloat16),
        scratch_shapes=[
            pltpu.VMEM((32, 128, 128), jnp.float32),
            pltpu.VMEM((32, 128, 128), jnp.float32),
        ],
        compiler_params=pltpu.CompilerParams(vmem_limit_bytes=VMEM_LIMIT),
        cost_estimate=TINY,
    )(lo, blocks, grads, out, lse)


def turn_back_kernel(r_ref, halo_ref, cos_ref, up_ref, down_ref, out_ref, bias_ref):
    for j in range(2):
        sums = [jnp.zeros((1, 128), jnp.float32) for _ in range(3)]
        for x in range(4):
            rows = slice(x * 128, (x + 1) * 128)

            def turned(grad):
                return (
                    grad * cos_ref[rows]
                    - pltpu.roll(grad, 120, 1) * up_ref[rows]
                    - pltpu.roll(grad, 8, 1) * down_ref[rows]
                )

            def read(slot):
                later = r_ref[x + 1, j, 0, slot] if x < 3 else halo_ref[j, 0, slot]
                return r_ref[x, j, 0, slot + 2].astype(jnp.float32) + later.astype(jnp.float32)

            parts = (
                turned(r_ref[x, j, 0, 4].astype(jnp.float32)),
                turned(read(0)),
                read(1),
            )
            for part in range(3):
                grad = parts[part].astype(jnp.bfloat16)
                column = (j * 3 + part) * 128
                out_ref[0, rows, column : column + 128] = grad
                sums[part] = sums[part] + jnp.sum(grad.astype(jnp.float32), 0, keepdims=True)
        for part in range(3):
            column = (j * 3 + part) * 128
            bias_ref[0, :, column : column + 128] = sums[part]


def turn_back_call(blocks, halo, tables):
    table = pl.BlockSpec((512, 128), lambda h: (0, 0))
    return pl.pallas_call(
        turn_back_kernel,
        grid=(2,),
        in_specs=[
            pl.BlockSpec((4, 2, 1, 5, 128, 128), lambda h: (0, 0, h, 0, 0, 0)),
            pl.BlockSpec((2, 1, 2, 128, 128), lambda h: (0, h, 0, 0, 0)),
            table,
            table,
            table,
        ],
        out_specs=[
            pl.BlockSpec((1, 512, 768), lambda h: (h, 0, 0)),
            pl.BlockSpec((1, 1, 768), lambda h: (h, 0, 0)),
        ],
        out_shape=[
            jax.ShapeDtypeStruct((2, 512, 768), jnp.bfloat16),
            jax.ShapeDtypeStruct((2, 1, 768), jnp.float32),
        ],
        compiler_params=pltpu.CompilerParams(vmem_limit_bytes=VMEM_LIMIT),
        cost_estimate=TINY,
    )(blocks, halo, *tables)


def normed_back_kernel(g_ref, unit_ref, w_ref, out_ref, gain_grad_ref, shift_grad_ref):
    grads = jnp.concatenate([g_ref[0], g_ref[1]], 1)
    weights = jnp.concatenate(
        [
            w_ref[0, h, :, :128, j * 512 : j * 512 + 384].reshape(512, 384)
            for h in range(2)
            for j in range(2)
        ],
        1,
    )
    total = mm(grads, weights, 1, 1)
    out_ref[...] = total.astype(jnp.bfloat16).reshape(4, 128, 512)
    unit = unit_ref[...].reshape(512, 512).astype(jnp.float32)
    gain_grad_ref[...] = jnp.sum(total * unit, 0, keepdims=True)
    shift_grad_ref[...] = jnp.sum(total, 0, keepdims=True)


def normed_back_call(grad_joint, unit, weights):
    ring = pl.BlockSpec((4, 128, 512), lambda n: (0, 0, n))
    vector = pl.BlockSpec((1, 512), lambda n: (0, n))
    return pl.pallas_call(
        normed_back_kernel,
        grid=(4,),
        in_specs=[
            pl.BlockSpec((2, 512, 768), lambda n: (0, 0, 0)),
            ring,
            pl.BlockSpec((1, 2, 4, 144, 1024), lambda n: (n, 0, 0, 0, 0)),
        ],
        out_specs=[ring, vector, vector],
        out_shape=[
            jax.ShapeDtypeStruct((4, 128, D), jnp.bfloat16),
            jax.ShapeDtypeStruct((1, D), jnp.float32),
            jax.ShapeDtypeStruct((1, D), jnp.float32),
        ],
        compiler_params=pltpu.CompilerParams(vmem_limit_bytes=VMEM_LIMIT),
        cost_estimate=TINY,
    )(grad_joint, unit, weights)


def local(
    tokens,
    cotangent,
    doc_ids,
    ln1_gain,
    ln1_shift,
    w_qkv,
    b_qkv,
    w_out,
    ln2_gain,
    ln2_shift,
    w_gate,
    w_up,
    w_down,
):
    half = lax.axis_index("yh")
    blk = lax.axis_index(BLK)

    core = lax.axis_index("k").reshape(1)
    vectors = jnp.stack([ln1_gain, ln1_shift, ln2_gain, ln2_shift])
    joint_w = pack_joint_call(w_qkv.transpose(1, 0, 2), w_out, vectors, b_qkv)
    joint_w = lax.all_gather(joint_w, PLANE, axis=0).reshape(4, 2, 4, 144, 1024)
    ring = ring_gather(tokens)
    place = jnp.stack([lax.axis_index("x"), lax.axis_index("k")]).astype(jnp.int32)
    before = lax.ppermute(ring[3], ("yh",), [(0, 1)])
    ring_cot = lax.all_gather(after(cotangent, ring), "x", axis=0)
    rest = pack_hidden_call(w_gate.T, w_up.T, w_down)


    first_block = jnp.sum((doc_ids[None, :] < doc_ids[:, None]).astype(jnp.int32), axis=1)
    cycles = jnp.arange(4, dtype=jnp.int32) * 16 + half * 64 + blk
    cycles = jnp.concatenate([cycles, 48 + blk.reshape(1)])
    block_position = (cycles - first_block[cycles]) * BLK_TOK
    positions = (block_position[:, None] + jnp.arange(BLK_TOK, dtype=jnp.int32)).reshape(640)
    tables = rotary_tables(positions)
    first_query = half * 64 + (blk // 4) * 16
    lo = lax.dynamic_slice(first_block, (first_query,), (16,)) - (first_query - 16)

    unit_one = unit_call(ring, before)
    payload, normed_one = qkv_call(unit_one, joint_w, tables)
    out_w, payload = lax.optimization_barrier((joint_w, payload))
    vectors = out_w[:, 0, :, 128:132, :128].astype(jnp.float32).transpose(2, 0, 1, 3).reshape(4, D)
    gain_one, _, gain_two, shift_two = [vectors[i : i + 1] for i in range(4)]
    own_rows = out_rows_call(place, out_w)
    near_rows = [send(own_rows, ("x",), t) for t in (1, 3)]
    blocks = after(exchange(payload.reshape(16, 5, 128, 128), BLK), near_rows)
    rest = lax.all_gather(after(rest, blocks), PLANE, axis=0).reshape(4, 2, 512, 3 * HID_PAD)
    att32, att16, lse = attend_call(lo, blocks)
    far_rows = send(after(own_rows, blocks), ("x",), 2)
    attended = exchange(att16, BLK).reshape(4, 2, 2, 128, 128)
    own_rows = [own_rows, near_rows[0], after(far_rows, attended), near_rows[1]]
    other_rows = [swap_core(rows) for rows in own_rows]
    middle, normed_two = project_call(
        place, exchange(attended, ("x",)), tokens, gain_two, shift_two, own_rows, other_rows
    )

    ring_two = exchange(normed_two, ("x",))
    active, grad_gu, ring_grad, ring_out = feed_forward_call(ring_two, ring_cot, rest)
    shared = plane_grad_call(core, with_other(ring_cot), with_other(active), HID_PAD, 2 * HID_PAD)
    came = after(exchange(ring_grad, ("x",)), shared)
    grad_middle, grad_branch, grad_gain_two, grad_shift_two, grad_att = project_back_call(
        place, came, middle, cotangent, gain_two, own_rows, other_rows
    )
    grad_att = exchange(grad_att, ("x",))
    ring_branch = lax.all_gather(after(grad_branch, grad_att), "x", axis=0)
    joint_left = own_rows_call(place, with_other(normed_one))
    grad_att = after(exchange(grad_att.reshape(16, 128, 128), BLK), joint_left)
    attended_pair = with_other(attended.transpose(2, 0, 3, 1, 4).reshape(2, 512, 256))

    mixed = lax.psum_scatter(
        after(ring_out, grad_att).reshape(512, D), "x", scatter_dimension=0, tiled=True
    )
    back = attend_back_call(lo, blocks, grad_att, att32, lse)
    hidden_pair = with_other(ring_two), with_other(grad_gu)
    shared = plane_grad_call(core, *after(hidden_pair, back), 2 * HID_PAD, 0, shared)
    branch_pair = with_other(after(ring_branch, back))
    shared = plane_grad_call(core, branch_pair, attended_pair, 256, 3 * HID_PAD, shared)
    back = exchange(back, BLK).reshape(4, 2, 2, 5, 128, 128)
    back, shared = lax.optimization_barrier((back, shared))
    shared = plane_sum(shared)
    mixed = (middle + after(mixed, back).astype(jnp.float32)).astype(jnp.bfloat16)
    halo_back = lax.ppermute(back[0, :, :, :2], ("yh",), [(1, 0)])
    back = after(back, mixed)
    grad_joint, grad_bias = turn_back_call(back, halo_back, tables)
    places = (chip_places(True), chip_places(False))
    parts = joint_grad_call(places, joint_left, with_other(grad_joint))
    ring_one, grad_gain_one, grad_shift_one = normed_back_call(grad_joint, unit_one, joint_w)
    pair_came = [first_send(parts[4 * j : 4 * j + 4], j == 0) for j in range(2)]

    norms = jnp.concatenate([grad_gain_one, grad_shift_one, grad_gain_two, grad_shift_two], 0)
    norms = norms.reshape(4, 2, 4, 16, 16).transpose(1, 2, 3, 0, 4).reshape(2, 4, 16, 64)
    biases = grad_bias.reshape(2, 2, 3, 8, 16).transpose(0, 1, 3, 2, 4).reshape(2, 1, 16, 48)
    plane = jnp.arange(4).reshape(1, 4, 1, 1) == lax.axis_index("x")
    biases = jnp.where(plane, biases, 0.0)
    sums = jnp.concatenate([norms, biases, jnp.zeros((2, 4, 16, 16), jnp.float32)], 3)
    sums = jnp.sum(exchange(sums.reshape(128, 128), AXES), 0)
    norms = sums[:64].reshape(4, 16)

    came = exchange(after(ring_one, norms, parts[0]), ("x",))
    input_grad = whole_call(
        input_back_kernel,
        jax.ShapeDtypeStruct((128, D), jnp.float32),
        came,
        tokens,
        grad_middle,
        gain_one,
    )
    pair_came[1] = after(pair_came[1], input_grad)
    pair_came = [second_send(first_sum(part, j == 0), j == 0) for j, part in enumerate(pair_came)]

    def shape(*dims):
        return jax.ShapeDtypeStruct(dims, jnp.float32)

    grad_gate, grad_up, grad_down, grad_out = whole_call(
        shared_end_kernel, [shape(HID, 128)] * 3 + [shape(256, 128)], after(shared, input_grad)
    )
    grad_qkv = whole_call(joint_end_kernel, shape(3, 128, 256), *pair_came[0], *pair_came[1])

    return (
        mixed,
        input_grad,
        norms[0],
        norms[1],
        grad_qkv.transpose(1, 0, 2),
        sums[64:112].reshape(3, 16),
        grad_out,
        norms[2],
        norms[3],
        grad_gate.T,
        grad_up.T,
        grad_down,
    )


def solution(mesh):
    whole = Mesh(mesh.devices.reshape(2, 4, 4, 2, 2), AXES)
    ulysses, blk = ("yh", "x"), BLK
    both = ulysses + blk
    placed = (
        P(both, None),
        P(both, None),
        P(),
        P(blk),
        P(blk),
        P(blk, None, ulysses),
        P(None, both),
        P(ulysses, blk),
        P(blk),
        P(blk),
        P(blk, ulysses),
        P(blk, ulysses),
        P(ulysses, blk),
    )
    return jax.shard_map(
        local,
        mesh=whole,
        in_specs=placed,
        out_specs=(
            P(both, None),
            P(both, None),
            P(both),
            P(both),
            P(blk, None, ulysses),
            P(None, both),
            P(ulysses, blk),
            P(both),
            P(both),
            P(blk, ulysses),
            P(blk, ulysses),
            P(ulysses, blk),
        ),
        check_vma=False,
    )
```
